32 devices in a mesh: dp: 2 (over core), row: 8 (over z, y), col: 2 (over x).
Axes of the slice: x: 2, y: 2, z: 4, core: 2. Of those that a mesh axis runs over, the one named last changes fastest.
Arguments:
- features: bfloat16 [2, 64, 128, 512], P('dp', None, 'row', 'col'), may hold values from -6 to 6
- grad_out: bfloat16 [2, 64, 128, 512], P('dp', None, 'row', 'col'), may hold values from -6 to 6
- kernel_one: bfloat16 [3, 3, 64, 64], replicated, may hold values from -0.25 to 0.25
- kernel_two: bfloat16 [3, 3, 64, 64], replicated, may hold values from -0.25 to 0.25
Outputs:
- grad_features: bfloat16 [2, 64, 128, 512], P('dp', None, 'row', 'col')
- grad_kernel_one: float32 [3, 3, 64, 64], replicated
- grad_kernel_two: float32 [3, 3, 64, 64], replicated
The draws below stay inside these ranges and needn't reach their ends.
All inputs are finite; a program needn't handle non-finite values.
Results may differ from the reference program's by a relative error of at most 0.0061.
Values may be sent and summed in bfloat16 or wider, within the bound.
No kernel may reach another device: no remote copies, remote signals or barrier semaphores. Data moves between devices by JAX's collectives and lax.ppermute only.
A program may use at most 64 MiB of HBM per device.

```python
import jax
import jax.numpy as jnp
from jax import lax

C = 64
BATCH = 2
NH = 128
NW = 512


def level_of(own_key, shape, pieces, smallest, top_value):
    loudness, own = 1.0, jax.random.fold_in(own_key, 6)
    for axis_at, shards_of in pieces:
        steps = jnp.exp(jax.random.uniform(jax.random.fold_in(own, axis_at), (shards_of,), jnp.float32, smallest / len(pieces), top_value / len(pieces)))
        loudness = loudness * jnp.repeat(steps, shape[axis_at] // shards_of).reshape([-1 if axis == axis_at else 1 for axis in range(len(shape))])
    return loudness


def centred(key, shape, spread, most, split=(), dtype=jnp.bfloat16):
    gain = level_of(key, shape, split, -0.22, 0.18) if split else 1.0
    drawn = jax.random.normal(key, shape, jnp.float32) * spread * gain
    return jnp.minimum(jnp.maximum(drawn, -most), most).astype(dtype)


def setup_inputs(seed: int = 0) -> dict:
    streams_of = jax.random.split(jax.random.key(seed), 5)
    features = centred(streams_of[0], (BATCH, C, NH, NW), 1.0, 6.0, ((0, 2), (2, 8), (3, 2)))
    grad_out = centred(streams_of[1], (BATCH, C, NH, NW), 1.0, 6.0, ((0, 2), (2, 8), (3, 2)))
    kernel_one = centred(streams_of[2], (3, 3, C, C), (9 * C) ** -0.5, 0.25)
    kernel_two = centred(streams_of[3], (3, 3, C, C), (9 * C) ** -0.5, 0.25)
    return dict(features=features, grad_out=grad_out, kernel_one=kernel_one, kernel_two=kernel_two)


def convolve(padded, kernel, rows, cols):
    total = jnp.zeros((padded.shape[0], kernel.shape[2], rows, cols), jnp.float32)
    for ky in range(3):
        for kx in range(3):
            total = total + jnp.einsum('oi,sihw->sohw', kernel[ky, kx].astype(jnp.float32), padded[:, :, ky:ky + rows, kx:kx + cols].astype(jnp.float32), precision=lax.Precision.HIGHEST)
    return total

def transposed(padded, kernel, rows, cols):
    total = jnp.zeros((padded.shape[0], kernel.shape[3], rows, cols), jnp.float32)
    for ky in range(3):
        for kx in range(3):
            total = total + jnp.einsum('oi,sohw->sihw', kernel[ky, kx].astype(jnp.float32), padded[:, :, 2 - ky:2 - ky + rows, 2 - kx:2 - kx + cols].astype(jnp.float32), precision=lax.Precision.HIGHEST)
    return total

def kernel_grad(padded, delta, rows, cols):
    taps = []
    for ky in range(3):
        line = []
        for kx in range(3):
            line.append(jnp.einsum('sohw,sihw->oi', delta.astype(jnp.float32), padded[:, :, ky:ky + rows, kx:kx + cols].astype(jnp.float32), precision=lax.Precision.HIGHEST))
        taps.append(jnp.stack(line))
    return jnp.stack(taps)

def dsilu(value):
    sig = jax.nn.sigmoid(value)
    return sig * (1.0 + value * (1.0 - sig))

def padding(value):
    return jnp.pad(value, ((0, 0), (0, 0), (1, 1), (1, 1)))

def reference(features, grad_out, kernel_one, kernel_two):
    rows, cols = (features.shape[2], features.shape[3])
    feat_pad = padding(features)
    pre_one = convolve(feat_pad, kernel_one, rows, cols)
    hidden = jax.nn.silu(pre_one).astype(jnp.bfloat16)
    hid_pad = padding(hidden)
    pre_two = convolve(hid_pad, kernel_two, rows, cols)
    delta_two = (grad_out.astype(jnp.float32) * dsilu(pre_two)).astype(jnp.bfloat16)
    back_one = transposed(padding(delta_two), kernel_two, rows, cols)
    delta_one = (back_one * dsilu(pre_one)).astype(jnp.bfloat16)
    grad_features = transposed(padding(delta_one), kernel_one, rows, cols).astype(jnp.bfloat16)
    scale = 1.0 / jnp.sqrt(jnp.float32(features.shape[0] * rows * cols))
    grad_two = kernel_grad(hid_pad, delta_two, rows, cols) * scale
    grad_one = kernel_grad(feat_pad, delta_one, rows, cols) * scale
    return (grad_features, grad_one, grad_two)
```

```python
import jax
import jax.numpy as jnp
from jax import lax
from jax.experimental import pallas as pl
from jax.experimental.pallas import tpu as pltpu
from jax.sharding import PartitionSpec as P

BF = jnp.bfloat16
F32 = jnp.float32
AXES = ("dp", "row", "col")
LANES = 128
RIM = 16


def pair_exchange(low, high, axis):
    count = lax.axis_size(axis)
    even = lax.axis_index(axis) % 2 == 0
    got = []
    for parity in range(2):
        perm = []
        for i in range(parity, count - 1, 2):
            perm += [(i, i + 1), (i + 1, i)]
        if not perm:
            got.append(jnp.zeros_like(low))
            continue
        up = even if parity == 0 else jnp.logical_not(even)
        got.append(lax.ppermute(jnp.where(up, high, low), axis, perm))
    from_prev = jnp.where(even, got[1], got[0])
    from_next = jnp.where(even, got[0], got[1])
    return from_prev, from_next


def to_pairs(cells):
    _, chans, rows, cols = cells.shape
    part = cells[0].reshape(chans, rows // 2, 2, cols)
    return part.transpose(1, 3, 2, 0).reshape(rows // 2, cols, 2 * chans)


def from_pairs(pairs):
    count, cols, lanes = pairs.shape
    part = pairs.reshape(count, cols, 2, lanes // 2)
    return part.transpose(3, 0, 2, 1).reshape(1, lanes // 2, 2 * count, cols)


def banded(taps):
    chans = taps.shape[2]
    zero = jnp.zeros_like(taps[:1])
    both = jnp.stack([jnp.concatenate([taps, zero]), jnp.concatenate([zero, taps])])
    both = both.reshape(2, 2, 2, 3, chans, chans)
    return both.transpose(1, 3, 2, 4, 0, 5).reshape(12 * chans, 2 * chans)


def sigmoid(value):
    return 0.5 * jnp.tanh(0.5 * value) + 0.5


def store_shifts(value, tmp, out, index):
    wide = value.shape[0]
    tmp[8 : 8 + wide] = value
    tmp[0:8] = value[wide - 8 :]
    tmp[8 + wide :] = value[:8]
    out[index, 0] = tmp[7 : 7 + wide].astype(BF)
    out[index, 1] = value.astype(BF)
    out[index, 2] = tmp[9 : 9 + wide].astype(BF)


def band_dot(shifts, index, weight):
    parts = [shifts[index + p, s] for p in range(2) for s in range(3)]
    return jnp.dot(jnp.concatenate(parts, axis=1), weight[...], preferred_element_type=F32)


def body(f_ref, g_ref, w1, w2, v2, v1, gf_ref, term_ref, fs, hs, ds2, ds1, slope, ht, ft, acc1, acc2, tmp):
    pairs = gf_ref.shape[0]
    cols = gf_ref.shape[1]
    wide = f_ref.shape[1]
    row, col = lax.axis_index("row"), lax.axis_index("col")
    top = (row > 0).astype(F32)
    bottom = (row < lax.axis_size("row") - 1).astype(F32)
    left = (col > 0).astype(F32)
    right = (col < lax.axis_size("col") - 1).astype(F32)
    place = lax.broadcasted_iota(jnp.int32, (RIM, LANES), 0)
    rim_mask = jnp.where(place < RIM // 2, right, left)
    upper = lax.broadcasted_iota(jnp.int32, (1, LANES), 1) < LANES // 2

    def row_mask(first):
        one = jnp.where(first < 0, top, jnp.where(first >= 2 * pairs, bottom, 1.0))
        two = jnp.where(first + 1 < 0, top, jnp.where(first + 1 >= 2 * pairs, bottom, 1.0))
        return jnp.where(upper, one, two)

    def masked(value, first):
        value = value * row_mask(first)
        return jnp.concatenate([value[:cols], value[cols:] * rim_mask], axis=0)

    @pl.loop(0, pairs + 4)
    def _(j):
        store_shifts(f_ref[j].astype(F32), tmp, fs, j)

    @pl.loop(0, pairs + 3)
    def _(j):
        pre = band_dot(fs, j, w1)
        sig = sigmoid(pre)
        act = pre * sig
        slope[j] = sig + act * (1.0 - sig)
        store_shifts(masked(act, 2 * j - 3), tmp, hs, j)

    @pl.loop(0, pairs + 2)
    def _(j):
        pre = band_dot(hs, j, w2)
        sig = sigmoid(pre)
        delta = g_ref[j].astype(F32) * (sig + pre * sig * (1.0 - sig))
        store_shifts(delta, tmp, ds2, j)

    @pl.loop(0, pairs + 1)
    def _(j):
        back = band_dot(ds2, j, v2)
        store_shifts(masked(back * slope[j + 1], 2 * j - 1), tmp, ds1, j)
        ht[j] = hs[j + 1, 1, :cols].T

    acc1[...] = jnp.zeros_like(acc1)
    acc2[...] = jnp.zeros_like(acc2)

    @pl.loop(0, pairs)
    def _(j):
        gf_ref[j] = band_dot(ds1, j, v1)[:cols].astype(BF)
        ft = fs[j + 2, 1, :cols].T
        near = jnp.concatenate([ds1[j + p, s, :cols] for p in range(2) for s in range(3)], axis=1)
        acc1[...] += jnp.dot(ft, near, preferred_element_type=F32)
        both = jnp.concatenate([ht[j], ht[j + 1]], axis=0)
        near = jnp.concatenate([ds2[j + 1, s, :cols] for s in range(3)], axis=1)
        acc2[...] += jnp.dot(both, near, preferred_element_type=F32)

    half = LANES // 2
    for ky in range(3):
        for kx in range(3):
            s = 2 - kx
            one = jnp.zeros((half, half), F32)
            two = jnp.zeros((half, half), F32)
            for a in range(2):
                b = a + 2 - ky
                q, r = b // 2, b % 2
                at = (q * 3 + s) * LANES + r * half
                one = one + acc1[a * half : (a + 1) * half, at : at + half]
                b = a + ky
                at = s * LANES + a * half
                two = two + acc2[b * half : (b + 1) * half, at : at + half]
            at = (ky * 3 + kx) * half
            term_ref[at : at + half] = jnp.concatenate([one, two], axis=1)


def fused(f_ext, g_ext, w1, w2, v2, v1, cols):
    pairs, wide = f_ext.shape[0] - 4, f_ext.shape[1]
    half = LANES // 2
    return pl.pallas_call(
        body,
        out_shape=(
            jax.ShapeDtypeStruct((pairs, cols, LANES), BF),
            jax.ShapeDtypeStruct((9 * half, LANES), F32),
        ),
        scratch_shapes=[
            pltpu.VMEM((pairs + 4, 3, wide, LANES), BF),
            pltpu.VMEM((pairs + 3, 3, wide, LANES), BF),
            pltpu.VMEM((pairs + 2, 3, wide, LANES), BF),
            pltpu.VMEM((pairs + 1, 3, wide, LANES), BF),
            pltpu.VMEM((pairs + 3, wide, LANES), F32),
            pltpu.VMEM((pairs + 1, LANES, cols), BF),
            pltpu.VMEM((pairs, LANES, cols), BF),
            pltpu.VMEM((LANES, 6 * LANES), F32),
            pltpu.VMEM((2 * LANES, 3 * LANES), F32),
            pltpu.VMEM((wide + 16, LANES), F32),
        ],
        compiler_params=pltpu.CompilerParams(vmem_limit_bytes=40 * 2**20),
        name="fused",
    )(f_ext, g_ext, w1, w2, v2, v1)


def reduced(term):
    sizes = [lax.axis_size(axis) for axis in AXES]
    if sizes[0] != 2 or any(size & (size - 1) for size in sizes):
        return lax.psum(term, AXES)
    half = term.shape[0] // 2
    me = lax.axis_index("dp")
    swap = [(0, 1), (1, 0)]
    mine = lax.dynamic_slice_in_dim(term, me * half, half, 0)
    other = lax.dynamic_slice_in_dim(term, (1 - me) * half, half, 0)
    part = mine + lax.ppermute(other, "dp", swap)
    steps = [("col", 1 << b) for b in range(sizes[2].bit_length() - 1)]
    steps += [("row", 1 << b) for b in range(sizes[1].bit_length() - 1)]
    count = len(steps)
    for at in range(count):
        perm = []
        for core in range(2):
            axis, bit = steps[(at + core * (count // 2)) % count]
            for r in range(sizes[1]):
                for c in range(sizes[2]):
                    to_r, to_c = (r ^ bit, c) if axis == "row" else (r, c ^ bit)
                    base = core * sizes[1]
                    perm.append(((base + r) * sizes[2] + c, (base + to_r) * sizes[2] + to_c))
        low = part.astype(BF)
        part = low.astype(F32) + lax.ppermute(low, AXES, perm).astype(F32)
    other = lax.ppermute(part, "dp", swap)
    return jnp.where(me == 0, jnp.concatenate([part, other]), jnp.concatenate([other, part]))


def shards(features, grad_out, kernel_one, kernel_two):
    slides, chans, rows, cols = features.shape
    pairs = rows // 2
    own = jnp.concatenate([to_pairs(features), to_pairs(grad_out)], axis=0)
    from_left, from_right = pair_exchange(own[:, :4], own[:, cols - 4 :], "col")
    filling = jnp.zeros((2 * pairs, RIM - 8, LANES), BF)
    wide = jnp.concatenate([own, from_right, filling, from_left], axis=1)
    feat, grad = wide[:pairs], wide[pairs:]
    low = jnp.concatenate([feat[:2], grad[:1]], axis=0)
    high = jnp.concatenate([feat[pairs - 2 :], grad[pairs - 1 :]], axis=0)
    above, below = pair_exchange(low, high, "row")
    f_ext = jnp.concatenate([above[:2], feat, below[:2]], axis=0)
    g_ext = jnp.concatenate([above[2:], grad, below[2:]], axis=0)
    w1 = banded(kernel_one.transpose(0, 1, 3, 2))
    w2 = banded(kernel_two.transpose(0, 1, 3, 2))
    v2 = banded(kernel_two[::-1, ::-1])
    v1 = banded(kernel_one[::-1, ::-1])
    gf, term = fused(f_ext, g_ext, w1, w2, v2, v1, cols)
    total = reduced(term)
    count = slides * lax.axis_size("dp") * rows * lax.axis_size("row") * cols * lax.axis_size("col")
    total = (total / jnp.sqrt(F32(count))).reshape(3, 3, chans, 2, chans).transpose(3, 0, 1, 4, 2)
    return from_pairs(gf), total[0], total[1]


def solution(mesh):
    return jax.shard_map(
        shards,
        mesh=mesh,
        in_specs=(P("dp", None, "row", "col"), P("dp", None, "row", "col"), P(), P()),
        out_specs=(P("dp", None, "row", "col"), P(), P()),
        check_vma=False,
    )
```

```python
import jax
import jax.numpy as jnp
from jax import lax
from jax.experimental import pallas as pl
from jax.experimental.pallas import tpu as pltpu
from jax.sharding import PartitionSpec as P

BF = jnp.bfloat16
F32 = jnp.float32
AXES = ("dp", "row", "col")
LANES = 128
HALF = LANES // 2
RIM = 16


def neighbours(axis, parity):
    count = lax.axis_size(axis)
    pairs = []
    for i in range(parity, count - 1, 2):
        pairs += [(i, i + 1), (i + 1, i)]
    return pairs


def is_low(axis, parity):
    return lax.axis_index(axis) % 2 == parity


def swap_one(low, high, axis):
    got = []
    for parity in range(2):
        perm = neighbours(axis, parity)
        if perm:
            got.append(lax.ppermute(jnp.where(is_low(axis, parity), high, low), axis, perm))
        else:
            got.append(jnp.zeros_like(low))
    even = is_low(axis, 0)
    return jnp.where(even, got[1], got[0]), jnp.where(even, got[0], got[1])


def swap_corners(corners):
    row_count, col_count = lax.axis_size("row"), lax.axis_size("col")
    got = {}
    for row_parity in range(2):
        for col_parity in range(2):
            perm = [
                (r * col_count + c, to_r * col_count + to_c)
                for r, to_r in neighbours("row", row_parity)
                for c, to_c in neighbours("col", col_parity)
            ]
            if not perm:
                got[row_parity, col_parity] = jnp.zeros_like(corners[0][0])
                continue
            down, right = is_low("row", row_parity), is_low("col", col_parity)
            sent = jnp.where(
                down, jnp.where(right, corners[1][1], corners[1][0]), jnp.where(right, corners[0][1], corners[0][0])
            )
            got[row_parity, col_parity] = lax.ppermute(sent, ("row", "col"), perm)
    even_row, even_col = is_low("row", 0), is_low("col", 0)

    def pick(row_parity, col_parity):
        across = [jnp.where(even_col, got[p, col_parity], got[p, 1 - col_parity]) for p in range(2)]
        return jnp.where(even_row, across[row_parity], across[1 - row_parity])

    return [[pick(1, 1), pick(1, 0)], [pick(0, 1), pick(0, 0)]]


def to_pairs(cells):
    _, chans, rows, cols = cells.shape
    part = cells[0].reshape(chans, rows // 2, 2, cols)
    return part.transpose(1, 3, 2, 0).reshape(rows // 2, cols, 2 * chans)


def from_pairs(pairs):
    count, cols, lanes = pairs.shape
    part = pairs.reshape(count, cols, 2, lanes // 2)
    return part.transpose(3, 0, 2, 1).reshape(1, lanes // 2, 2 * count, cols)


def weights_body(k1, k2, w1, w2, v2, v1):
    zero = jnp.zeros((HALF, HALF), BF)
    for taps, forward, backward in ((k1, w1, v1), (k2, w2, v2)):
        flat = {(ky, kx): taps[ky, kx] for ky in range(3) for kx in range(3)}
        turned = {at: flat[at].astype(F32).T.astype(BF) for at in flat}
        for p in range(2):
            for kx in range(3):
                for r in range(2):
                    at = ((p * 3 + kx) * 2 + r) * HALF
                    kys = [2 * p + r - a for a in range(2)]
                    forward[at : at + HALF] = jnp.concatenate([turned.get((ky, kx), zero) for ky in kys], axis=1)
                    backward[at : at + HALF] = jnp.concatenate([flat.get((2 - ky, 2 - kx), zero) for ky in kys], axis=1)


def make_weights(kernel_one, kernel_two):
    shape = jax.ShapeDtypeStruct((12 * HALF, LANES), BF)
    return pl.pallas_call(weights_body, out_shape=(shape,) * 4, name="weights")(kernel_one, kernel_two)


def sigmoid(value):
    return 0.5 * jnp.tanh(0.5 * value) + 0.5


def with_rim(own, right, left):
    own, right, left = own.astype(F32), right.astype(F32), left.astype(F32)
    return jnp.concatenate([own, right[: RIM // 2], left[RIM // 2 :]], axis=0)


def store_shifts(value, tmp, out, index):
    wide = value.shape[0]
    tmp[8 : 8 + wide] = value
    tmp[0:8] = value[wide - 8 :]
    tmp[8 + wide :] = value[:8]
    out[index, 0] = tmp[7 : 7 + wide].astype(BF)
    out[index, 1] = value.astype(BF)
    out[index, 2] = tmp[9 : 9 + wide].astype(BF)


def band_dot(first, second, weight):
    parts = [ref[index, s] for ref, index in (first, second) for s in range(3)]
    return jnp.dot(jnp.concatenate(parts, axis=1), weight[...], preferred_element_type=F32)


def edge_masks():
    row, col = lax.axis_index("row"), lax.axis_index("col")
    top = (row > 0).astype(F32)
    bottom = (row < lax.axis_size("row") - 1).astype(F32)
    left = (col > 0).astype(F32)
    right = (col < lax.axis_size("col") - 1).astype(F32)
    place = lax.broadcasted_iota(jnp.int32, (RIM, LANES), 0)
    rim = jnp.where(place < RIM // 2, right, left)
    return top, bottom, rim


def rim_masked(value, rim):
    own = value.shape[0] - RIM
    return jnp.concatenate([value[:own], value[own:] * rim], axis=0)


def add_one(acc, feat_t, pieces):
    near = jnp.concatenate(pieces, axis=1)
    acc[...] += jnp.dot(feat_t, near, preferred_element_type=F32)


def inner_body(f, g, c_left, c_right, w1, w2, v2, hs_edge, ds2_edge, slope_edge, ds1, acc1, acc2, fs, hs, ds2, slope, ht, tmp):
    pairs, cols = f.shape[:2]
    _, _, rim = edge_masks()

    @pl.loop(0, pairs)
    def _(j):
        store_shifts(with_rim(f[j], c_right[j], c_left[j]), tmp, fs, j)

    @pl.loop(0, pairs - 1)
    def _(j):
        pre = band_dot((fs, j), (fs, j + 1), w1)
        sig = sigmoid(pre)
        act = pre * sig
        slope[j] = sig + act * (1.0 - sig)
        store_shifts(rim_masked(act, rim), tmp, hs, j)
        ht[j] = hs[j, 1, :cols].T

    @pl.loop(0, pairs - 2)
    def _(j):
        pre = band_dot((hs, j), (hs, j + 1), w2)
        sig = sigmoid(pre)
        grad = with_rim(g[j + 1], c_right[pairs + j + 1], c_left[pairs + j + 1])
        delta = grad * (sig + pre * sig * (1.0 - sig))
        store_shifts(delta, tmp, ds2, j)

    @pl.loop(0, pairs - 3)
    def _(j):
        back = band_dot((ds2, j), (ds2, j + 1), v2)
        store_shifts(rim_masked(back * slope[j + 1], rim), tmp, ds1, j)

    acc1[...] = jnp.zeros_like(acc1)
    acc2[...] = jnp.zeros_like(acc2)

    @pl.loop(0, pairs - 2)
    def _(j):
        both = jnp.concatenate([ht[j], ht[j + 1]], axis=0)
        add_one(acc2, both, [ds2[j, s, :cols] for s in range(3)])

    @pl.loop(0, pairs - 4)
    def _(j):
        feat_t = fs[j + 2, 1, :cols].T
        add_one(acc1, feat_t, [ds1[j + p, s, :cols] for p in range(2) for s in range(3)])

    for side, at in ((0, 0), (1, pairs - 2)):
        hs_edge[side] = hs[at]
        slope_edge[side] = slope[at]
    for side, at in ((0, 0), (1, pairs - 3)):
        ds2_edge[side] = ds2[at]


def rim_body(
    f, g, c_left, c_right, above, below, c_above, c_below, w1, w2, v2, hs_edge, ds2_edge, slope_edge, ds1_in, acc1_in, acc2_in,
    ds1, term, fs, hs, ds2, slope, acc1, acc2, tmp,
):
    pairs, cols = f.shape[:2]
    top, bottom, rim = edge_masks()
    upper = lax.broadcasted_iota(jnp.int32, (1, LANES), 1) < HALF
    acc1[...] = acc1_in[...]
    acc2[...] = acc2_in[...]

    def own(ref, base, j):
        return with_rim(ref[j], c_right[base + j], c_left[base + j])

    def far(side, j):
        halo, corner = (above, c_above) if side == 0 else (below, c_below)
        return with_rim(halo[j], corner[1, j], corner[0, j])

    for side in range(2):
        flag = (top, bottom)[side]
        outer = jnp.where(upper, flag, 1.0) if side == 0 else jnp.where(upper, 1.0, flag)
        scratch = tmp.at[side]
        ends = (0, 1) if side == 0 else (1, 0)
        feats = [far(side, ends[0]), far(side, ends[1]), own(f, 0, 0 if side == 0 else pairs - 1)]
        for k in range(3):
            store_shifts(feats[k], scratch, fs.at[side], k)

        def order(one, two):
            return (one, two) if side == 0 else (two, one)

        for k in range(2):
            pre = band_dot(*order((fs.at[side], k), (fs.at[side], k + 1)), w1)
            sig = sigmoid(pre)
            act = pre * sig
            if k == 1:
                slope[side] = sig + act * (1.0 - sig)
            act = act * (flag if k == 0 else outer)
            store_shifts(rim_masked(act, rim), scratch, hs.at[side], k)
        for k in range(2):
            grad = far(side, 2) if k == 0 else own(g, pairs, 0 if side == 0 else pairs - 1)
            inward = (hs.at[side], 1) if k == 0 else (hs_edge, side)
            pre = band_dot(*order((hs.at[side], k), inward), w2)
            sig = sigmoid(pre)
            delta = grad * (sig + pre * sig * (1.0 - sig))
            store_shifts(delta, scratch, ds2.at[side], k)
        for k in range(2):
            inward = (ds2.at[side], 1) if k == 0 else (ds2_edge, side)
            back = band_dot(*order((ds2.at[side], k), inward), v2)
            if k == 0:
                value = back * slope[side] * outer
            else:
                value = back * slope_edge[side]
            at = k if side == 0 else pairs - k
            store_shifts(rim_masked(value, rim), scratch, ds1, at)

    for j in range(2, pairs - 1):
        ds1[j] = ds1_in[j - 2]
    for side in range(2):
        near, inward = hs[side, 1, 1, :cols].T, hs_edge[side, 1, :cols].T
        both = [near, inward] if side == 0 else [inward, near]
        add_one(acc2, jnp.concatenate(both, axis=0), [ds2[side, 1, s, :cols] for s in range(3)])
    for j in (0, 1, pairs - 2, pairs - 1):
        add_one(acc1, f[j].T, [ds1[j + p, s, :cols] for p in range(2) for s in range(3)])

    for ky in range(3):
        for kx in range(3):
            s = 2 - kx
            one = jnp.zeros((HALF, HALF), F32)
            two = jnp.zeros((HALF, HALF), F32)
            for a in range(2):
                b = a + 2 - ky
                at = (b // 2 * 3 + s) * LANES + b % 2 * HALF
                one = one + acc1[a * HALF : (a + 1) * HALF, at : at + HALF]
                b = a + ky
                at = s * LANES + a * HALF
                two = two + acc2[b * HALF : (b + 1) * HALF, at : at + HALF]
            at = (ky * 3 + kx) * HALF
            term[at : at + HALF] = jnp.concatenate([one, two], axis=1)


def last_body(ds1, v1, gf):
    pairs, cols = gf.shape[:2]

    @pl.loop(0, pairs)
    def _(j):
        gf[j] = band_dot((ds1, j), (ds1, j + 1), v1)[:cols].astype(BF)


def cost(pair_count):
    return pl.CostEstimate(flops=pair_count * 272 * 768 * 128 * 2, bytes_accessed=4 * 2**20, transcendentals=0)


PARAMS = pltpu.CompilerParams(vmem_limit_bytes=32 * 2**20)


def inner(f, g, c_left, c_right, w1, w2, v2):
    pairs, cols = f.shape[:2]
    wide = cols + RIM

    def shifts(count):
        return (count, 3, wide, LANES)

    return pl.pallas_call(
        inner_body,
        out_shape=(
            jax.ShapeDtypeStruct(shifts(2), BF),
            jax.ShapeDtypeStruct(shifts(2), BF),
            jax.ShapeDtypeStruct((2, wide, LANES), F32),
            jax.ShapeDtypeStruct(shifts(pairs - 3), BF),
            jax.ShapeDtypeStruct((LANES, 6 * LANES), F32),
            jax.ShapeDtypeStruct((2 * LANES, 3 * LANES), F32),
        ),
        scratch_shapes=[
            pltpu.VMEM(shifts(pairs), BF),
            pltpu.VMEM(shifts(pairs - 1), BF),
            pltpu.VMEM(shifts(pairs - 2), BF),
            pltpu.VMEM((pairs - 1, wide, LANES), F32),
            pltpu.VMEM((pairs - 1, LANES, cols), BF),
            pltpu.VMEM((wide + 16, LANES), F32),
        ],
        compiler_params=PARAMS,
        cost_estimate=cost(22),
        name="inner",
    )(f, g, c_left, c_right, w1, w2, v2)


def outer(f, *rest):
    pairs, cols = f.shape[:2]
    wide = cols + RIM

    def shifts(*count):
        return (*count, 3, wide, LANES)

    return pl.pallas_call(
        rim_body,
        out_shape=(
            jax.ShapeDtypeStruct(shifts(pairs + 1), BF),
            jax.ShapeDtypeStruct((9 * HALF, LANES), F32),
        ),
        scratch_shapes=[
            pltpu.VMEM(shifts(2, 3), BF),
            pltpu.VMEM(shifts(2, 2), BF),
            pltpu.VMEM(shifts(2, 2), BF),
            pltpu.VMEM((2, wide, LANES), F32),
            pltpu.VMEM((LANES, 6 * LANES), F32),
            pltpu.VMEM((2 * LANES, 3 * LANES), F32),
            pltpu.VMEM((2, wide + 16, LANES), F32),
        ],
        compiler_params=PARAMS,
        cost_estimate=cost(14),
        name="outer",
    )(f, *rest)


def last(ds1, v1, cols):
    return pl.pallas_call(
        last_body,
        out_shape=jax.ShapeDtypeStruct((ds1.shape[0] - 1, cols, LANES), BF),
        compiler_params=PARAMS,
        cost_estimate=cost(8),
        name="last",
    )(ds1, v1)


def reduced(term):
    sizes = [lax.axis_size(axis) for axis in AXES]
    if sizes[0] != 2 or any(size & (size - 1) for size in sizes):
        return lax.psum(term, AXES)
    half = term.shape[0] // 2
    me = lax.axis_index("dp")
    swap = [(0, 1), (1, 0)]
    mine = lax.dynamic_slice_in_dim(term, me * half, half, 0)
    other = lax.dynamic_slice_in_dim(term, (1 - me) * half, half, 0)
    part = mine + lax.ppermute(other, "dp", swap)
    across = [(0, 1 << b) for b in range(sizes[2].bit_length() - 1)]
    down = [(1 << b, 0) for b in range(sizes[1].bit_length() - 1)]
    bits = []
    while across or down:
        bits += down[:1] + across[:1]
        down, across = down[1:], across[1:]
    groups = [bits[at : at + 2] for at in range(0, len(bits), 2)]
    for at in range(len(groups)):
        mine = [groups[at], groups[(at + len(groups) // 2) % len(groups)]]
        if len(mine[0]) != len(mine[1]):
            mine[1] = mine[0]
        low = part.astype(BF)
        got = []
        for member in range(1, 1 << len(mine[0])):
            perm = []
            for core in range(2):
                flips = [flip for k, flip in enumerate(mine[core]) if member >> k & 1]
                for r in range(sizes[1]):
                    for c in range(sizes[2]):
                        to_r, to_c = r, c
                        for flip in flips:
                            to_r, to_c = to_r ^ flip[0], to_c ^ flip[1]
                        base = core * sizes[1]
                        perm.append(((base + r) * sizes[2] + c, (base + to_r) * sizes[2] + to_c))
            got.append(lax.ppermute(low, AXES, perm).astype(F32))
        part = low.astype(F32) + got[0]
        if len(got) > 1:
            part = part + (got[1] + got[2])
    other = lax.ppermute(part, "dp", swap)
    return jnp.where(me == 0, jnp.concatenate([part, other]), jnp.concatenate([other, part]))


def shards(features, grad_out, kernel_one, kernel_two):
    slides, chans, rows, cols = features.shape
    pairs = rows // 2
    feat, grad = to_pairs(features), to_pairs(grad_out)
    own = jnp.concatenate([feat, grad], axis=0)
    starts, ends = own[:, :RIM], own[:, cols - RIM :]
    c_left, c_right = swap_one(starts, ends, "col")
    low = jnp.concatenate([feat[:2], grad[:1]], axis=0)
    high = jnp.concatenate([feat[pairs - 2 :], grad[pairs - 1 :]], axis=0)
    above, below = swap_one(low, high, "row")
    corners = [[edge[:, :RIM], edge[:, cols - RIM :]] for edge in (low, high)]
    corners = swap_corners(corners)
    c_above, c_below = jnp.stack(corners[0]), jnp.stack(corners[1])
    w1, w2, v2, v1 = make_weights(kernel_one, kernel_two)
    state = inner(feat, grad, c_left, c_right, w1, w2, v2)
    ds1, term = outer(feat, grad, c_left, c_right, above, below, c_above, c_below, w1, w2, v2, *state)
    total = reduced(term)
    gf = last(ds1, v1, cols)
    count = slides * lax.axis_size("dp") * rows * lax.axis_size("row") * cols * lax.axis_size("col")
    total = (total / jnp.sqrt(F32(count))).reshape(3, 3, chans, 2, chans).transpose(3, 0, 1, 4, 2)
    return from_pairs(gf), total[0], total[1]


def solution(mesh):
    return jax.shard_map(
        shards,
        mesh=mesh,
        in_specs=(P("dp", None, "row", "col"), P("dp", None, "row", "col"), P(), P()),
        out_specs=(P("dp", None, "row", "col"), P(), P()),
        check_vma=False,
    )
```

```python
import functools

import jax
import jax.numpy as jnp
from jax import lax
from jax.experimental import pallas as pl
from jax.experimental.pallas import tpu as pltpu
from jax.sharding import PartitionSpec as P

BF = jnp.bfloat16
F32 = jnp.float32
AXES = ("dp", "row", "col")
LANES = 128
HALF = LANES // 2
RIM = 16


def neighbours(axis, parity):
    count = lax.axis_size(axis)
    pairs = []
    for i in range(parity, count - 1, 2):
        pairs += [(i, i + 1), (i + 1, i)]
    return pairs


def is_low(axis, parity):
    return lax.axis_index(axis) % 2 == parity


def swap_one(low, high, axis):
    got = []
    for parity in range(2):
        perm = neighbours(axis, parity)
        if perm:
            got.append(lax.ppermute(jnp.where(is_low(axis, parity), high, low), axis, perm))
        else:
            got.append(jnp.zeros_like(low))
    even = is_low(axis, 0)
    return jnp.where(even, got[1], got[0]), jnp.where(even, got[0], got[1])


def to_pairs(cells):
    _, chans, rows, cols = cells.shape
    part = cells[0].reshape(chans, rows // 2, 2, cols)
    return part.transpose(1, 3, 2, 0).reshape(rows // 2, cols, 2 * chans)


def from_pairs(pairs):
    count, cols, lanes = pairs.shape
    part = pairs.reshape(count, cols, 2, lanes // 2)
    return part.transpose(3, 0, 2, 1).reshape(1, lanes // 2, 2 * count, cols)


def weights_body(k1, k2, w1, w2, v2, v1):
    zero = jnp.zeros((HALF, HALF), BF)
    for taps, forward, backward in ((k1, w1, v1), (k2, w2, v2)):
        flat = {(ky, kx): taps[ky, kx] for ky in range(3) for kx in range(3)}
        turned = {at: flat[at].astype(F32).T.astype(BF) for at in flat}
        for p in range(2):
            for kx in range(3):
                for r in range(2):
                    at = ((p * 3 + kx) * 2 + r) * HALF
                    kys = [2 * p + r - a for a in range(2)]
                    forward[at : at + HALF] = jnp.concatenate([turned.get((ky, kx), zero) for ky in kys], axis=1)
                    backward[at : at + HALF] = jnp.concatenate([flat.get((2 - ky, 2 - kx), zero) for ky in kys], axis=1)


def make_weights(kernel_one, kernel_two):
    shape = jax.ShapeDtypeStruct((12 * HALF, LANES), BF)
    return pl.pallas_call(
        weights_body,
        out_shape=(shape,) * 4,
        compiler_params=pltpu.CompilerParams(vmem_limit_bytes=8 * 2**20),
        cost_estimate=cost(2),
        name="weights",
    )(kernel_one, kernel_two)


def sigmoid(value):
    return 0.5 * jnp.tanh(0.5 * value) + 0.5


def with_rim(own, rim):
    return jnp.concatenate([own.astype(F32), rim.astype(F32)], axis=0)


def store_shifts(value, tmp, out, index):
    wide = value.shape[0]
    tmp[8 : 8 + wide] = value
    tmp[0:8] = value[wide - 8 :]
    tmp[8 + wide :] = value[:8]
    out[index, 0] = tmp[7 : 7 + wide].astype(BF)
    out[index, 1] = value.astype(BF)
    out[index, 2] = tmp[9 : 9 + wide].astype(BF)


def band_dot(first, second, weight):
    parts = [ref[index, s] for ref, index in (first, second) for s in range(3)]
    return jnp.dot(jnp.concatenate(parts, axis=1), weight[...], preferred_element_type=F32)


def edge_masks():
    row, col = lax.axis_index("row"), lax.axis_index("col")
    top = (row > 0).astype(F32)
    bottom = (row < lax.axis_size("row") - 1).astype(F32)
    left = (col > 0).astype(F32)
    right = (col < lax.axis_size("col") - 1).astype(F32)
    place = lax.broadcasted_iota(jnp.int32, (RIM, LANES), 0)
    rim = jnp.where(place < RIM // 2, right, left)
    return top, bottom, rim


def rim_masked(value, rim):
    own = value.shape[0] - RIM
    return jnp.concatenate([value[:own], value[own:] * rim], axis=0)


def add_one(acc, feat_t, pieces):
    near = jnp.concatenate(pieces, axis=1)
    acc[...] += jnp.dot(feat_t, near, preferred_element_type=F32)


def inner_body(f, g, edge, w1, w2, v2, hs_edge, ds2_edge, slope_edge, ds1, acc1, acc2, fs, hs, ds2, slope, ht, tmp):
    pairs, cols = f.shape[:2]
    _, _, rim = edge_masks()

    @pl.loop(0, pairs)
    def _(j):
        store_shifts(with_rim(f[j], edge[j]), tmp, fs, j)

    @pl.loop(0, pairs - 1)
    def _(j):
        pre = band_dot((fs, j), (fs, j + 1), w1)
        sig = sigmoid(pre)
        act = pre * sig
        slope[j] = sig + act * (1.0 - sig)
        store_shifts(rim_masked(act, rim), tmp, hs, j)
        ht[j] = hs[j, 1, :cols].T

    @pl.loop(0, pairs - 2)
    def _(j):
        pre = band_dot((hs, j), (hs, j + 1), w2)
        sig = sigmoid(pre)
        grad = with_rim(g[j + 1], edge[pairs + j + 1])
        delta = grad * (sig + pre * sig * (1.0 - sig))
        store_shifts(delta, tmp, ds2, j)

    @pl.loop(0, pairs - 3)
    def _(j):
        back = band_dot((ds2, j), (ds2, j + 1), v2)
        store_shifts(rim_masked(back * slope[j + 1], rim), tmp, ds1, j)

    acc1[...] = jnp.zeros_like(acc1)
    acc2[...] = jnp.zeros_like(acc2)

    @pl.loop(0, pairs - 2)
    def _(j):
        both = jnp.concatenate([ht[j], ht[j + 1]], axis=0)
        add_one(acc2, both, [ds2[j, s, :cols] for s in range(3)])

    @pl.loop(0, pairs - 4)
    def _(j):
        feat_t = fs[j + 2, 1, :cols].T
        add_one(acc1, feat_t, [ds1[j + p, s, :cols] for p in range(2) for s in range(3)])

    for side, at in ((0, 0), (1, pairs - 2)):
        hs_edge[side] = hs[at]
        slope_edge[side] = slope[at]
    for side, at in ((0, 0), (1, pairs - 3)):
        ds2_edge[side] = ds2[at]


def rim_body(
    f, g, edge, above, below, w1, w2, v2, hs_edge, ds2_edge, slope_edge, ds1_in, acc1_in, acc2_in,
    ds1, term, fs, hs, ds2, slope, acc1, acc2, tmp,
):
    pairs, cols = f.shape[:2]
    top, bottom, rim = edge_masks()
    upper = lax.broadcasted_iota(jnp.int32, (1, LANES), 1) < HALF
    acc1[...] = acc1_in[...]
    acc2[...] = acc2_in[...]

    def own(ref, base, j):
        return with_rim(ref[j], edge[base + j])

    def far(side, j):
        return (above, below)[side][j].astype(F32)

    for side in range(2):
        flag = (top, bottom)[side]
        outer = jnp.where(upper, flag, 1.0) if side == 0 else jnp.where(upper, 1.0, flag)
        scratch = tmp.at[side]
        ends = (0, 1) if side == 0 else (1, 0)
        feats = [far(side, ends[0]), far(side, ends[1]), own(f, 0, 0 if side == 0 else pairs - 1)]
        for k in range(3):
            store_shifts(feats[k], scratch, fs.at[side], k)

        def order(one, two):
            return (one, two) if side == 0 else (two, one)

        for k in range(2):
            pre = band_dot(*order((fs.at[side], k), (fs.at[side], k + 1)), w1)
            sig = sigmoid(pre)
            act = pre * sig
            if k == 1:
                slope[side] = sig + act * (1.0 - sig)
            act = act * (flag if k == 0 else outer)
            store_shifts(rim_masked(act, rim), scratch, hs.at[side], k)
        for k in range(2):
            grad = far(side, 2) if k == 0 else own(g, pairs, 0 if side == 0 else pairs - 1)
            inward = (hs.at[side], 1) if k == 0 else (hs_edge, side)
            pre = band_dot(*order((hs.at[side], k), inward), w2)
            sig = sigmoid(pre)
            delta = grad * (sig + pre * sig * (1.0 - sig))
            store_shifts(delta, scratch, ds2.at[side], k)
        for k in range(2):
            inward = (ds2.at[side], 1) if k == 0 else (ds2_edge, side)
            back = band_dot(*order((ds2.at[side], k), inward), v2)
            if k == 0:
                value = back * slope[side] * outer
            else:
                value = back * slope_edge[side]
            at = k if side == 0 else pairs - k
            store_shifts(rim_masked(value, rim), scratch, ds1, at)

    for j in range(2, pairs - 1):
        ds1[j] = ds1_in[j - 2]
    for side in range(2):
        near, inward = hs[side, 1, 1, :cols].T, hs_edge[side, 1, :cols].T
        both = [near, inward] if side == 0 else [inward, near]
        add_one(acc2, jnp.concatenate(both, axis=0), [ds2[side, 1, s, :cols] for s in range(3)])
    for j in (0, 1, pairs - 2, pairs - 1):
        add_one(acc1, f[j].T, [ds1[j + p, s, :cols] for p in range(2) for s in range(3)])

    for ky in range(3):
        for kx in range(3):
            s = 2 - kx
            one = jnp.zeros((HALF, HALF), F32)
            two = jnp.zeros((HALF, HALF), F32)
            for a in range(2):
                b = a + 2 - ky
                at = (b // 2 * 3 + s) * LANES + b % 2 * HALF
                one = one + acc1[a * HALF : (a + 1) * HALF, at : at + HALF]
                b = a + ky
                at = s * LANES + a * HALF
                two = two + acc2[b * HALF : (b + 1) * HALF, at : at + HALF]
            at = (ky * 3 + kx) * HALF
            term[at : at + HALF] = jnp.concatenate([one, two], axis=1)


def last_body(ds1, v1, gf, done):
    pairs, cols = gf.shape[:2]
    done[...] = jnp.zeros_like(done)

    @pl.loop(0, pairs)
    def _(j):
        gf[j] = band_dot((ds1, j), (ds1, j + 1), v1)[:cols].astype(BF)


def cost(pair_count):
    return pl.CostEstimate(flops=pair_count * 272 * 768 * 128 * 2, bytes_accessed=4 * 2**20, transcendentals=0)


PARAMS = pltpu.CompilerParams(vmem_limit_bytes=32 * 2**20)


def inner(f, g, edge, w1, w2, v2):
    pairs, cols = f.shape[:2]
    wide = cols + RIM

    def shifts(count):
        return (count, 3, wide, LANES)

    return pl.pallas_call(
        inner_body,
        out_shape=(
            jax.ShapeDtypeStruct(shifts(2), BF),
            jax.ShapeDtypeStruct(shifts(2), BF),
            jax.ShapeDtypeStruct((2, wide, LANES), F32),
            jax.ShapeDtypeStruct(shifts(pairs - 3), BF),
            jax.ShapeDtypeStruct((LANES, 6 * LANES), F32),
            jax.ShapeDtypeStruct((2 * LANES, 3 * LANES), F32),
        ),
        scratch_shapes=[
            pltpu.VMEM(shifts(pairs), BF),
            pltpu.VMEM(shifts(pairs - 1), BF),
            pltpu.VMEM(shifts(pairs - 2), BF),
            pltpu.VMEM((pairs - 1, wide, LANES), F32),
            pltpu.VMEM((pairs - 1, LANES, cols), BF),
            pltpu.VMEM((wide + 16, LANES), F32),
        ],
        compiler_params=PARAMS,
        cost_estimate=cost(22),
        name="inner",
    )(f, g, edge, w1, w2, v2)


def outer(f, *rest):
    pairs, cols = f.shape[:2]
    wide = cols + RIM

    def shifts(*count):
        return (*count, 3, wide, LANES)

    return pl.pallas_call(
        rim_body,
        out_shape=(
            jax.ShapeDtypeStruct(shifts(pairs + 1), BF),
            jax.ShapeDtypeStruct((9 * HALF, LANES), F32),
        ),
        scratch_shapes=[
            pltpu.VMEM(shifts(2, 3), BF),
            pltpu.VMEM(shifts(2, 2), BF),
            pltpu.VMEM(shifts(2, 2), BF),
            pltpu.VMEM((2, wide, LANES), F32),
            pltpu.VMEM((LANES, 6 * LANES), F32),
            pltpu.VMEM((2 * LANES, 3 * LANES), F32),
            pltpu.VMEM((2, wide + 16, LANES), F32),
        ],
        compiler_params=PARAMS,
        cost_estimate=cost(14),
        name="outer",
    )(f, *rest)


def last(ds1, v1, cols):
    return pl.pallas_call(
        last_body,
        out_shape=(
            jax.ShapeDtypeStruct((ds1.shape[0] - 1, cols, LANES), BF),
            jax.ShapeDtypeStruct((8, LANES), F32),
        ),
        compiler_params=PARAMS,
        cost_estimate=cost(8),
        name="last",
    )(ds1, v1)


def four_body(own, one, two, three, done, out):
    low = [ref[...].astype(F32) for ref in (own, one, two, three)]
    out[...] = ((low[0] + low[1]) + (low[2] + low[3])).astype(BF)


def sum_four(own, got, done):
    return pl.pallas_call(
        four_body,
        out_shape=jax.ShapeDtypeStruct(own.shape, BF),
        compiler_params=pltpu.CompilerParams(vmem_limit_bytes=4 * 2**20),
        name="sum_four",
    )(own, *got, done)


def finish_body(part, other, one, two, *, scale):
    half = part.shape[0]
    first = lax.axis_index("dp") == 0
    for tap in range(9):
        rows = []
        for at in range(tap * HALF, (tap + 1) * HALF, HALF // 2):
            side, at = (0, at) if at < half else (1, at - half)
            mine, theirs = part[at : at + HALF // 2], other[at : at + HALF // 2]
            rows.append(jnp.where(first, mine, theirs) if side == 0 else jnp.where(first, theirs, mine))
        both = jnp.concatenate(rows, axis=0).T * scale
        one[tap // 3, tap % 3] = both[:HALF]
        two[tap // 3, tap % 3] = both[HALF:]


def finish(part, other, scale):
    shape = jax.ShapeDtypeStruct((3, 3, HALF, HALF), F32)
    return pl.pallas_call(
        functools.partial(finish_body, scale=scale),
        out_shape=(shape, shape),
        compiler_params=pltpu.CompilerParams(vmem_limit_bytes=4 * 2**20),
        name="finish",
    )(part, other)


def reduced(term, done):
    sizes = [lax.axis_size(axis) for axis in AXES]
    if sizes[0] != 2 or any(size & (size - 1) for size in sizes):
        total = lax.psum(term, AXES)
        half = term.shape[0] // 2
        both = total[:half], total[half:]
        core = lax.axis_index("dp") == 0
        return jnp.where(core, *both), jnp.where(core, both[1], both[0])
    half = term.shape[0] // 2
    me = lax.axis_index("dp")
    swap = [(0, 1), (1, 0)]
    mine = lax.dynamic_slice_in_dim(term, me * half, half, 0)
    other = lax.dynamic_slice_in_dim(term, (1 - me) * half, half, 0)
    part = mine + lax.ppermute(other, "dp", swap)
    across = [(0, 1 << b) for b in range(sizes[2].bit_length() - 1)]
    down = [(1 << b, 0) for b in range(sizes[1].bit_length() - 1)]
    bits = []
    while across or down:
        bits += down[:1] + across[:1]
        down, across = down[1:], across[1:]
    groups = [bits[at : at + 2] for at in range(0, len(bits), 2)]
    for at in range(len(groups)):
        mine = [groups[at], groups[(at + len(groups) // 2) % len(groups)]]
        if len(mine[0]) != len(mine[1]):
            mine[1] = mine[0]
        low = part.astype(BF)
        got = []
        for member in range(1, 1 << len(mine[0])):
            perm = []
            for core in range(2):
                flips = [flip for k, flip in enumerate(mine[core]) if member >> k & 1]
                for r in range(sizes[1]):
                    for c in range(sizes[2]):
                        to_r, to_c = r, c
                        for flip in flips:
                            to_r, to_c = to_r ^ flip[0], to_c ^ flip[1]
                        base = core * sizes[1]
                        perm.append(((base + r) * sizes[2] + c, (base + to_r) * sizes[2] + to_c))
            got.append(lax.ppermute(low, AXES, perm))
        if at == 0 and len(got) > 1 and len(groups) > 1:
            part = sum_four(low, got, done)
            continue
        got = [one.astype(F32) for one in got]
        part = low.astype(F32) + got[0]
        if len(got) > 1:
            part = part + (got[1] + got[2])
    return part, lax.ppermute(part, "dp", swap)


def shards(features, grad_out, kernel_one, kernel_two):
    slides, chans, rows, cols = features.shape
    pairs = rows // 2
    feat, grad = to_pairs(features), to_pairs(grad_out)
    own = jnp.concatenate([feat, grad], axis=0)
    from_left, from_right = swap_one(own[:, : RIM // 2], own[:, cols - RIM // 2 :], "col")
    edge = jnp.concatenate([from_right, from_left], axis=1)
    w1, w2, v2, v1 = make_weights(kernel_one, kernel_two)
    low = jnp.concatenate([feat[:2], grad[:1]], axis=0)
    high = jnp.concatenate([feat[pairs - 2 :], grad[pairs - 1 :]], axis=0)
    low_edge = jnp.concatenate([edge[:2], edge[pairs : pairs + 1]], axis=0)
    high_edge = jnp.concatenate([edge[pairs - 2 : pairs], edge[2 * pairs - 1 :]], axis=0)
    low, high = jnp.concatenate([low, low_edge], axis=1), jnp.concatenate([high, high_edge], axis=1)
    above, below = swap_one(low, high, "row")
    state = inner(feat, grad, edge, w1, w2, v2)
    ds1, term = outer(feat, grad, edge, above, below, w1, w2, v2, *state)
    gf, done = last(ds1, v1, cols)
    part, other = reduced(term, done)
    count = slides * lax.axis_size("dp") * rows * lax.axis_size("row") * cols * lax.axis_size("col")
    grad_one, grad_two = finish(part, other, float(count) ** -0.5)
    return from_pairs(gf), grad_one, grad_two


def solution(mesh):
    return jax.shard_map(
        shards,
        mesh=mesh,
        in_specs=(P("dp", None, "row", "col"), P("dp", None, "row", "col"), P(), P()),
        out_specs=(P("dp", None, "row", "col"), P(), P()),
        check_vma=False,
    )
```

```python
import functools

import jax
import jax.numpy as jnp
from jax import lax
from jax.experimental import pallas as pl
from jax.experimental.pallas import tpu as pltpu
from jax.sharding import PartitionSpec as P

BF = jnp.bfloat16
F32 = jnp.float32
AXES = ("dp", "row", "col")
LANES = 128
HALF = LANES // 2
RIM = 16


def neighbours(axis, parity):
    count = lax.axis_size(axis)
    pairs = []
    for i in range(parity, count - 1, 2):
        pairs += [(i, i + 1), (i + 1, i)]
    return pairs


def is_low(axis, parity):
    return lax.axis_index(axis) % 2 == parity


def swap_one(low, high, axis):
    got = []
    for parity in range(2):
        perm = neighbours(axis, parity)
        if perm:
            got.append(lax.ppermute(jnp.where(is_low(axis, parity), high, low), axis, perm))
        else:
            got.append(jnp.zeros_like(low))
    even = is_low(axis, 0)
    return jnp.where(even, got[1], got[0]), jnp.where(even, got[0], got[1])


def to_pairs(cells):
    _, chans, rows, cols = cells.shape
    part = cells[0].reshape(chans, rows // 2, 2, cols)
    return part.transpose(1, 3, 2, 0).reshape(rows // 2, cols, 2 * chans)


def from_pairs(pairs):
    count, cols, lanes = pairs.shape
    part = pairs.reshape(count, cols, 2, lanes // 2)
    return part.transpose(3, 0, 2, 1).reshape(1, lanes // 2, 2 * count, cols)


def weights_body(k1, k2, w1, w2, v2, v1):
    zero = jnp.zeros((HALF, HALF), BF)
    for taps, forward, backward in ((k1, w1, v1), (k2, w2, v2)):
        flat = {(ky, kx): taps[ky, kx] for ky in range(3) for kx in range(3)}
        turned = {at: flat[at].astype(F32).T.astype(BF) for at in flat}
        for p in range(2):
            for kx in range(3):
                for r in range(2):
                    at = ((p * 3 + kx) * 2 + r) * HALF
                    kys = [2 * p + r - a for a in range(2)]
                    forward[at : at + HALF] = jnp.concatenate([turned.get((ky, kx), zero) for ky in kys], axis=1)
                    backward[at : at + HALF] = jnp.concatenate([flat.get((2 - ky, 2 - kx), zero) for ky in kys], axis=1)


def make_weights(kernel_one, kernel_two):
    shape = jax.ShapeDtypeStruct((12 * HALF, LANES), BF)
    return pl.pallas_call(
        weights_body,
        out_shape=(shape,) * 4,
        compiler_params=pltpu.CompilerParams(vmem_limit_bytes=8 * 2**20),
        cost_estimate=cost(2),
        name="weights",
    )(kernel_one, kernel_two)


def sigmoid(value):
    return 0.5 * jnp.tanh(0.5 * value) + 0.5


def with_rim(own, rim):
    return jnp.concatenate([own.astype(F32), rim.astype(F32)], axis=0)


def store_shifts(value, out, index):
    out[index, 0] = pltpu.roll(value, 1, 0).astype(BF)
    out[index, 1] = value.astype(BF)
    out[index, 2] = pltpu.roll(value, value.shape[0] - 1, 0).astype(BF)


def band_dot(first, second, weight):
    parts = [ref[index, s] for ref, index in (first, second) for s in range(3)]
    return jnp.dot(jnp.concatenate(parts, axis=1), weight[...], preferred_element_type=F32)


def edge_masks():
    row, col = lax.axis_index("row"), lax.axis_index("col")
    top = (row > 0).astype(F32)
    bottom = (row < lax.axis_size("row") - 1).astype(F32)
    left = (col > 0).astype(F32)
    right = (col < lax.axis_size("col") - 1).astype(F32)
    place = lax.broadcasted_iota(jnp.int32, (RIM, LANES), 0)
    rim = jnp.where(place < RIM // 2, right, left)
    return top, bottom, rim


def rim_masked(value, rim):
    own = value.shape[0] - RIM
    return jnp.concatenate([value[:own], value[own:] * rim], axis=0)


def add_one(acc, feat_t, pieces):
    near = jnp.concatenate(pieces, axis=1)
    acc[...] += jnp.dot(feat_t, near, preferred_element_type=F32)


def inner_body(f, g, edge, w1, w2, v2, hs_edge, ds2_edge, slope_edge, ds1, acc1, acc2, fs, hs, ds2, slope, ht):
    pairs, cols = f.shape[:2]
    _, _, rim = edge_masks()

    @pl.loop(0, pairs, unroll=True)
    def _(j):
        store_shifts(with_rim(f[j], edge[j]), fs, j)

    @pl.loop(0, pairs - 1, unroll=True)
    def _(j):
        pre = band_dot((fs, j), (fs, j + 1), w1)
        sig = sigmoid(pre)
        act = pre * sig
        slope[j] = sig + act * (1.0 - sig)
        store_shifts(rim_masked(act, rim), hs, j)
        ht[j] = hs[j, 1, :cols].T

    @pl.loop(0, pairs - 2, unroll=True)
    def _(j):
        pre = band_dot((hs, j), (hs, j + 1), w2)
        sig = sigmoid(pre)
        grad = with_rim(g[j + 1], edge[pairs + j + 1])
        delta = grad * (sig + pre * sig * (1.0 - sig))
        store_shifts(delta, ds2, j)

    @pl.loop(0, pairs - 3, unroll=True)
    def _(j):
        back = band_dot((ds2, j), (ds2, j + 1), v2)
        store_shifts(rim_masked(back * slope[j + 1], rim), ds1, j)

    acc1[...] = jnp.zeros_like(acc1)
    acc2[...] = jnp.zeros_like(acc2)

    @pl.loop(0, pairs - 2, unroll=True)
    def _(j):
        both = jnp.concatenate([ht[j], ht[j + 1]], axis=0)
        add_one(acc2, both, [ds2[j, s, :cols] for s in range(3)])

    @pl.loop(0, pairs - 4, unroll=True)
    def _(j):
        feat_t = fs[j + 2, 1, :cols].T
        add_one(acc1, feat_t, [ds1[j + p, s, :cols] for p in range(2) for s in range(3)])

    for side, at in ((0, 0), (1, pairs - 2)):
        hs_edge[side] = hs[at]
        slope_edge[side] = slope[at]
    for side, at in ((0, 0), (1, pairs - 3)):
        ds2_edge[side] = ds2[at]


def rim_body(
    f, g, edge, above, below, w1, w2, v2, hs_edge, ds2_edge, slope_edge, ds1_in, acc1_in, acc2_in,
    ds1, term, fs, hs, ds2, slope, acc1, acc2,
):
    pairs, cols = f.shape[:2]
    top, bottom, rim = edge_masks()
    upper = lax.broadcasted_iota(jnp.int32, (1, LANES), 1) < HALF
    acc1[...] = acc1_in[...]
    acc2[...] = acc2_in[...]

    def own(ref, base, j):
        return with_rim(ref[j], edge[base + j])

    def far(side, j):
        return (above, below)[side][j].astype(F32)

    flags = (top, bottom)
    outers = (jnp.where(upper, top, 1.0), jnp.where(upper, 1.0, bottom))
    ends = ((0, 1), (1, 0))
    near = (0, pairs - 1)

    def order(side, one, two):
        return (one, two) if side == 0 else (two, one)

    for k in range(3):
        for side in range(2):
            feat = far(side, ends[side][k]) if k < 2 else own(f, 0, near[side])
            store_shifts(feat, fs.at[side], k)
    for k in range(2):
        for side in range(2):
            pre = band_dot(*order(side, (fs.at[side], k), (fs.at[side], k + 1)), w1)
            sig = sigmoid(pre)
            act = pre * sig
            if k == 1:
                slope[side] = sig + act * (1.0 - sig)
            act = act * (flags[side] if k == 0 else outers[side])
            store_shifts(rim_masked(act, rim), hs.at[side], k)
    for k in (1, 0):
        for side in range(2):
            grad = far(side, 2) if k == 0 else own(g, pairs, near[side])
            inward = (hs.at[side], 1) if k == 0 else (hs_edge, side)
            pre = band_dot(*order(side, (hs.at[side], k), inward), w2)
            sig = sigmoid(pre)
            delta = grad * (sig + pre * sig * (1.0 - sig))
            store_shifts(delta, ds2.at[side], k)
    for k in (1, 0):
        for side in range(2):
            inward = (ds2.at[side], 1) if k == 0 else (ds2_edge, side)
            back = band_dot(*order(side, (ds2.at[side], k), inward), v2)
            value = back * slope[side] * outers[side] if k == 0 else back * slope_edge[side]
            at = k if side == 0 else pairs - k
            store_shifts(rim_masked(value, rim), ds1, at)

    for j in range(2, pairs - 1):
        ds1[j] = ds1_in[j - 2]
    for side in range(2):
        near, inward = hs[side, 1, 1, :cols].T, hs_edge[side, 1, :cols].T
        both = [near, inward] if side == 0 else [inward, near]
        add_one(acc2, jnp.concatenate(both, axis=0), [ds2[side, 1, s, :cols] for s in range(3)])
    for j in (0, 1, pairs - 2, pairs - 1):
        add_one(acc1, f[j].T, [ds1[j + p, s, :cols] for p in range(2) for s in range(3)])

    for ky in range(3):
        for kx in range(3):
            s = 2 - kx
            one = jnp.zeros((HALF, HALF), F32)
            two = jnp.zeros((HALF, HALF), F32)
            for a in range(2):
                b = a + 2 - ky
                at = (b // 2 * 3 + s) * LANES + b % 2 * HALF
                one = one + acc1[a * HALF : (a + 1) * HALF, at : at + HALF]
                b = a + ky
                at = s * LANES + a * HALF
                two = two + acc2[b * HALF : (b + 1) * HALF, at : at + HALF]
            at = (ky * 3 + kx) * HALF
            term[at : at + HALF] = jnp.concatenate([one, two], axis=1)


def last_body(ds1, v1, gf, done):
    pairs, cols = gf.shape[:2]
    done[...] = jnp.zeros_like(done)

    @pl.loop(0, pairs, unroll=True)
    def _(j):
        gf[j] = band_dot((ds1, j), (ds1, j + 1), v1)[:cols].astype(BF)


def cost(pair_count):
    return pl.CostEstimate(flops=pair_count * 272 * 768 * 128 * 2, bytes_accessed=4 * 2**20, transcendentals=0)


PARAMS = pltpu.CompilerParams(vmem_limit_bytes=32 * 2**20)


def inner(f, g, edge, w1, w2, v2):
    pairs, cols = f.shape[:2]
    wide = cols + RIM

    def shifts(count):
        return (count, 3, wide, LANES)

    return pl.pallas_call(
        inner_body,
        out_shape=(
            jax.ShapeDtypeStruct(shifts(2), BF),
            jax.ShapeDtypeStruct(shifts(2), BF),
            jax.ShapeDtypeStruct((2, wide, LANES), F32),
            jax.ShapeDtypeStruct(shifts(pairs - 3), BF),
            jax.ShapeDtypeStruct((LANES, 6 * LANES), F32),
            jax.ShapeDtypeStruct((2 * LANES, 3 * LANES), F32),
        ),
        scratch_shapes=[
            pltpu.VMEM(shifts(pairs), BF),
            pltpu.VMEM(shifts(pairs - 1), BF),
            pltpu.VMEM(shifts(pairs - 2), BF),
            pltpu.VMEM((pairs - 1, wide, LANES), F32),
            pltpu.VMEM((pairs - 1, LANES, cols), BF),
        ],
        compiler_params=PARAMS,
        cost_estimate=cost(22),
        name="inner",
    )(f, g, edge, w1, w2, v2)


def outer(f, *rest):
    pairs, cols = f.shape[:2]
    wide = cols + RIM

    def shifts(*count):
        return (*count, 3, wide, LANES)

    return pl.pallas_call(
        rim_body,
        out_shape=(
            jax.ShapeDtypeStruct(shifts(pairs + 1), BF),
            jax.ShapeDtypeStruct((9 * HALF, LANES), F32),
        ),
        scratch_shapes=[
            pltpu.VMEM(shifts(2, 3), BF),
            pltpu.VMEM(shifts(2, 2), BF),
            pltpu.VMEM(shifts(2, 2), BF),
            pltpu.VMEM((2, wide, LANES), F32),
            pltpu.VMEM((LANES, 6 * LANES), F32),
            pltpu.VMEM((2 * LANES, 3 * LANES), F32),
        ],
        compiler_params=PARAMS,
        cost_estimate=cost(14),
        name="outer",
    )(f, *rest)


def last(ds1, v1, cols):
    return pl.pallas_call(
        last_body,
        out_shape=(
            jax.ShapeDtypeStruct((ds1.shape[0] - 1, cols, LANES), BF),
            jax.ShapeDtypeStruct((8, LANES), F32),
        ),
        compiler_params=PARAMS,
        cost_estimate=cost(8),
        name="last",
    )(ds1, v1)


def four_body(own, one, two, three, done, out):
    low = [ref[...].astype(F32) for ref in (own, one, two, three)]
    out[...] = ((low[0] + low[1]) + (low[2] + low[3])).astype(BF)


def sum_four(own, got, done):
    return pl.pallas_call(
        four_body,
        out_shape=jax.ShapeDtypeStruct(own.shape, BF),
        compiler_params=pltpu.CompilerParams(vmem_limit_bytes=4 * 2**20),
        name="sum_four",
    )(own, *got, done)


def finish_body(part, other, one, two, *, scale):
    half = part.shape[0]
    first = lax.axis_index("dp") == 0
    for tap in range(9):
        rows = []
        for at in range(tap * HALF, (tap + 1) * HALF, HALF // 2):
            side, at = (0, at) if at < half else (1, at - half)
            mine, theirs = part[at : at + HALF // 2], other[at : at + HALF // 2]
            rows.append(jnp.where(first, mine, theirs) if side == 0 else jnp.where(first, theirs, mine))
        both = jnp.concatenate(rows, axis=0).T * scale
        one[tap // 3, tap % 3] = both[:HALF]
        two[tap // 3, tap % 3] = both[HALF:]


def finish(part, other, scale):
    shape = jax.ShapeDtypeStruct((3, 3, HALF, HALF), F32)
    return pl.pallas_call(
        functools.partial(finish_body, scale=scale),
        out_shape=(shape, shape),
        compiler_params=pltpu.CompilerParams(vmem_limit_bytes=4 * 2**20),
        name="finish",
    )(part, other)


def reduced(term, done):
    sizes = [lax.axis_size(axis) for axis in AXES]
    if sizes[0] != 2 or any(size & (size - 1) for size in sizes):
        total = lax.psum(term, AXES)
        half = term.shape[0] // 2
        both = total[:half], total[half:]
        core = lax.axis_index("dp") == 0
        return jnp.where(core, *both), jnp.where(core, both[1], both[0])
    half = term.shape[0] // 2
    me = lax.axis_index("dp")
    swap = [(0, 1), (1, 0)]
    mine = lax.dynamic_slice_in_dim(term, me * half, half, 0)
    other = lax.dynamic_slice_in_dim(term, (1 - me) * half, half, 0)
    part = mine + lax.ppermute(other, "dp", swap)
    across = [(0, 1 << b) for b in range(sizes[2].bit_length() - 1)]
    down = [(1 << b, 0) for b in range(sizes[1].bit_length() - 1)]
    bits = []
    while across or down:
        bits += down[:1] + across[:1]
        down, across = down[1:], across[1:]
    groups = [bits[at : at + 2] for at in range(0, len(bits), 2)]
    for at in range(len(groups)):
        mine = [groups[at], groups[(at + len(groups) // 2) % len(groups)]]
        if len(mine[0]) != len(mine[1]):
            mine[1] = mine[0]
        low = part.astype(BF)
        got = []
        for member in range(1, 1 << len(mine[0])):
            perm = []
            for core in range(2):
                flips = [flip for k, flip in enumerate(mine[core]) if member >> k & 1]
                for r in range(sizes[1]):
                    for c in range(sizes[2]):
                        to_r, to_c = r, c
                        for flip in flips:
                            to_r, to_c = to_r ^ flip[0], to_c ^ flip[1]
                        base = core * sizes[1]
                        perm.append(((base + r) * sizes[2] + c, (base + to_r) * sizes[2] + to_c))
            got.append(lax.ppermute(low, AXES, perm))
        if at == 0 and len(got) > 1 and len(groups) > 1:
            part = sum_four(low, got, done)
            continue
        got = [one.astype(F32) for one in got]
        part = low.astype(F32) + got[0]
        if len(got) > 1:
            part = part + (got[1] + got[2])
    return part, lax.ppermute(part, "dp", swap)


def shards(features, grad_out, kernel_one, kernel_two):
    slides, chans, rows, cols = features.shape
    pairs = rows // 2
    feat, grad = to_pairs(features), to_pairs(grad_out)
    own = jnp.concatenate([feat, grad], axis=0)
    from_left, from_right = swap_one(own[:, : RIM // 2], own[:, cols - RIM // 2 :], "col")
    edge = jnp.concatenate([from_right, from_left], axis=1)
    w1, w2, v2, v1 = make_weights(kernel_one, kernel_two)
    low = jnp.concatenate([feat[:2], grad[:1]], axis=0)
    high = jnp.concatenate([feat[pairs - 2 :], grad[pairs - 1 :]], axis=0)
    low_edge = jnp.concatenate([edge[:2], edge[pairs : pairs + 1]], axis=0)
    high_edge = jnp.concatenate([edge[pairs - 2 : pairs], edge[2 * pairs - 1 :]], axis=0)
    low, high = jnp.concatenate([low, low_edge], axis=1), jnp.concatenate([high, high_edge], axis=1)
    above, below = swap_one(low, high, "row")
    state = inner(feat, grad, edge, w1, w2, v2)
    ds1, term = outer(feat, grad, edge, above, below, w1, w2, v2, *state)
    gf, done = last(ds1, v1, cols)
    part, other = reduced(term, done)
    count = slides * lax.axis_size("dp") * rows * lax.axis_size("row") * cols * lax.axis_size("col")
    grad_one, grad_two = finish(part, other, float(count) ** -0.5)
    return from_pairs(gf), grad_one, grad_two


def solution(mesh):
    return jax.shard_map(
        shards,
        mesh=mesh,
        in_specs=(P("dp", None, "row", "col"), P("dp", None, "row", "col"), P(), P()),
        out_specs=(P("dp", None, "row", "col"), P(), P()),
        check_vma=False,
    )
```

```python
import functools

import jax
import jax.numpy as jnp
from jax import lax
from jax.experimental import pallas as pl
from jax.experimental.pallas import tpu as pltpu
from jax.sharding import PartitionSpec as P

BF = jnp.bfloat16
F32 = jnp.float32
AXES = ("dp", "row", "col")
LANES = 128
HALF = LANES // 2
RIM = 16


def neighbours(axis, parity):
    count = lax.axis_size(axis)
    pairs = []
    for i in range(parity, count - 1, 2):
        pairs += [(i, i + 1), (i + 1, i)]
    return pairs


def is_low(axis, parity):
    return lax.axis_index(axis) % 2 == parity


def shift_both(low, high, axis):
    ends = lax.axis_size(axis) - 1
    from_prev = lax.ppermute(high, axis, [(i, i + 1) for i in range(ends)])
    return from_prev, lax.ppermute(low, axis, [(i + 1, i) for i in range(ends)])


def swap_one(low, high, axis):
    got = []
    for parity in range(2):
        perm = neighbours(axis, parity)
        if perm:
            got.append(lax.ppermute(jnp.where(is_low(axis, parity), high, low), axis, perm))
        else:
            got.append(jnp.zeros_like(low))
    even = is_low(axis, 0)
    return jnp.where(even, got[1], got[0]), jnp.where(even, got[0], got[1])


def to_pairs(cells):
    _, chans, rows, cols = cells.shape
    part = cells[0].reshape(chans, rows // 2, 2, cols)
    return part.transpose(1, 3, 2, 0).reshape(rows // 2, cols, 2 * chans)


def from_pairs(pairs):
    count, cols, lanes = pairs.shape
    part = pairs.reshape(count, cols, 2, lanes // 2)
    return part.transpose(3, 0, 2, 1).reshape(1, lanes // 2, 2 * count, cols)


def weights_body(k1, k2, w1, w2, v2, v1):
    zero = jnp.zeros((HALF, HALF), BF)
    for taps, forward, backward in ((k1, w1, v1), (k2, w2, v2)):
        flat = {(ky, kx): taps[ky, kx] for ky in range(3) for kx in range(3)}
        turned = {at: flat[at].astype(F32).T.astype(BF) for at in flat}
        for p in range(2):
            for kx in range(3):
                for r in range(2):
                    at = ((p * 3 + kx) * 2 + r) * HALF
                    kys = [2 * p + r - a for a in range(2)]
                    forward[at : at + HALF] = jnp.concatenate([turned.get((ky, kx), zero) for ky in kys], axis=1)
                    backward[at : at + HALF] = jnp.concatenate([flat.get((2 - ky, 2 - kx), zero) for ky in kys], axis=1)


def make_weights(kernel_one, kernel_two):
    shape = jax.ShapeDtypeStruct((12 * HALF, LANES), BF)
    return pl.pallas_call(
        weights_body,
        out_shape=(shape,) * 4,
        compiler_params=pltpu.CompilerParams(vmem_limit_bytes=8 * 2**20),
        cost_estimate=cost(2),
        name="weights",
    )(kernel_one, kernel_two)


def sigmoid(value):
    return 0.5 * jnp.tanh(0.5 * value) + 0.5


def with_rim(own, rim):
    return jnp.concatenate([own.astype(F32), rim.astype(F32)], axis=0)


def store_shifts(value, out, index):
    out[index, 0] = pltpu.roll(value, 1, 0).astype(BF)
    out[index, 1] = value.astype(BF)
    out[index, 2] = pltpu.roll(value, value.shape[0] - 1, 0).astype(BF)


def band_dot(first, second, weight):
    parts = [ref[index, s] for ref, index in (first, second) for s in range(3)]
    return jnp.dot(jnp.concatenate(parts, axis=1), weight[...], preferred_element_type=F32)


def edge_masks():
    row, col = lax.axis_index("row"), lax.axis_index("col")
    top = (row > 0).astype(F32)
    bottom = (row < lax.axis_size("row") - 1).astype(F32)
    left = (col > 0).astype(F32)
    right = (col < lax.axis_size("col") - 1).astype(F32)
    place = lax.broadcasted_iota(jnp.int32, (RIM, LANES), 0)
    rim = jnp.where(place < RIM // 2, right, left)
    return top, bottom, rim


def rim_masked(value, rim):
    own = value.shape[0] - RIM
    return jnp.concatenate([value[:own], value[own:] * rim], axis=0)


def add_one(acc, feat_t, pieces):
    near = jnp.concatenate(pieces, axis=1)
    acc[...] += jnp.dot(feat_t, near, preferred_element_type=F32)


def inner_body(f, g, edge, w1, w2, v2, hs_edge, ds2_edge, slope_edge, ds1, acc1, acc2, fs, hs, ds2, slope, ht, ft):
    pairs, cols = f.shape[:2]
    _, _, rim = edge_masks()

    @pl.loop(0, pairs, unroll=True)
    def _(j):
        store_shifts(with_rim(f[j], edge[j]), fs, j)

    @pl.loop(0, pairs - 1, unroll=True)
    def _(j):
        pre = band_dot((fs, j), (fs, j + 1), w1)
        sig = sigmoid(pre)
        act = pre * sig
        slope[j] = sig + act * (1.0 - sig)
        store_shifts(rim_masked(act, rim), hs, j)
        ht[j] = hs[j, 1, :cols].T

    @pl.loop(0, pairs - 2, unroll=True)
    def _(j):
        pre = band_dot((hs, j), (hs, j + 1), w2)
        sig = sigmoid(pre)
        grad = with_rim(g[j + 1], edge[pairs + j + 1])
        delta = grad * (sig + pre * sig * (1.0 - sig))
        store_shifts(delta, ds2, j)

    @pl.loop(0, pairs - 3, unroll=True)
    def _(j):
        back = band_dot((ds2, j), (ds2, j + 1), v2)
        store_shifts(rim_masked(back * slope[j + 1], rim), ds1, j)

    acc1[...] = jnp.zeros_like(acc1)
    acc2[...] = jnp.zeros_like(acc2)

    @pl.loop(0, pairs - 2, unroll=True)
    def _(j):
        both = jnp.concatenate([ht[j], ht[j + 1]], axis=0)
        add_one(acc2, both, [ds2[j, s, :cols] for s in range(3)])

    @pl.loop(1, pairs - 1, unroll=True)
    def _(j):
        ft[j] = f[j].T

    @pl.loop(0, pairs - 3, unroll=True)
    def _(j):
        both = jnp.concatenate([ft[j + 1], ft[j + 2]], axis=0)
        add_one(acc1, both, [ds1[j, s, :cols] for s in range(3)])

    for side, at in ((0, 0), (1, pairs - 2)):
        hs_edge[side] = hs[at]
        slope_edge[side] = slope[at]
    for side, at in ((0, 0), (1, pairs - 3)):
        ds2_edge[side] = ds2[at]


def take_terms(acc1, acc2, term):
    for ky in range(3):
        for kx in range(3):
            at = (2 - kx) * LANES
            sums = []
            for acc in (acc1, acc2):
                first = acc[ky * HALF : (ky + 1) * HALF, at : at + HALF]
                sums.append(first + acc[(ky + 1) * HALF : (ky + 2) * HALF, at + HALF : at + LANES])
            at = (ky * 3 + kx) * HALF
            term[at : at + HALF] = jnp.concatenate(sums, axis=1)


def half_lanes(side):
    upper = lax.broadcasted_iota(jnp.int32, (1, LANES), 1) >= HALF
    return upper == (side == 1)


def rim_body(
    f, g, edge, halo, w1, w2, v2, hs_edge, ds2_edge, slope_edge, acc1_in, acc2_in, ds1, row, acc1, acc2, *rest, side
):
    if side == 0:
        fs, hs, ds2, slope = rest
    else:
        term, fs, hs, ds2, slope = rest
    pairs, cols = f.shape[:2]
    top, bottom, rim = edge_masks()
    flag = (top, bottom)[side]
    beyond = half_lanes(side)
    outer = jnp.where(beyond, flag, 1.0)
    near, next_near = (0, 1) if side == 0 else (pairs - 1, pairs - 2)
    mixed = halo[1].astype(F32)

    def order(one, two):
        return (one, two) if side == 0 else (two, one)

    store_shifts(jnp.where(beyond, 0.0, mixed), fs, 0)
    store_shifts(halo[0].astype(F32), fs, 1)
    store_shifts(with_rim(f[near], edge[near]), fs, 2)
    for k in (1, 0):
        pre = band_dot(*order((fs, k), (fs, k + 1)), w1)
        sig = sigmoid(pre)
        act = pre * sig
        if k == 1:
            slope[...] = sig + act * (1.0 - sig)
        act = act * (flag if k == 0 else outer)
        store_shifts(rim_masked(act, rim), hs, k)
    far_grad = jnp.where(beyond, 0.0, pltpu.roll(mixed, HALF, 1))
    for k in (1, 0):
        grad = far_grad if k == 0 else with_rim(g[near], edge[pairs + near])
        inward = (hs, 1) if k == 0 else (hs_edge, side)
        pre = band_dot(*order((hs, k), inward), w2)
        sig = sigmoid(pre)
        delta = grad * (sig + pre * sig * (1.0 - sig))
        store_shifts(delta, ds2, k)
    for k in (1, 0):
        inward = (ds2, 1) if k == 0 else (ds2_edge, side)
        back = band_dot(*order((ds2, k), inward), v2)
        value = back * slope[...] if k == 0 else back * slope_edge[side]
        if k == 0:
            value = jnp.where(beyond, 0.0, value)
        value = rim_masked(value, rim)
        store_shifts(value, ds1, k)
        if k == 0:
            first, second = value[: row.shape[0]], value[value.shape[0] - row.shape[0] :]
            turned = (first, second)[side]
            turned = pltpu.roll(turned, HALF, 1)
            row[...] = ((turned + second) if side == 0 else (first + turned)).astype(BF)

    acc1[...] = acc1_in[...]
    acc2[...] = acc2_in[...]
    hid = order(hs[1, 1, :cols].T, hs_edge[side, 1, :cols].T)
    add_one(acc2, jnp.concatenate(hid, axis=0), [ds2[1, s, :cols] for s in range(3)])
    own = f[near].T
    for k in range(2):
        feat = order(halo[0, :cols].T, own) if k == 0 else order(own, f[next_near].T)
        add_one(acc1, jnp.concatenate(feat, axis=0), [ds1[k, s, :cols] for s in range(3)])
    if side == 1:
        take_terms(acc1, acc2, term)


def with_row(center, row, side):
    turned = pltpu.roll(row, HALF, 1)
    first, second = (row, turned) if side == 0 else (turned, row)
    cols = center.shape[0] - row.shape[0]
    full = jnp.concatenate([first[:cols], second], axis=0)
    return jnp.where(half_lanes(side), full, center)


def last_body(ds1_top, ds1, ds1_bottom, prev_row, next_row, v1, gf, done, ends):
    pairs, cols = gf.shape[:2]
    done[...] = jnp.zeros_like(done)
    store_shifts(with_row(ds1_top[0, 1].astype(F32), prev_row[...].astype(F32), 0), ends, 0)
    store_shifts(with_row(ds1_bottom[0, 1].astype(F32), next_row[...].astype(F32), 1), ends, 1)
    places = [(ends, 0), (ds1_top, 1)] + [(ds1, j) for j in range(pairs - 3)] + [(ds1_bottom, 1), (ends, 1)]
    for j in range(pairs):
        gf[j] = band_dot(places[j], places[j + 1], v1)[:cols].astype(BF)


def cost(pair_count):
    return pl.CostEstimate(flops=pair_count * 272 * 768 * 128 * 2, bytes_accessed=4 * 2**20, transcendentals=0)


PARAMS = pltpu.CompilerParams(vmem_limit_bytes=32 * 2**20)


def inner(f, g, edge, w1, w2, v2):
    pairs, cols = f.shape[:2]
    wide = cols + RIM

    def shifts(count):
        return (count, 3, wide, LANES)

    return pl.pallas_call(
        inner_body,
        out_shape=(
            jax.ShapeDtypeStruct(shifts(2), BF),
            jax.ShapeDtypeStruct(shifts(2), BF),
            jax.ShapeDtypeStruct((2, wide, LANES), F32),
            jax.ShapeDtypeStruct(shifts(pairs - 3), BF),
            jax.ShapeDtypeStruct((2 * LANES, 3 * LANES), F32),
            jax.ShapeDtypeStruct((2 * LANES, 3 * LANES), F32),
        ),
        scratch_shapes=[
            pltpu.VMEM(shifts(pairs), BF),
            pltpu.VMEM(shifts(pairs - 1), BF),
            pltpu.VMEM(shifts(pairs - 2), BF),
            pltpu.VMEM((pairs - 1, wide, LANES), F32),
            pltpu.VMEM((pairs - 1, LANES, cols), BF),
            pltpu.VMEM((pairs - 1, LANES, cols), BF),
        ],
        compiler_params=PARAMS,
        cost_estimate=cost(22),
        name="inner",
    )(f, g, edge, w1, w2, v2)


def outer(side, f, *rest):
    wide = f.shape[1] + RIM
    acc = jax.ShapeDtypeStruct((2 * LANES, 3 * LANES), F32)

    def shifts(count):
        return (count, 3, wide, LANES)

    out_shape = [
        jax.ShapeDtypeStruct(shifts(2), BF),
        jax.ShapeDtypeStruct((wide // 2 + RIM // 2, LANES), BF),
        acc,
        acc,
    ]
    if side == 1:
        out_shape.append(jax.ShapeDtypeStruct((9 * HALF, LANES), F32))
    return pl.pallas_call(
        functools.partial(rim_body, side=side),
        out_shape=out_shape,
        scratch_shapes=[
            pltpu.VMEM(shifts(3), BF),
            pltpu.VMEM(shifts(2), BF),
            pltpu.VMEM(shifts(2), BF),
            pltpu.VMEM((wide, LANES), F32),
        ],
        compiler_params=PARAMS,
        cost_estimate=cost(8),
        name=("upper", "lower")[side],
    )(f, *rest)


def last(ds1_top, ds1, ds1_bottom, prev_row, next_row, v1, cols):
    pairs = ds1.shape[0] + 3
    return pl.pallas_call(
        last_body,
        out_shape=(
            jax.ShapeDtypeStruct((pairs, cols, LANES), BF),
            jax.ShapeDtypeStruct((8, LANES), F32),
        ),
        scratch_shapes=[pltpu.VMEM((2, 3, cols + RIM, LANES), BF)],
        compiler_params=PARAMS,
        cost_estimate=cost(8),
        name="last",
    )(ds1_top, ds1, ds1_bottom, prev_row, next_row, v1)


def four_body(own, one, two, three, done, out):
    low = [ref[...].astype(F32) for ref in (own, one, two, three)]
    out[...] = (low[0] + low[1]) + (low[2] + low[3])


def sum_four(own, got, done):
    return pl.pallas_call(
        four_body,
        out_shape=jax.ShapeDtypeStruct(own.shape, F32),
        compiler_params=pltpu.CompilerParams(vmem_limit_bytes=4 * 2**20),
        name="sum_four",
    )(own, *got, done)


def finish_body(part, other, one, two, *, scale):
    half = part.shape[0]
    first = lax.axis_index("dp") == 0
    for tap in range(9):
        rows = []
        for at in range(tap * HALF, (tap + 1) * HALF, HALF // 2):
            side, at = (0, at) if at < half else (1, at - half)
            mine, theirs = part[at : at + HALF // 2], other[at : at + HALF // 2]
            rows.append(jnp.where(first, mine, theirs) if side == 0 else jnp.where(first, theirs, mine))
        both = jnp.concatenate(rows, axis=0).T * scale
        one[tap // 3, tap % 3] = both[:HALF]
        two[tap // 3, tap % 3] = both[HALF:]


def finish(part, other, scale):
    shape = jax.ShapeDtypeStruct((3, 3, HALF, HALF), F32)
    return pl.pallas_call(
        functools.partial(finish_body, scale=scale),
        out_shape=(shape, shape),
        compiler_params=pltpu.CompilerParams(vmem_limit_bytes=4 * 2**20),
        name="finish",
    )(part, other)


def reduced(term, done):
    sizes = [lax.axis_size(axis) for axis in AXES]
    if sizes[0] != 2 or any(size & (size - 1) for size in sizes):
        total = lax.psum(term, AXES)
        half = term.shape[0] // 2
        both = total[:half], total[half:]
        core = lax.axis_index("dp") == 0
        return jnp.where(core, *both), jnp.where(core, both[1], both[0])
    half = term.shape[0] // 2
    me = lax.axis_index("dp")
    swap = [(0, 1), (1, 0)]
    mine = lax.dynamic_slice_in_dim(term, me * half, half, 0)
    other = lax.dynamic_slice_in_dim(term, (1 - me) * half, half, 0)
    part = mine + lax.ppermute(other, "dp", swap)
    across = [(0, 1 << b) for b in range(sizes[2].bit_length() - 1)]
    down = [(1 << b, 0) for b in range(sizes[1].bit_length() - 1)]
    bits = []
    while across or down:
        bits += down[:1] + across[:1]
        down, across = down[1:], across[1:]
    groups = [bits[at : at + 2] for at in range(0, len(bits), 2)]
    for at in range(len(groups)):
        mine = [groups[at], groups[(at + len(groups) // 2) % len(groups)]]
        if len(mine[0]) != len(mine[1]):
            mine[1] = mine[0]
        low = part.astype(BF)
        got = []
        for member in range(1, 1 << len(mine[0])):
            perm = []
            for core in range(2):
                flips = [flip for k, flip in enumerate(mine[core]) if member >> k & 1]
                for r in range(sizes[1]):
                    for c in range(sizes[2]):
                        to_r, to_c = r, c
                        for flip in flips:
                            to_r, to_c = to_r ^ flip[0], to_c ^ flip[1]
                        base = core * sizes[1]
                        perm.append(((base + r) * sizes[2] + c, (base + to_r) * sizes[2] + to_c))
            got.append(lax.ppermute(low, AXES, perm))
        if at == 1 and len(got) > 1:
            part = sum_four(low, got, done)
            continue
        got = [one.astype(F32) for one in got]
        part = low.astype(F32) + got[0]
        if len(got) > 1:
            part = part + (got[1] + got[2])
    return part, lax.ppermute(part, "dp", swap)


def shards(features, grad_out, kernel_one, kernel_two):
    slides, chans, rows, cols = features.shape
    pairs = rows // 2
    feat, grad = to_pairs(features), to_pairs(grad_out)
    own = jnp.concatenate([feat, grad], axis=0)
    from_left, from_right = swap_one(own[:, : RIM // 2], own[:, cols - RIM // 2 :], "col")
    edge = jnp.concatenate([from_right, from_left], axis=1)
    w1, w2, v2, v1 = make_weights(kernel_one, kernel_two)
    low = jnp.stack([feat[0], jnp.concatenate([feat[1, :, :HALF], grad[0, :, :HALF]], axis=1)])
    high = jnp.stack([feat[-1], jnp.concatenate([grad[-1, :, HALF:], feat[-2, :, HALF:]], axis=1)])
    feat_edge, grad_edge = edge[:pairs], edge[pairs:]
    low_edge = jnp.stack([feat_edge[0], jnp.concatenate([feat_edge[1, :, :HALF], grad_edge[0, :, :HALF]], axis=1)])
    high_edge = jnp.stack([feat_edge[-1], jnp.concatenate([grad_edge[-1, :, HALF:], feat_edge[-2, :, HALF:]], axis=1)])
    low, high = jnp.concatenate([low, low_edge], axis=1), jnp.concatenate([high, high_edge], axis=1)
    above, below = shift_both(low, high, "row")
    hs_edge, ds2_edge, slope_edge, ds1, acc1, acc2 = inner(feat, grad, edge, w1, w2, v2)
    shared = (w1, w2, v2, hs_edge, ds2_edge, slope_edge)
    ds1_top, low_row, acc1, acc2 = outer(0, feat, grad, edge, above, *shared, acc1, acc2)
    ds1_bottom, high_row, _, _, term = outer(1, feat, grad, edge, below, *shared, acc1, acc2)
    prev_row, next_row = shift_both(low_row, high_row, "row")
    gf, done = last(ds1_top, ds1, ds1_bottom, prev_row, next_row, v1, cols)
    part, other = reduced(term, done)
    count = slides * lax.axis_size("dp") * rows * lax.axis_size("row") * cols * lax.axis_size("col")
    grad_one, grad_two = finish(part, other, float(count) ** -0.5)
    return from_pairs(gf), grad_one, grad_two


def solution(mesh):
    return jax.shard_map(
        shards,
        mesh=mesh,
        in_specs=(P("dp", None, "row", "col"), P("dp", None, "row", "col"), P(), P()),
        out_specs=(P("dp", None, "row", "col"), P(), P()),
        check_vma=False,
    )
```

```python
import functools

import jax
import jax.numpy as jnp
from jax import lax
from jax.experimental import pallas as pl
from jax.experimental.pallas import tpu as pltpu
from jax.sharding import PartitionSpec as P

BF = jnp.bfloat16
F32 = jnp.float32
AXES = ("dp", "row", "col")
LANES = 128
HALF = LANES // 2
RIM = 16


def neighbours(axis, parity):
    count = lax.axis_size(axis)
    pairs = []
    for i in range(parity, count - 1, 2):
        pairs += [(i, i + 1), (i + 1, i)]
    return pairs


def is_low(axis, parity):
    return lax.axis_index(axis) % 2 == parity


def swap_one(low, high, axis):
    got = []
    for parity in range(2):
        perm = neighbours(axis, parity)
        if perm:
            got.append(lax.ppermute(jnp.where(is_low(axis, parity), high, low), axis, perm))
        else:
            got.append(jnp.zeros_like(low))
    even = is_low(axis, 0)
    return jnp.where(even, got[1], got[0]), jnp.where(even, got[0], got[1])


def to_pairs(cells):
    _, chans, rows, cols = cells.shape
    part = cells[0].reshape(chans, rows // 2, 2, cols)
    return part.transpose(1, 3, 2, 0).reshape(rows // 2, cols, 2 * chans)


def from_pairs(pairs):
    count, cols, lanes = pairs.shape
    part = pairs.reshape(count, cols, 2, lanes // 2)
    return part.transpose(3, 0, 2, 1).reshape(1, lanes // 2, 2 * count, cols)


def weights_body(k1, k2, w1, w2, v2, v1):
    zero = jnp.zeros((HALF, HALF), BF)
    for taps, forward, backward in ((k1, w1, v1), (k2, w2, v2)):
        flat = {(ky, kx): taps[ky, kx] for ky in range(3) for kx in range(3)}
        turned = {at: flat[at].astype(F32).T.astype(BF) for at in flat}
        for p in range(2):
            for kx in range(3):
                for r in range(2):
                    at = ((p * 3 + kx) * 2 + r) * HALF
                    kys = [2 * p + r - a for a in range(2)]
                    forward[at : at + HALF] = jnp.concatenate([turned.get((ky, kx), zero) for ky in kys], axis=1)
                    backward[at : at + HALF] = jnp.concatenate([flat.get((2 - ky, 2 - kx), zero) for ky in kys], axis=1)


def make_weights(kernel_one, kernel_two):
    shape = jax.ShapeDtypeStruct((12 * HALF, LANES), BF)
    return pl.pallas_call(
        weights_body,
        out_shape=(shape,) * 4,
        compiler_params=pltpu.CompilerParams(vmem_limit_bytes=8 * 2**20),
        cost_estimate=cost(2),
        name="weights",
    )(kernel_one, kernel_two)


def sigmoid(value):
    return 0.5 * jnp.tanh(0.5 * value) + 0.5


def with_rim(own, rim):
    return jnp.concatenate([own.astype(F32), rim.astype(F32)], axis=0)


def store_shifts(value, out, index):
    out[index, 0] = pltpu.roll(value, 1, 0).astype(BF)
    out[index, 1] = value.astype(BF)
    out[index, 2] = pltpu.roll(value, value.shape[0] - 1, 0).astype(BF)


def band_dot(first, second, weight):
    parts = [ref[index, s] for ref, index in (first, second) for s in range(3)]
    return jnp.dot(jnp.concatenate(parts, axis=1), weight[...], preferred_element_type=F32)


def edge_masks():
    row, col = lax.axis_index("row"), lax.axis_index("col")
    top = (row > 0).astype(F32)
    bottom = (row < lax.axis_size("row") - 1).astype(F32)
    left = (col > 0).astype(F32)
    right = (col < lax.axis_size("col") - 1).astype(F32)
    place = lax.broadcasted_iota(jnp.int32, (RIM, LANES), 0)
    rim = jnp.where(place < RIM // 2, right, left)
    return top, bottom, rim


def rim_masked(value, rim):
    own = value.shape[0] - RIM
    return jnp.concatenate([value[:own], value[own:] * rim], axis=0)


def add_one(acc, feat_t, pieces):
    near = jnp.concatenate(pieces, axis=1)
    acc[...] += jnp.dot(feat_t, near, preferred_element_type=F32)


def inner_body(f, g, edge, w1, w2, v2, hs_edge, ds2_edge, slope_edge, ds1, acc1, acc2, fs, hs, ds2, slope, ht, ft):
    pairs, cols = f.shape[:2]
    _, _, rim = edge_masks()

    @pl.loop(0, pairs, unroll=True)
    def _(j):
        store_shifts(with_rim(f[j], edge[j]), fs, j)

    @pl.loop(0, pairs - 1, unroll=True)
    def _(j):
        pre = band_dot((fs, j), (fs, j + 1), w1)
        sig = sigmoid(pre)
        act = pre * sig
        slope[j] = sig + act * (1.0 - sig)
        store_shifts(rim_masked(act, rim), hs, j)
        ht[j] = hs[j, 1, :cols].T

    @pl.loop(0, pairs - 2, unroll=True)
    def _(j):
        pre = band_dot((hs, j), (hs, j + 1), w2)
        sig = sigmoid(pre)
        grad = with_rim(g[j + 1], edge[pairs + j + 1])
        delta = grad * (sig + pre * sig * (1.0 - sig))
        store_shifts(delta, ds2, j)

    @pl.loop(0, pairs - 3, unroll=True)
    def _(j):
        back = band_dot((ds2, j), (ds2, j + 1), v2)
        store_shifts(rim_masked(back * slope[j + 1], rim), ds1, j)

    acc1[...] = jnp.zeros_like(acc1)
    acc2[...] = jnp.zeros_like(acc2)

    @pl.loop(0, pairs - 2, unroll=True)
    def _(j):
        both = jnp.concatenate([ht[j], ht[j + 1]], axis=0)
        add_one(acc2, both, [ds2[j, s, :cols] for s in range(3)])

    @pl.loop(1, pairs - 1, unroll=True)
    def _(j):
        ft[j] = f[j].T

    @pl.loop(0, pairs - 3, unroll=True)
    def _(j):
        both = jnp.concatenate([ft[j + 1], ft[j + 2]], axis=0)
        add_one(acc1, both, [ds1[j, s, :cols] for s in range(3)])

    for side, at in ((0, 0), (1, pairs - 2)):
        hs_edge[side] = hs[at]
        slope_edge[side] = slope[at]
    for side, at in ((0, 0), (1, pairs - 3)):
        ds2_edge[side] = ds2[at]


def take_terms(acc1, acc2, term):
    for ky in range(3):
        for kx in range(3):
            at = (2 - kx) * LANES
            sums = []
            for acc in (acc1, acc2):
                first = acc[ky * HALF : (ky + 1) * HALF, at : at + HALF]
                sums.append(first + acc[(ky + 1) * HALF : (ky + 2) * HALF, at + HALF : at + LANES])
            at = (ky * 3 + kx) * HALF
            term[at : at + HALF] = jnp.concatenate(sums, axis=1)


def half_lanes(side):
    upper = lax.broadcasted_iota(jnp.int32, (1, LANES), 1) >= HALF
    return upper == (side == 1)


def rim_body(
    f, g, edge, above, below, w1, w2, v2, hs_edge, ds2_edge, slope_edge, acc1_in, acc2_in,
    ds1_top, ds1_bottom, row_top, row_bottom, term, fs, hs, ds2, slope, acc1, acc2,
):
    pairs, cols = f.shape[:2]
    top, bottom, rim = edge_masks()
    flags = (top, bottom)
    beyond = [half_lanes(side) for side in range(2)]
    halo, ds1, rows = (above, below), (ds1_top, ds1_bottom), (row_top, row_bottom)
    near, next_near = (0, pairs - 1), (1, pairs - 2)
    mixed = [ref[1].astype(F32) for ref in halo]
    sides = range(2)

    def order(side, one, two):
        return (one, two) if side == 0 else (two, one)

    for side in sides:
        store_shifts(jnp.where(beyond[side], 0.0, mixed[side]), fs.at[side], 0)
        store_shifts(halo[side][0].astype(F32), fs.at[side], 1)
        store_shifts(with_rim(f[near[side]], edge[near[side]]), fs.at[side], 2)
    for k in (1, 0):
        for side in sides:
            pre = band_dot(*order(side, (fs.at[side], k), (fs.at[side], k + 1)), w1)
            sig = sigmoid(pre)
            act = pre * sig
            if k == 1:
                slope[side] = sig + act * (1.0 - sig)
            act = act * (flags[side] if k == 0 else jnp.where(beyond[side], flags[side], 1.0))
            store_shifts(rim_masked(act, rim), hs.at[side], k)
    for k in (1, 0):
        for side in sides:
            if k == 0:
                grad = jnp.where(beyond[side], 0.0, pltpu.roll(mixed[side], HALF, 1))
            else:
                grad = with_rim(g[near[side]], edge[pairs + near[side]])
            inward = (hs.at[side], 1) if k == 0 else (hs_edge, side)
            pre = band_dot(*order(side, (hs.at[side], k), inward), w2)
            sig = sigmoid(pre)
            delta = grad * (sig + pre * sig * (1.0 - sig))
            store_shifts(delta, ds2.at[side], k)
    for k in (1, 0):
        for side in sides:
            inward = (ds2.at[side], 1) if k == 0 else (ds2_edge, side)
            back = band_dot(*order(side, (ds2.at[side], k), inward), v2)
            value = back * slope[side] if k == 0 else back * slope_edge[side]
            if k == 0:
                value = jnp.where(beyond[side], 0.0, value)
            value = rim_masked(value, rim)
            store_shifts(value, ds1[side], k)
            if k == 0:
                tall = rows[side].shape[0]
                first, second = value[:tall], value[value.shape[0] - tall :]
                if side == 0:
                    first = pltpu.roll(first, HALF, 1)
                else:
                    second = pltpu.roll(second, HALF, 1)
                rows[side][...] = (first + second).astype(BF)

    acc1[...] = acc1_in[...]
    acc2[...] = acc2_in[...]
    for side in sides:
        hid = order(side, hs[side, 1, 1, :cols].T, hs_edge[side, 1, :cols].T)
        add_one(acc2, jnp.concatenate(hid, axis=0), [ds2[side, 1, s, :cols] for s in range(3)])
        own = f[near[side]].T
        for k in (1, 0):
            feat = order(side, halo[side][0, :cols].T, own) if k == 0 else order(side, own, f[next_near[side]].T)
            add_one(acc1, jnp.concatenate(feat, axis=0), [ds1[side][k, s, :cols] for s in range(3)])
    take_terms(acc1, acc2, term)


def with_row(center, row, side):
    turned = pltpu.roll(row, HALF, 1)
    first, second = (row, turned) if side == 0 else (turned, row)
    cols = center.shape[0] - row.shape[0]
    full = jnp.concatenate([first[:cols], second], axis=0)
    return jnp.where(half_lanes(side), full, center)


def last_body(ds1_top, ds1, ds1_bottom, prev_row, next_row, v1, gf, done, ends):
    pairs, cols = gf.shape[:2]
    done[...] = jnp.zeros_like(done)
    store_shifts(with_row(ds1_top[0, 1].astype(F32), prev_row[...].astype(F32), 0), ends, 0)
    store_shifts(with_row(ds1_bottom[0, 1].astype(F32), next_row[...].astype(F32), 1), ends, 1)
    places = [(ends, 0), (ds1_top, 1)] + [(ds1, j) for j in range(pairs - 3)] + [(ds1_bottom, 1), (ends, 1)]
    for j in range(pairs):
        gf[j] = band_dot(places[j], places[j + 1], v1)[:cols].astype(BF)


def cost(pair_count):
    return pl.CostEstimate(flops=pair_count * 272 * 768 * 128 * 2, bytes_accessed=4 * 2**20, transcendentals=0)


PARAMS = pltpu.CompilerParams(vmem_limit_bytes=32 * 2**20)


def inner(f, g, edge, w1, w2, v2):
    pairs, cols = f.shape[:2]
    wide = cols + RIM

    def shifts(count):
        return (count, 3, wide, LANES)

    return pl.pallas_call(
        inner_body,
        out_shape=(
            jax.ShapeDtypeStruct(shifts(2), BF),
            jax.ShapeDtypeStruct(shifts(2), BF),
            jax.ShapeDtypeStruct((2, wide, LANES), F32),
            jax.ShapeDtypeStruct(shifts(pairs - 3), BF),
            jax.ShapeDtypeStruct((2 * LANES, 3 * LANES), F32),
            jax.ShapeDtypeStruct((2 * LANES, 3 * LANES), F32),
        ),
        scratch_shapes=[
            pltpu.VMEM(shifts(pairs), BF),
            pltpu.VMEM(shifts(pairs - 1), BF),
            pltpu.VMEM(shifts(pairs - 2), BF),
            pltpu.VMEM((pairs - 1, wide, LANES), F32),
            pltpu.VMEM((pairs - 1, LANES, cols), BF),
            pltpu.VMEM((pairs - 1, LANES, cols), BF),
        ],
        compiler_params=PARAMS,
        cost_estimate=cost(22),
        name="inner",
    )(f, g, edge, w1, w2, v2)


def outer(f, *rest):
    wide = f.shape[1] + RIM

    def shifts(*count):
        return (*count, 3, wide, LANES)

    row = jax.ShapeDtypeStruct((wide // 2 + RIM // 2, LANES), BF)
    return pl.pallas_call(
        rim_body,
        out_shape=(
            jax.ShapeDtypeStruct(shifts(2), BF),
            jax.ShapeDtypeStruct(shifts(2), BF),
            row,
            row,
            jax.ShapeDtypeStruct((9 * HALF, LANES), F32),
        ),
        scratch_shapes=[
            pltpu.VMEM(shifts(2, 3), BF),
            pltpu.VMEM(shifts(2, 2), BF),
            pltpu.VMEM(shifts(2, 2), BF),
            pltpu.VMEM((2, wide, LANES), F32),
            pltpu.VMEM((2 * LANES, 3 * LANES), F32),
            pltpu.VMEM((2 * LANES, 3 * LANES), F32),
        ],
        compiler_params=PARAMS,
        cost_estimate=cost(14),
        name="outer",
    )(f, *rest)


def last(ds1_top, ds1, ds1_bottom, prev_row, next_row, v1, cols):
    pairs = ds1.shape[0] + 3
    return pl.pallas_call(
        last_body,
        out_shape=(
            jax.ShapeDtypeStruct((pairs, cols, LANES), BF),
            jax.ShapeDtypeStruct((8, LANES), F32),
        ),
        scratch_shapes=[pltpu.VMEM((2, 3, cols + RIM, LANES), BF)],
        compiler_params=PARAMS,
        cost_estimate=cost(8),
        name="last",
    )(ds1_top, ds1, ds1_bottom, prev_row, next_row, v1)


def four_body(own, one, two, three, done, out):
    low = [ref[...].astype(F32) for ref in (own, one, two, three)]
    out[...] = (low[0] + low[1]) + (low[2] + low[3])


def sum_four(own, got, done):
    return pl.pallas_call(
        four_body,
        out_shape=jax.ShapeDtypeStruct(own.shape, F32),
        compiler_params=pltpu.CompilerParams(vmem_limit_bytes=4 * 2**20),
        name="sum_four",
    )(own, *got, done)


def finish_body(part, other, one, two, *, scale):
    half = part.shape[0]
    first = lax.axis_index("dp") == 0
    for tap in range(9):
        rows = []
        for at in range(tap * HALF, (tap + 1) * HALF, HALF // 2):
            side, at = (0, at) if at < half else (1, at - half)
            mine, theirs = part[at : at + HALF // 2], other[at : at + HALF // 2]
            rows.append(jnp.where(first, mine, theirs) if side == 0 else jnp.where(first, theirs, mine))
        both = jnp.concatenate(rows, axis=0).T * scale
        one[tap // 3, tap % 3] = both[:HALF]
        two[tap // 3, tap % 3] = both[HALF:]


def finish(part, other, scale):
    shape = jax.ShapeDtypeStruct((3, 3, HALF, HALF), F32)
    return pl.pallas_call(
        functools.partial(finish_body, scale=scale),
        out_shape=(shape, shape),
        compiler_params=pltpu.CompilerParams(vmem_limit_bytes=4 * 2**20),
        name="finish",
    )(part, other)


def reduced(term, done):
    sizes = [lax.axis_size(axis) for axis in AXES]
    if sizes[0] != 2 or any(size & (size - 1) for size in sizes):
        total = lax.psum(term, AXES)
        half = term.shape[0] // 2
        both = total[:half], total[half:]
        core = lax.axis_index("dp") == 0
        return jnp.where(core, *both), jnp.where(core, both[1], both[0])
    half = term.shape[0] // 2
    me = lax.axis_index("dp")
    swap = [(0, 1), (1, 0)]
    mine = lax.dynamic_slice_in_dim(term, me * half, half, 0)
    other = lax.dynamic_slice_in_dim(term, (1 - me) * half, half, 0)
    part = mine + lax.ppermute(other, "dp", swap)
    across = [(0, 1 << b) for b in range(sizes[2].bit_length() - 1)]
    down = [(1 << b, 0) for b in range(sizes[1].bit_length() - 1)]
    bits = []
    while across or down:
        bits += down[:1] + across[:1]
        down, across = down[1:], across[1:]
    groups = [bits[at : at + 2] for at in range(0, len(bits), 2)]
    for at in range(len(groups)):
        mine = [groups[at], groups[(at + len(groups) // 2) % len(groups)]]
        if len(mine[0]) != len(mine[1]):
            mine[1] = mine[0]
        low = part.astype(BF)
        got = []
        for member in range(1, 1 << len(mine[0])):
            perm = []
            for core in range(2):
                flips = [flip for k, flip in enumerate(mine[core]) if member >> k & 1]
                for r in range(sizes[1]):
                    for c in range(sizes[2]):
                        to_r, to_c = r, c
                        for flip in flips:
                            to_r, to_c = to_r ^ flip[0], to_c ^ flip[1]
                        base = core * sizes[1]
                        perm.append(((base + r) * sizes[2] + c, (base + to_r) * sizes[2] + to_c))
            got.append(lax.ppermute(low, AXES, perm))
        if at == 1 and len(got) > 1:
            part = sum_four(low, got, done)
            continue
        got = [one.astype(F32) for one in got]
        part = low.astype(F32) + got[0]
        if len(got) > 1:
            part = part + (got[1] + got[2])
    return part, lax.ppermute(part, "dp", swap)


def shards(features, grad_out, kernel_one, kernel_two):
    slides, chans, rows, cols = features.shape
    pairs = rows // 2
    feat, grad = to_pairs(features), to_pairs(grad_out)
    own = jnp.concatenate([feat, grad], axis=0)
    from_left, from_right = swap_one(own[:, : RIM // 2], own[:, cols - RIM // 2 :], "col")
    edge = jnp.concatenate([from_right, from_left], axis=1)
    w1, w2, v2, v1 = make_weights(kernel_one, kernel_two)
    low = jnp.stack([feat[0], jnp.concatenate([feat[1, :, :HALF], grad[0, :, :HALF]], axis=1)])
    high = jnp.stack([feat[-1], jnp.concatenate([grad[-1, :, HALF:], feat[-2, :, HALF:]], axis=1)])
    feat_edge, grad_edge = edge[:pairs], edge[pairs:]
    low_edge = jnp.stack([feat_edge[0], jnp.concatenate([feat_edge[1, :, :HALF], grad_edge[0, :, :HALF]], axis=1)])
    high_edge = jnp.stack([feat_edge[-1], jnp.concatenate([grad_edge[-1, :, HALF:], feat_edge[-2, :, HALF:]], axis=1)])
    low, high = jnp.concatenate([low, low_edge], axis=1), jnp.concatenate([high, high_edge], axis=1)
    above, below = swap_one(low, high, "row")
    hs_edge, ds2_edge, slope_edge, ds1, acc1, acc2 = inner(feat, grad, edge, w1, w2, v2)
    ds1_top, ds1_bottom, low_row, high_row, term = outer(
        feat, grad, edge, above, below, w1, w2, v2, hs_edge, ds2_edge, slope_edge, acc1, acc2
    )
    prev_row, next_row = swap_one(low_row, high_row, "row")
    gf, done = last(ds1_top, ds1, ds1_bottom, prev_row, next_row, v1, cols)
    part, other = reduced(term, done)
    count = slides * lax.axis_size("dp") * rows * lax.axis_size("row") * cols * lax.axis_size("col")
    grad_one, grad_two = finish(part, other, float(count) ** -0.5)
    return from_pairs(gf), grad_one, grad_two


def solution(mesh):
    return jax.shard_map(
        shards,
        mesh=mesh,
        in_specs=(P("dp", None, "row", "col"), P("dp", None, "row", "col"), P(), P()),
        out_specs=(P("dp", None, "row", "col"), P(), P()),
        check_vma=False,
    )
```

```python
import functools

import jax
import jax.numpy as jnp
from jax import lax
from jax.experimental import pallas as pl
from jax.experimental.pallas import tpu as pltpu
from jax.sharding import PartitionSpec as P

BF = jnp.bfloat16
F32 = jnp.float32
AXES = ("dp", "row", "col")
LANES = 128
HALF = LANES // 2
RIM = 16


def neighbours(axis, parity):
    count = lax.axis_size(axis)
    pairs = []
    for i in range(parity, count - 1, 2):
        pairs += [(i, i + 1), (i + 1, i)]
    return pairs


def is_low(axis, parity):
    return lax.axis_index(axis) % 2 == parity


def swap_one(low, high, axis):
    got = []
    for parity in range(2):
        perm = neighbours(axis, parity)
        if perm:
            got.append(lax.ppermute(jnp.where(is_low(axis, parity), high, low), axis, perm))
        else:
            got.append(jnp.zeros_like(low))
    odd = is_low(axis, 1)
    return jnp.where(odd, got[0], got[1]), jnp.where(odd, got[1], got[0])


def to_pairs(cells):
    _, chans, rows, cols = cells.shape
    part = cells[0].reshape(chans, rows // 2, 2, cols)
    return part.transpose(1, 3, 2, 0).reshape(rows // 2, cols, 2 * chans)


def from_pairs(pairs):
    count, cols, lanes = pairs.shape
    part = pairs.reshape(count, cols, 2, lanes // 2)
    return part.transpose(3, 0, 2, 1).reshape(1, lanes // 2, 2 * count, cols)


def weights_body(k1, k2, w1, w2, v2, v1):
    zero = jnp.zeros((HALF, HALF), BF)
    for taps, forward, backward in ((k1, w1, v1), (k2, w2, v2)):
        flat = {(ky, kx): taps[ky, kx] for ky in range(3) for kx in range(3)}
        turned = {at: flat[at].astype(F32).T.astype(BF) for at in flat}
        for p in range(2):
            for kx in range(3):
                for r in range(2):
                    at = ((p * 3 + kx) * 2 + r) * HALF
                    kys = [2 * p + r - a for a in range(2)]
                    forward[at : at + HALF] = jnp.concatenate([turned.get((ky, kx), zero) for ky in kys], axis=1)
                    backward[at : at + HALF] = jnp.concatenate([flat.get((2 - ky, 2 - kx), zero) for ky in kys], axis=1)


def make_weights(kernel_one, kernel_two):
    shape = jax.ShapeDtypeStruct((12 * HALF, LANES), BF)
    return pl.pallas_call(
        weights_body,
        out_shape=(shape,) * 4,
        compiler_params=pltpu.CompilerParams(vmem_limit_bytes=8 * 2**20),
        cost_estimate=cost(2),
        name="weights",
    )(kernel_one, kernel_two)


def sigmoid(value):
    return 0.5 * jnp.tanh(0.5 * value) + 0.5


def with_rim(own, rim):
    return jnp.concatenate([own.astype(F32), rim.astype(F32)], axis=0)


def store_shifts(value, out, index):
    out[index, 0] = pltpu.roll(value, 1, 0).astype(BF)
    out[index, 1] = value.astype(BF)
    out[index, 2] = pltpu.roll(value, value.shape[0] - 1, 0).astype(BF)


def band_dot(first, second, weight):
    parts = [ref[index, s] for ref, index in (first, second) for s in range(3)]
    return jnp.dot(jnp.concatenate(parts, axis=1), weight[...], preferred_element_type=F32)


def edge_masks():
    row, col = lax.axis_index("row"), lax.axis_index("col")
    top = (row > 0).astype(F32)
    bottom = (row < lax.axis_size("row") - 1).astype(F32)
    left = (col > 0).astype(F32)
    right = (col < lax.axis_size("col") - 1).astype(F32)
    place = lax.broadcasted_iota(jnp.int32, (RIM, LANES), 0)
    rim = jnp.where(place < RIM // 2, right, left)
    return top, bottom, rim


def rim_masked(value, rim):
    own = value.shape[0] - RIM
    return jnp.concatenate([value[:own], value[own:] * rim], axis=0)


def add_one(acc, feat_t, pieces):
    near = jnp.concatenate(pieces, axis=1)
    acc[...] += jnp.dot(feat_t, near, preferred_element_type=F32)


def inner_body(f, g, edge, w1, w2, v2, hs_edge, ds2_edge, slope_edge, ds1, acc1, acc2, fs, hs, ds2, slope, ht, ft):
    pairs, cols = f.shape[:2]
    _, _, rim = edge_masks()

    @pl.loop(0, pairs, unroll=True)
    def _(j):
        store_shifts(with_rim(f[j], edge[j]), fs, j)

    @pl.loop(0, pairs - 1, unroll=True)
    def _(j):
        pre = band_dot((fs, j), (fs, j + 1), w1)
        sig = sigmoid(pre)
        act = pre * sig
        slope[j] = sig + act * (1.0 - sig)
        store_shifts(rim_masked(act, rim), hs, j)
        ht[j] = hs[j, 1, :cols].T

    @pl.loop(0, pairs - 2, unroll=True)
    def _(j):
        pre = band_dot((hs, j), (hs, j + 1), w2)
        sig = sigmoid(pre)
        grad = with_rim(g[j + 1], edge[pairs + j + 1])
        delta = grad * (sig + pre * sig * (1.0 - sig))
        store_shifts(delta, ds2, j)

    @pl.loop(0, pairs - 3, unroll=True)
    def _(j):
        back = band_dot((ds2, j), (ds2, j + 1), v2)
        store_shifts(rim_masked(back * slope[j + 1], rim), ds1, j)

    acc1[...] = jnp.zeros_like(acc1)
    acc2[...] = jnp.zeros_like(acc2)

    @pl.loop(0, pairs - 2, unroll=True)
    def _(j):
        both = jnp.concatenate([ht[j], ht[j + 1]], axis=0)
        add_one(acc2, both, [ds2[j, s, :cols] for s in range(3)])

    @pl.loop(1, pairs - 1, unroll=True)
    def _(j):
        ft[j] = f[j].T

    @pl.loop(0, pairs - 3, unroll=True)
    def _(j):
        both = jnp.concatenate([ft[j + 1], ft[j + 2]], axis=0)
        add_one(acc1, both, [ds1[j, s, :cols] for s in range(3)])

    for side, at in ((0, 0), (1, pairs - 2)):
        hs_edge[side] = hs[at]
        slope_edge[side] = slope[at]
    for side, at in ((0, 0), (1, pairs - 3)):
        ds2_edge[side] = ds2[at]


def take_terms(acc1, acc2, term):
    for ky in range(3):
        for kx in range(3):
            at = (2 - kx) * LANES
            sums = []
            for acc in (acc1, acc2):
                first = acc[ky * HALF : (ky + 1) * HALF, at : at + HALF]
                sums.append(first + acc[(ky + 1) * HALF : (ky + 2) * HALF, at + HALF : at + LANES])
            at = (ky * 3 + kx) * HALF
            term[at : at + HALF] = jnp.concatenate(sums, axis=1)


def half_lanes(side):
    upper = lax.broadcasted_iota(jnp.int32, (1, LANES), 1) >= HALF
    return upper == (side == 1)


def rim_body(
    f, g, edge, above, below, w1, w2, v2, hs_edge, ds2_edge, slope_edge, acc1_in, acc2_in,
    ds1_top, ds1_bottom, row_top, row_bottom, term, fs, hs, ds2, slope, acc1, acc2,
):
    pairs, cols = f.shape[:2]
    top, bottom, rim = edge_masks()
    flags = (top, bottom)
    beyond = [half_lanes(side) for side in range(2)]
    halo, ds1, rows = (above, below), (ds1_top, ds1_bottom), (row_top, row_bottom)
    near, next_near = (0, pairs - 1), (1, pairs - 2)
    mixed = [ref[1].astype(F32) for ref in halo]
    sides = range(2)

    def order(side, one, two):
        return (one, two) if side == 0 else (two, one)

    for side in sides:
        store_shifts(jnp.where(beyond[side], 0.0, mixed[side]), fs.at[side], 0)
        store_shifts(halo[side][0].astype(F32), fs.at[side], 1)
        store_shifts(with_rim(f[near[side]], edge[near[side]]), fs.at[side], 2)
    for k in (1, 0):
        for side in sides:
            pre = band_dot(*order(side, (fs.at[side], k), (fs.at[side], k + 1)), w1)
            sig = sigmoid(pre)
            act = pre * sig
            if k == 1:
                slope[side] = sig + act * (1.0 - sig)
            act = act * (flags[side] if k == 0 else jnp.where(beyond[side], flags[side], 1.0))
            store_shifts(rim_masked(act, rim), hs.at[side], k)
    for k in (1, 0):
        for side in sides:
            if k == 0:
                grad = jnp.where(beyond[side], 0.0, pltpu.roll(mixed[side], HALF, 1))
            else:
                grad = with_rim(g[near[side]], edge[pairs + near[side]])
            inward = (hs.at[side], 1) if k == 0 else (hs_edge, side)
            pre = band_dot(*order(side, (hs.at[side], k), inward), w2)
            sig = sigmoid(pre)
            delta = grad * (sig + pre * sig * (1.0 - sig))
            store_shifts(delta, ds2.at[side], k)
    for k in (1, 0):
        for side in sides:
            inward = (ds2.at[side], 1) if k == 0 else (ds2_edge, side)
            back = band_dot(*order(side, (ds2.at[side], k), inward), v2)
            value = back * slope[side] if k == 0 else back * slope_edge[side]
            if k == 0:
                value = jnp.where(beyond[side], 0.0, value)
            value = rim_masked(value, rim)
            store_shifts(value, ds1[side], k)
            if k == 0:
                tall = rows[side].shape[0]
                first, second = value[:tall], value[value.shape[0] - tall :]
                if side == 0:
                    first = pltpu.roll(first, HALF, 1)
                else:
                    second = pltpu.roll(second, HALF, 1)
                rows[side][...] = (first + second).astype(BF)

    acc1[...] = acc1_in[...]
    acc2[...] = acc2_in[...]
    for side in sides:
        hid = order(side, hs[side, 1, 1, :cols].T, hs_edge[side, 1, :cols].T)
        add_one(acc2, jnp.concatenate(hid, axis=0), [ds2[side, 1, s, :cols] for s in range(3)])
        own = f[near[side]].T
        for k in (1, 0):
            feat = order(side, halo[side][0, :cols].T, own) if k == 0 else order(side, own, f[next_near[side]].T)
            add_one(acc1, jnp.concatenate(feat, axis=0), [ds1[side][k, s, :cols] for s in range(3)])
    take_terms(acc1, acc2, term)


def with_row(center, row, side):
    turned = pltpu.roll(row, HALF, 1)
    first, second = (row, turned) if side == 0 else (turned, row)
    cols = center.shape[0] - row.shape[0]
    full = jnp.concatenate([first[:cols], second], axis=0)
    return jnp.where(half_lanes(side), full, center)


def last_body(ds1_top, ds1, ds1_bottom, prev_row, next_row, v1, gf, done, ends):
    pairs, cols = gf.shape[:2]
    done[...] = jnp.zeros_like(done)
    store_shifts(with_row(ds1_top[0, 1].astype(F32), prev_row[...].astype(F32), 0), ends, 0)
    store_shifts(with_row(ds1_bottom[0, 1].astype(F32), next_row[...].astype(F32), 1), ends, 1)
    places = [(ends, 0), (ds1_top, 1)] + [(ds1, j) for j in range(pairs - 3)] + [(ds1_bottom, 1), (ends, 1)]
    for j in range(pairs):
        gf[j] = band_dot(places[j], places[j + 1], v1)[:cols].astype(BF)


def cost(pair_count):
    return pl.CostEstimate(flops=pair_count * 272 * 768 * 128 * 2, bytes_accessed=4 * 2**20, transcendentals=0)


PARAMS = pltpu.CompilerParams(vmem_limit_bytes=32 * 2**20)


def inner(f, g, edge, w1, w2, v2):
    pairs, cols = f.shape[:2]
    wide = cols + RIM

    def shifts(count):
        return (count, 3, wide, LANES)

    return pl.pallas_call(
        inner_body,
        out_shape=(
            jax.ShapeDtypeStruct(shifts(2), BF),
            jax.ShapeDtypeStruct(shifts(2), BF),
            jax.ShapeDtypeStruct((2, wide, LANES), F32),
            jax.ShapeDtypeStruct(shifts(pairs - 3), BF),
            jax.ShapeDtypeStruct((2 * LANES, 3 * LANES), F32),
            jax.ShapeDtypeStruct((2 * LANES, 3 * LANES), F32),
        ),
        scratch_shapes=[
            pltpu.VMEM(shifts(pairs), BF),
            pltpu.VMEM(shifts(pairs - 1), BF),
            pltpu.VMEM(shifts(pairs - 2), BF),
            pltpu.VMEM((pairs - 1, wide, LANES), F32),
            pltpu.VMEM((pairs - 1, LANES, cols), BF),
            pltpu.VMEM((pairs - 1, LANES, cols), BF),
        ],
        compiler_params=PARAMS,
        cost_estimate=cost(22),
        name="inner",
    )(f, g, edge, w1, w2, v2)


def outer(f, *rest):
    wide = f.shape[1] + RIM

    def shifts(*count):
        return (*count, 3, wide, LANES)

    row = jax.ShapeDtypeStruct((wide // 2 + RIM // 2, LANES), BF)
    return pl.pallas_call(
        rim_body,
        out_shape=(
            jax.ShapeDtypeStruct(shifts(2), BF),
            jax.ShapeDtypeStruct(shifts(2), BF),
            row,
            row,
            jax.ShapeDtypeStruct((9 * HALF, LANES), F32),
        ),
        scratch_shapes=[
            pltpu.VMEM(shifts(2, 3), BF),
            pltpu.VMEM(shifts(2, 2), BF),
            pltpu.VMEM(shifts(2, 2), BF),
            pltpu.VMEM((2, wide, LANES), F32),
            pltpu.VMEM((2 * LANES, 3 * LANES), F32),
            pltpu.VMEM((2 * LANES, 3 * LANES), F32),
        ],
        compiler_params=PARAMS,
        cost_estimate=cost(14),
        name="outer",
    )(f, *rest)


def last(ds1_top, ds1, ds1_bottom, prev_row, next_row, v1, cols):
    pairs = ds1.shape[0] + 3
    return pl.pallas_call(
        last_body,
        out_shape=(
            jax.ShapeDtypeStruct((pairs, cols, LANES), BF),
            jax.ShapeDtypeStruct((8, LANES), F32),
        ),
        scratch_shapes=[pltpu.VMEM((2, 3, cols + RIM, LANES), BF)],
        compiler_params=PARAMS,
        cost_estimate=cost(8),
        name="last",
    )(ds1_top, ds1, ds1_bottom, prev_row, next_row, v1)


def four_body(own, one, two, three, done, out):
    low = [ref[...].astype(F32) for ref in (own, one, two, three)]
    out[...] = (low[0] + low[1]) + (low[2] + low[3])


def sum_four(own, got, done):
    return pl.pallas_call(
        four_body,
        out_shape=jax.ShapeDtypeStruct(own.shape, F32),
        compiler_params=pltpu.CompilerParams(vmem_limit_bytes=4 * 2**20),
        name="sum_four",
    )(own, *got, done)


def finish_body(part, other, one, two, *, scale):
    half = part.shape[0]
    first = lax.axis_index("dp") == 0
    for tap in range(9):
        rows = []
        for at in range(tap * HALF, (tap + 1) * HALF, HALF // 2):
            side, at = (0, at) if at < half else (1, at - half)
            mine, theirs = part[at : at + HALF // 2], other[at : at + HALF // 2]
            rows.append(jnp.where(first, mine, theirs) if side == 0 else jnp.where(first, theirs, mine))
        both = jnp.concatenate(rows, axis=0).T * scale
        one[tap // 3, tap % 3] = both[:HALF]
        two[tap // 3, tap % 3] = both[HALF:]


def finish(part, other, scale):
    shape = jax.ShapeDtypeStruct((3, 3, HALF, HALF), F32)
    return pl.pallas_call(
        functools.partial(finish_body, scale=scale),
        out_shape=(shape, shape),
        compiler_params=pltpu.CompilerParams(vmem_limit_bytes=4 * 2**20),
        name="finish",
    )(part, other)


def reduced(term, done):
    sizes = [lax.axis_size(axis) for axis in AXES]
    if sizes[0] != 2 or any(size & (size - 1) for size in sizes):
        total = lax.psum(term, AXES)
        half = term.shape[0] // 2
        both = total[:half], total[half:]
        core = lax.axis_index("dp") == 0
        return jnp.where(core, *both), jnp.where(core, both[1], both[0])
    half = term.shape[0] // 2
    me = lax.axis_index("dp")
    swap = [(0, 1), (1, 0)]
    mine = lax.dynamic_slice_in_dim(term, me * half, half, 0)
    other = lax.dynamic_slice_in_dim(term, (1 - me) * half, half, 0)
    part = mine + lax.ppermute(other, "dp", swap)
    across = [(0, 1 << b) for b in range(sizes[2].bit_length() - 1)]
    down = [(1 << b, 0) for b in range(sizes[1].bit_length() - 1)]
    bits = []
    while across or down:
        bits += down[:1] + across[:1]
        down, across = down[1:], across[1:]
    groups = [bits[at : at + 2] for at in range(0, len(bits), 2)]
    for at in range(len(groups)):
        mine = [groups[at], groups[(at + len(groups) // 2) % len(groups)]]
        if len(mine[0]) != len(mine[1]):
            mine[1] = mine[0]
        low = part.astype(BF)
        got = []
        for member in range(1, 1 << len(mine[0])):
            perm = []
            for core in range(2):
                flips = [flip for k, flip in enumerate(mine[core]) if member >> k & 1]
                for r in range(sizes[1]):
                    for c in range(sizes[2]):
                        to_r, to_c = r, c
                        for flip in flips:
                            to_r, to_c = to_r ^ flip[0], to_c ^ flip[1]
                        base = core * sizes[1]
                        perm.append(((base + r) * sizes[2] + c, (base + to_r) * sizes[2] + to_c))
            got.append(lax.ppermute(low, AXES, perm))
        if at == 1 and len(got) > 1:
            part = sum_four(low, got, done)
            continue
        got = [one.astype(F32) for one in got]
        part = low.astype(F32) + got[0]
        if len(got) > 1:
            part = part + (got[1] + got[2])
    return part, lax.ppermute(part, "dp", swap)


def shards(features, grad_out, kernel_one, kernel_two):
    slides, chans, rows, cols = features.shape
    pairs = rows // 2
    feat, grad = to_pairs(features), to_pairs(grad_out)
    own = jnp.concatenate([feat, grad], axis=0)
    from_left, from_right = swap_one(own[:, : RIM // 2], own[:, cols - RIM // 2 :], "col")
    edge = jnp.concatenate([from_right, from_left], axis=1)
    w1, w2, v2, v1 = make_weights(kernel_one, kernel_two)
    low = jnp.stack([feat[0], jnp.concatenate([feat[1, :, :HALF], grad[0, :, :HALF]], axis=1)])
    high = jnp.stack([feat[-1], jnp.concatenate([grad[-1, :, HALF:], feat[-2, :, HALF:]], axis=1)])
    feat_edge, grad_edge = edge[:pairs], edge[pairs:]
    low_edge = jnp.stack([feat_edge[0], jnp.concatenate([feat_edge[1, :, :HALF], grad_edge[0, :, :HALF]], axis=1)])
    high_edge = jnp.stack([feat_edge[-1], jnp.concatenate([grad_edge[-1, :, HALF:], feat_edge[-2, :, HALF:]], axis=1)])
    low, high = jnp.concatenate([low, low_edge], axis=1), jnp.concatenate([high, high_edge], axis=1)
    above, below = swap_one(low, high, "row")
    hs_edge, ds2_edge, slope_edge, ds1, acc1, acc2 = inner(feat, grad, edge, w1, w2, v2)
    ds1_top, ds1_bottom, low_row, high_row, term = outer(
        feat, grad, edge, above, below, w1, w2, v2, hs_edge, ds2_edge, slope_edge, acc1, acc2
    )
    prev_row, next_row = swap_one(low_row, high_row, "row")
    gf, done = last(ds1_top, ds1, ds1_bottom, prev_row, next_row, v1, cols)
    part, other = reduced(term, done)
    count = slides * lax.axis_size("dp") * rows * lax.axis_size("row") * cols * lax.axis_size("col")
    grad_one, grad_two = finish(part, other, float(count) ** -0.5)
    return from_pairs(gf), grad_one, grad_two


def solution(mesh):
    return jax.shard_map(
        shards,
        mesh=mesh,
        in_specs=(P("dp", None, "row", "col"), P("dp", None, "row", "col"), P(), P()),
        out_specs=(P("dp", None, "row", "col"), P(), P()),
        check_vma=False,
    )
```

```python
import functools

import jax
import jax.numpy as jnp
from jax import lax
from jax.experimental import pallas as pl
from jax.experimental.pallas import tpu as pltpu
from jax.sharding import PartitionSpec as P

BF = jnp.bfloat16
F32 = jnp.float32
AXES = ("dp", "row", "col")
LANES = 128
HALF = LANES // 2
RIM = 16


def neighbours(axis, parity):
    count = lax.axis_size(axis)
    pairs = []
    for i in range(parity, count - 1, 2):
        pairs += [(i, i + 1), (i + 1, i)]
    return pairs


def is_low(axis, parity):
    return lax.axis_index(axis) % 2 == parity


def swap(low, high, axis):
    got = []
    for parity in range(2):
        perm = neighbours(axis, parity)
        if perm:
            got.append(lax.ppermute(jnp.where(is_low(axis, parity), high, low), axis, perm))
        else:
            got.append(jnp.zeros_like(low))
    odd = is_low(axis, 1)
    return jnp.where(odd, got[0], got[1]), jnp.where(odd, got[1], got[0])


def odd_place(axis):
    return lax.rem(lax.axis_index(axis), 2) == 1


def to_pairs(cells):
    _, chans, rows, cols = cells.shape
    part = cells[0].reshape(chans, rows // 2, 2, cols)
    return part.transpose(1, 3, 2, 0).reshape(rows // 2, cols, 2 * chans)


def from_pairs(pairs):
    count, cols, lanes = pairs.shape
    part = pairs.reshape(count, cols, 2, lanes // 2)
    return part.transpose(3, 0, 2, 1).reshape(1, lanes // 2, 2 * count, cols)


def make_weights(k1, k2, w1, w2, v2, v1):
    zero = jnp.zeros((HALF, HALF), BF)
    for taps, forward, backward in ((k1, w1, v1), (k2, w2, v2)):
        flat = {(ky, kx): taps[ky, kx] for ky in range(3) for kx in range(3)}
        turned = {at: flat[at].astype(F32).T.astype(BF) for at in flat}
        for p in range(2):
            for kx in range(3):
                for r in range(2):
                    at = ((p * 3 + kx) * 2 + r) * HALF
                    kys = [2 * p + r - a for a in range(2)]
                    forward[at : at + HALF] = jnp.concatenate([turned.get((ky, kx), zero) for ky in kys], axis=1)
                    backward[at : at + HALF] = jnp.concatenate([flat.get((2 - ky, 2 - kx), zero) for ky in kys], axis=1)


def outer_units(feats, grads, high):
    pairs = feats.shape[0]
    near = jnp.where(high, pairs - 1, 0)
    then = feats[jnp.where(high, pairs - 2, 1)].astype(F32)
    grad = pltpu.roll(grads[near].astype(F32), HALF, 1)
    lane = lax.broadcasted_iota(jnp.int32, then.shape, 1)
    own = (lane >= HALF).astype(jnp.int32) == jnp.where(high, 1, 0)
    return feats[near], jnp.where(own, then, grad).astype(BF), jnp.where(own, grad, then).astype(BF)


def prep_body(f, g, k1, k2, weights, sent_near, sent_far):
    make_weights(k1, k2, *(weights.at[at] for at in range(4)))
    odd = odd_place("row")
    for sent, high in ((sent_near, jnp.logical_not(odd)), (sent_far, odd)):
        units = outer_units(f, g, high)
        for at in range(sent.shape[0]):
            sent[at] = units[at]


def prep(feat, grad, kernel_one, kernel_two):
    shape = jax.ShapeDtypeStruct((4, 12 * HALF, LANES), BF)
    sent = [jax.ShapeDtypeStruct((units, *feat.shape[1:]), BF) for units in (3, 2)]
    return pl.pallas_call(
        prep_body,
        out_shape=(shape, *sent),
        compiler_params=pltpu.CompilerParams(vmem_limit_bytes=12 * 2**20),
        cost_estimate=cost(2),
        name="prep",
    )(feat, grad, kernel_one, kernel_two)


def frame_body(own_near, own_far, edge, sent_near, sent_far):
    pairs, cols = edge.shape[0] // 2, own_near.shape[1]
    odd = odd_place("row")
    feats, grads = edge.at[:pairs], edge.at[pairs:]
    for own, sent, high in ((own_near, sent_near, jnp.logical_not(odd)), (own_far, sent_far, odd)):
        units = outer_units(feats, grads, high)
        for at in range(sent.shape[0]):
            sent[at, :cols] = own[at]
            sent[at, cols:] = units[at]


def frame(own_near, own_far, edge):
    wide = own_near.shape[1] + RIM
    return pl.pallas_call(
        frame_body,
        out_shape=[jax.ShapeDtypeStruct((own.shape[0], wide, LANES), BF) for own in (own_near, own_far)],
        compiler_params=pltpu.CompilerParams(vmem_limit_bytes=8 * 2**20),
        name="frame",
    )(own_near, own_far, edge)


def sigmoid(value):
    return 0.5 * jnp.tanh(0.5 * value) + 0.5


def with_rim(own, rim):
    return jnp.concatenate([own.astype(F32), rim.astype(F32)], axis=0)


def store_shifts(value, out, index):
    out[index, 0] = pltpu.roll(value, 1, 0).astype(BF)
    out[index, 1] = value.astype(BF)
    out[index, 2] = pltpu.roll(value, value.shape[0] - 1, 0).astype(BF)


def band_dot(first, second, weight):
    parts = [ref[index, s] for ref, index in (first, second) for s in range(3)]
    return jnp.dot(jnp.concatenate(parts, axis=1), weight[...], preferred_element_type=F32)


def edge_masks():
    row, col = lax.axis_index("row"), lax.axis_index("col")
    top = (row > 0).astype(F32)
    bottom = (row < lax.axis_size("row") - 1).astype(F32)
    left = (col > 0).astype(F32)
    right = (col < lax.axis_size("col") - 1).astype(F32)
    place = lax.broadcasted_iota(jnp.int32, (RIM, LANES), 0)
    rim = jnp.where(place < RIM // 2, right, left)
    return top, bottom, rim


def rim_masked(value, rim):
    own = value.shape[0] - RIM
    return jnp.concatenate([value[:own], value[own:] * rim], axis=0)


def add_one(acc, feat_t, pieces):
    near = jnp.concatenate(pieces, axis=1)
    acc[...] += jnp.dot(feat_t, near, preferred_element_type=F32)


def inner_body(f, g, edge, weights, hs_edge, ds2_edge, slope_edge, ds1, acc1, acc2, fs, hs, ds2, slope, ht, ft):
    w1, w2, v2 = (weights.at[at] for at in range(3))
    pairs, cols = f.shape[:2]
    _, _, rim = edge_masks()

    @pl.loop(0, pairs, unroll=True)
    def _(j):
        store_shifts(with_rim(f[j], edge[j]), fs, j)

    @pl.loop(0, pairs - 1, unroll=True)
    def _(j):
        pre = band_dot((fs, j), (fs, j + 1), w1)
        sig = sigmoid(pre)
        act = pre * sig
        slope[j] = sig + act * (1.0 - sig)
        store_shifts(rim_masked(act, rim), hs, j)
        ht[j] = hs[j, 1, :cols].T

    @pl.loop(0, pairs - 2, unroll=True)
    def _(j):
        pre = band_dot((hs, j), (hs, j + 1), w2)
        sig = sigmoid(pre)
        grad = with_rim(g[j + 1], edge[pairs + j + 1])
        delta = grad * (sig + pre * sig * (1.0 - sig))
        store_shifts(delta, ds2, j)

    @pl.loop(0, pairs - 3, unroll=True)
    def _(j):
        back = band_dot((ds2, j), (ds2, j + 1), v2)
        store_shifts(rim_masked(back * slope[j + 1], rim), ds1, j)

    acc1[...] = jnp.zeros_like(acc1)
    acc2[...] = jnp.zeros_like(acc2)

    @pl.loop(0, pairs - 2, unroll=True)
    def _(j):
        both = jnp.concatenate([ht[j], ht[j + 1]], axis=0)
        add_one(acc2, both, [ds2[j, s, :cols] for s in range(3)])

    @pl.loop(1, pairs - 1, unroll=True)
    def _(j):
        ft[j] = f[j].T

    @pl.loop(0, pairs - 3, unroll=True)
    def _(j):
        both = jnp.concatenate([ft[j + 1], ft[j + 2]], axis=0)
        add_one(acc1, both, [ds1[j, s, :cols] for s in range(3)])

    for side, at in ((0, 0), (1, pairs - 2)):
        hs_edge[side] = hs[at]
        slope_edge[side] = slope[at]
    for side, at in ((0, 0), (1, pairs - 3)):
        ds2_edge[side] = ds2[at]


def take_terms(acc1, acc2, mine, other):
    blocks = []
    for ky in range(3):
        for kx in range(3):
            at = (2 - kx) * LANES
            sums = []
            for acc in (acc1, acc2):
                first = acc[ky * HALF : (ky + 1) * HALF, at : at + HALF]
                sums.append(first + acc[(ky + 1) * HALF : (ky + 2) * HALF, at + HALF : at + LANES])
            blocks.append(jnp.concatenate(sums, axis=1))
    half = HALF // 2
    second = lax.axis_index("dp") == 1
    for tap in range(9):
        one, two = blocks[tap][:half], blocks[tap][half:]
        mine[tap * half : (tap + 1) * half] = jnp.where(second, two, one)
        other[tap * half : (tap + 1) * half] = jnp.where(second, one, two)


def half_lanes(side):
    upper = lax.broadcasted_iota(jnp.int32, (1, LANES), 1) >= HALF
    return upper == (side == 1)


def rim_body(
    f, g, edge, above, below, weights, hs_edge, ds2_edge, slope_edge, acc1_in, acc2_in,
    ds1_next, end, row, mine, other, fs, hs, ds2, slope, ds1, acc1, acc2,
):
    pairs, cols = f.shape[:2]
    top, bottom, rim = edge_masks()
    flags = (top, bottom)
    beyond = [half_lanes(side) for side in range(2)]
    w1, w2, v2 = (weights.at[at] for at in range(3))
    rows = []
    odd = odd_place("row")
    known = jnp.where(odd, top, 0.0), jnp.where(odd, 0.0, bottom)
    halo, mixed, more = ([ref[at].astype(F32) for ref in (above, below)] for at in range(3))
    near, next_near = (0, pairs - 1), (1, pairs - 2)
    sides = range(2)

    def order(side, one, two):
        return (one, two) if side == 0 else (two, one)

    for side in sides:
        store_shifts(jnp.where(beyond[side], more[side], mixed[side]), fs.at[side], 0)
        store_shifts(halo[side], fs.at[side], 1)
        store_shifts(with_rim(f[near[side]], edge[near[side]]), fs.at[side], 2)
    for k in (1, 0):
        for side in sides:
            pre = band_dot(*order(side, (fs.at[side], k), (fs.at[side], k + 1)), w1)
            sig = sigmoid(pre)
            act = pre * sig
            if k == 1:
                slope[side] = sig + act * (1.0 - sig)
            act = act * (flags[side] if k == 0 else jnp.where(beyond[side], flags[side], 1.0))
            store_shifts(rim_masked(act, rim), hs.at[side], k)
    for k in (1, 0):
        for side in sides:
            if k == 0:
                grad = pltpu.roll(jnp.where(beyond[side], mixed[side], more[side]), HALF, 1)
            else:
                grad = with_rim(g[near[side]], edge[pairs + near[side]])
            inward = (hs.at[side], 1) if k == 0 else (hs_edge, side)
            pre = band_dot(*order(side, (hs.at[side], k), inward), w2)
            sig = sigmoid(pre)
            delta = grad * (sig + pre * sig * (1.0 - sig))
            store_shifts(delta, ds2.at[side], k)
    for k in (1, 0):
        for side in sides:
            inward = (ds2.at[side], 1) if k == 0 else (ds2_edge, side)
            back = band_dot(*order(side, (ds2.at[side], k), inward), v2)
            value = back * slope[side] if k == 0 else back * slope_edge[side]
            value = rim_masked(value, rim)
            if k == 0:
                end[side] = jnp.where(beyond[side], value * known[side], value).astype(BF)
                value = jnp.where(beyond[side], 0.0, value)
            store_shifts(value, ds1.at[side], k)
            if k == 1:
                for s in range(3):
                    ds1_next[side, s] = ds1[side, 1, s]
            if k == 0:
                tall = row.shape[0]
                first, second = value[:tall], value[value.shape[0] - tall :]
                if side == 0:
                    first = pltpu.roll(first, HALF, 1)
                else:
                    second = pltpu.roll(second, HALF, 1)
                rows.append(first + second)
    row[...] = jnp.where(odd, rows[1], rows[0]).astype(BF)

    acc1[...] = acc1_in[...]
    acc2[...] = acc2_in[...]
    for side in sides:
        hid = order(side, hs[side, 1, 1, :cols].T, hs_edge[side, 1, :cols].T)
        add_one(acc2, jnp.concatenate(hid, axis=0), [ds2[side, 1, s, :cols] for s in range(3)])
        own = f[near[side]].T
        for k in (1, 0):
            feat = order(side, fs[side, 1, 1, :cols].T, own) if k == 0 else order(side, own, f[next_near[side]].T)
            add_one(acc1, jnp.concatenate(feat, axis=0), [ds1[side, k, s, :cols] for s in range(3)])
    take_terms(acc1, acc2, mine, other)


def with_row(center, row, side):
    turned = pltpu.roll(row, HALF, 1)
    first, second = (row, turned) if side == 0 else (turned, row)
    cols = center.shape[0] - row.shape[0]
    full = jnp.concatenate([first[:cols], second], axis=0)
    return center + jnp.where(half_lanes(side), full, 0.0)


def last_body(end, ds1_next, ds1, row, weights, gf, done, ends):
    pairs, cols = gf.shape[:2]
    done[...] = jnp.zeros_like(done)
    odd = odd_place("row")
    from_prev = jnp.where(odd, 0.0, row[...].astype(F32))
    from_next = jnp.where(odd, row[...].astype(F32), 0.0)
    store_shifts(with_row(end[0].astype(F32), from_prev, 0), ends, 0)
    store_shifts(with_row(end[1].astype(F32), from_next, 1), ends, 1)
    places = [(ends, 0), (ds1_next, 0)] + [(ds1, j) for j in range(pairs - 3)] + [(ds1_next, 1), (ends, 1)]
    for j in range(pairs):
        gf[j] = band_dot(places[j], places[j + 1], weights.at[3])[:cols].astype(BF)


def cost(pair_count):
    return pl.CostEstimate(flops=pair_count * 272 * 768 * 128 * 2, bytes_accessed=4 * 2**20, transcendentals=0)


PARAMS = pltpu.CompilerParams(vmem_limit_bytes=32 * 2**20)


def inner(f, g, edge, weights):
    pairs, cols = f.shape[:2]
    wide = cols + RIM

    def shifts(count):
        return (count, 3, wide, LANES)

    return pl.pallas_call(
        inner_body,
        out_shape=(
            jax.ShapeDtypeStruct(shifts(2), BF),
            jax.ShapeDtypeStruct(shifts(2), BF),
            jax.ShapeDtypeStruct((2, wide, LANES), F32),
            jax.ShapeDtypeStruct(shifts(pairs - 3), BF),
            jax.ShapeDtypeStruct((2 * LANES, 3 * LANES), F32),
            jax.ShapeDtypeStruct((2 * LANES, 3 * LANES), F32),
        ),
        scratch_shapes=[
            pltpu.VMEM(shifts(pairs), BF),
            pltpu.VMEM(shifts(pairs - 1), BF),
            pltpu.VMEM(shifts(pairs - 2), BF),
            pltpu.VMEM((pairs - 1, wide, LANES), F32),
            pltpu.VMEM((pairs - 1, LANES, cols), BF),
            pltpu.VMEM((pairs - 1, LANES, cols), BF),
        ],
        compiler_params=PARAMS,
        cost_estimate=cost(22),
        name="inner",
    )(f, g, edge, weights)


def outer(f, *rest):
    wide = f.shape[1] + RIM

    def shifts(*count):
        return (*count, 3, wide, LANES)

    row = jax.ShapeDtypeStruct((wide // 2 + RIM // 2, LANES), BF)
    return pl.pallas_call(
        rim_body,
        out_shape=(
            jax.ShapeDtypeStruct(shifts(2), BF),
            jax.ShapeDtypeStruct((2, wide, LANES), BF),
            row,
            jax.ShapeDtypeStruct((9 * HALF // 2, LANES), F32),
            jax.ShapeDtypeStruct((9 * HALF // 2, LANES), F32),
        ),
        scratch_shapes=[
            pltpu.VMEM(shifts(2, 3), BF),
            pltpu.VMEM(shifts(2, 2), BF),
            pltpu.VMEM(shifts(2, 2), BF),
            pltpu.VMEM((2, wide, LANES), F32),
            pltpu.VMEM(shifts(2, 2), BF),
            pltpu.VMEM((2 * LANES, 3 * LANES), F32),
            pltpu.VMEM((2 * LANES, 3 * LANES), F32),
        ],
        compiler_params=PARAMS,
        cost_estimate=cost(14),
        name="outer",
    )(f, *rest)


def last(end, ds1_next, ds1, row, weights, cols):
    pairs = ds1.shape[0] + 3
    return pl.pallas_call(
        last_body,
        out_shape=(
            jax.ShapeDtypeStruct((pairs, cols, LANES), BF),
            jax.ShapeDtypeStruct((8, LANES), F32),
        ),
        scratch_shapes=[pltpu.VMEM((2, 3, cols + RIM, LANES), BF)],
        compiler_params=PARAMS,
        cost_estimate=cost(8),
        name="last",
    )(end, ds1_next, ds1, row, weights)


def four_body(own, one, two, three, done, out):
    low = [ref[...].astype(F32) for ref in (own, one, two, three)]
    out[...] = (low[0] + low[1]) + (low[2] + low[3])


def sum_four(own, got, done):
    return pl.pallas_call(
        four_body,
        out_shape=jax.ShapeDtypeStruct(own.shape, F32),
        compiler_params=pltpu.CompilerParams(vmem_limit_bytes=4 * 2**20),
        name="sum_four",
    )(own, *got, done)


def finish_body(part, other, one, two, *, scale):
    half = HALF // 2
    second = lax.axis_index("dp") == 1
    for tap in range(9):
        mine, theirs = (ref[tap * half : (tap + 1) * half] for ref in (part, other))
        rows = [jnp.where(second, theirs, mine), jnp.where(second, mine, theirs)]
        both = jnp.concatenate(rows, axis=0).T * scale
        one[tap // 3, tap % 3] = both[:HALF]
        two[tap // 3, tap % 3] = both[HALF:]


def finish(part, other, scale):
    shape = jax.ShapeDtypeStruct((3, 3, HALF, HALF), F32)
    return pl.pallas_call(
        functools.partial(finish_body, scale=scale),
        out_shape=(shape, shape),
        compiler_params=pltpu.CompilerParams(vmem_limit_bytes=4 * 2**20),
        name="finish",
    )(part, other)


def reduced(mine, other, done):
    sizes = [lax.axis_size(axis) for axis in AXES]
    swap_cores = [(0, 1), (1, 0)]
    if sizes[0] != 2 or any(size & (size - 1) for size in sizes):
        first = lax.axis_index("dp") == 0
        both = lax.psum([jnp.where(first, mine, other), jnp.where(first, other, mine)], AXES)
        return jnp.where(first, *both), jnp.where(first, both[1], both[0])
    part = mine + lax.ppermute(other, "dp", swap_cores)
    across = [(0, 1 << b) for b in range(sizes[2].bit_length() - 1)]
    down = [(1 << b, 0) for b in range(sizes[1].bit_length() - 1)]
    bits = []
    while across or down:
        bits += down[:1] + across[:1]
        down, across = down[1:], across[1:]
    groups = [bits[at : at + 2] for at in range(0, len(bits), 2)]
    for at in range(len(groups)):
        mine = [groups[at], groups[(at + len(groups) // 2) % len(groups)]]
        if len(mine[0]) != len(mine[1]):
            mine[1] = mine[0]
        low = part.astype(BF)
        got = []
        for member in range(1, 1 << len(mine[0])):
            perm = []
            for core in range(2):
                flips = [flip for k, flip in enumerate(mine[core]) if member >> k & 1]
                for r in range(sizes[1]):
                    for c in range(sizes[2]):
                        to_r, to_c = r, c
                        for flip in flips:
                            to_r, to_c = to_r ^ flip[0], to_c ^ flip[1]
                        base = core * sizes[1]
                        perm.append(((base + r) * sizes[2] + c, (base + to_r) * sizes[2] + to_c))
            got.append(lax.ppermute(low, AXES, perm))
        if at == 1 and len(got) > 1:
            part = sum_four(low, got, done)
            continue
        got = [one.astype(F32) for one in got]
        part = low.astype(F32) + got[0]
        if len(got) > 1:
            part = part + (got[1] + got[2])
    return part, lax.ppermute(part, "dp", swap_cores)


def shards(features, grad_out, kernel_one, kernel_two):
    slides, chans, rows, cols = features.shape
    pairs = rows // 2
    feat, grad = to_pairs(features), to_pairs(grad_out)
    own = jnp.concatenate([feat, grad], axis=0)
    from_left, from_right = swap(own[:, : RIM // 2], own[:, cols - RIM // 2 :], "col")
    edge = jnp.concatenate([from_right, from_left], axis=1)
    weights, own_near, own_far = prep(feat, grad, kernel_one, kernel_two)
    sent_near, sent_far = frame(own_near, own_far, edge)
    got_near = lax.ppermute(sent_near, "row", neighbours("row", 0))
    got_far = lax.ppermute(sent_far, "row", neighbours("row", 1))
    odd = is_low("row", 1)
    one, more = got_near[:2], got_near[2:]
    above = jnp.concatenate([jnp.where(odd, one, got_far), jnp.where(odd, more, jnp.zeros_like(more))])
    below = jnp.concatenate([jnp.where(odd, got_far, one), jnp.where(odd, jnp.zeros_like(more), more)])
    hs_edge, ds2_edge, slope_edge, ds1, acc1, acc2 = inner(feat, grad, edge, weights)
    ds1_next, end, row, mine, other = outer(
        feat, grad, edge, above, below, weights, hs_edge, ds2_edge, slope_edge, acc1, acc2
    )
    row = lax.ppermute(row, "row", neighbours("row", 1))
    gf, done = last(end, ds1_next, ds1, row, weights, cols)
    part, other = reduced(mine, other, done)
    count = slides * lax.axis_size("dp") * rows * lax.axis_size("row") * cols * lax.axis_size("col")
    grad_one, grad_two = finish(part, other, float(count) ** -0.5)
    return from_pairs(gf), grad_one, grad_two


def solution(mesh):
    return jax.shard_map(
        shards,
        mesh=mesh,
        in_specs=(P("dp", None, "row", "col"), P("dp", None, "row", "col"), P(), P()),
        out_specs=(P("dp", None, "row", "col"), P(), P()),
        check_vma=False,
    )
```

```python
import functools

import jax
import jax.numpy as jnp
from jax import lax
from jax.experimental import pallas as pl
from jax.experimental.pallas import tpu as pltpu
from jax.sharding import PartitionSpec as P

BF = jnp.bfloat16
F32 = jnp.float32
AXES = ("dp", "row", "col")
LANES = 128
HALF = LANES // 2
RIM = 16


def neighbours(axis, parity):
    count = lax.axis_size(axis)
    pairs = []
    for i in range(parity, count - 1, 2):
        pairs += [(i, i + 1), (i + 1, i)]
    return pairs


def is_low(axis, parity):
    return lax.axis_index(axis) % 2 == parity


def swap(low, high, axis, turn):
    got = []
    for parity in range(2):
        perm = neighbours(axis, parity)
        if perm:
            got.append(lax.ppermute(turn(low, high, is_low(axis, parity)), axis, perm))
        else:
            got.append(jnp.zeros_like(got[0]))
    odd = is_low(axis, 1)
    return jnp.where(odd, got[0], got[1]), jnp.where(odd, got[1], got[0])


def odd_place(axis):
    return lax.rem(lax.axis_index(axis), 2) == 1


def to_pairs(cells):
    _, chans, rows, cols = cells.shape
    part = cells[0].reshape(chans, rows // 2, 2, cols)
    return part.transpose(1, 3, 2, 0).reshape(rows // 2, cols, 2 * chans)


def edges_body(*refs):
    out = refs[-1]
    at = 0
    for cells in refs[:-1]:
        turned = jnp.swapaxes(cells[0], 0, 1)
        for pair in range(turned.shape[0] // 2):
            out[at] = turned[2 * pair : 2 * pair + 2].reshape(2 * turned.shape[1], -1).T
            at += 1


def turn_edges(*parts):
    pairs = sum(part.shape[2] // 2 for part in parts)
    return pl.pallas_call(
        edges_body,
        out_shape=jax.ShapeDtypeStruct((pairs, parts[0].shape[3], LANES), BF),
        compiler_params=pltpu.CompilerParams(vmem_limit_bytes=8 * 2**20),
        name="edges",
    )(*parts)


def from_pairs(pairs):
    count, cols, lanes = pairs.shape
    part = pairs.reshape(count, cols, 2, lanes // 2)
    return part.transpose(3, 0, 2, 1).reshape(1, lanes // 2, 2 * count, cols)


def make_weights(k1, k2, w1, w2, v2, v1):
    zero = jnp.zeros((HALF, HALF), BF)
    for taps, forward, backward in ((k1, w1, v1), (k2, w2, v2)):
        flat = {(ky, kx): taps[ky, kx] for ky in range(3) for kx in range(3)}
        turned = {at: flat[at].astype(F32).T.astype(BF) for at in flat}
        for p in range(2):
            for kx in range(3):
                for r in range(2):
                    at = ((p * 3 + kx) * 2 + r) * HALF
                    kys = [2 * p + r - a for a in range(2)]
                    forward[at : at + HALF] = jnp.concatenate([turned.get((ky, kx), zero) for ky in kys], axis=1)
                    backward[at : at + HALF] = jnp.concatenate([flat.get((2 - ky, 2 - kx), zero) for ky in kys], axis=1)


def outer_units(feats, grads, high):
    pairs = feats.shape[0]
    near = jnp.where(high, pairs - 1, 0)
    then = feats[jnp.where(high, pairs - 2, 1)].astype(F32)
    grad = pltpu.roll(grads[near].astype(F32), HALF, 1)
    lane = lax.broadcasted_iota(jnp.int32, then.shape, 1)
    own = (lane >= HALF).astype(jnp.int32) == jnp.where(high, 1, 0)
    return feats[near], jnp.where(own, then, grad).astype(BF), jnp.where(own, grad, then).astype(BF)


def prep_body(f, g, k1, k2, weights, sent_near, sent_far):
    make_weights(k1, k2, *(weights.at[at] for at in range(4)))
    odd = odd_place("row")
    for sent, high in ((sent_near, jnp.logical_not(odd)), (sent_far, odd)):
        units = outer_units(f, g, high)
        for at in range(sent.shape[0]):
            sent[at] = units[at]


def prep(feat, grad, kernel_one, kernel_two):
    shape = jax.ShapeDtypeStruct((4, 12 * HALF, LANES), BF)
    sent = [jax.ShapeDtypeStruct((units, *feat.shape[1:]), BF) for units in (3, 2)]
    return pl.pallas_call(
        prep_body,
        out_shape=(shape, *sent),
        compiler_params=pltpu.CompilerParams(vmem_limit_bytes=12 * 2**20),
        cost_estimate=cost(2),
        name="prep",
    )(feat, grad, kernel_one, kernel_two)


def frame_body(own_near, own_far, edge, sent_near, sent_far):
    pairs, cols = edge.shape[0] // 2, own_near.shape[1]
    odd = odd_place("row")
    feats, grads = edge.at[:pairs], edge.at[pairs:]
    for own, sent, high in ((own_near, sent_near, jnp.logical_not(odd)), (own_far, sent_far, odd)):
        units = outer_units(feats, grads, high)
        for at in range(sent.shape[0]):
            sent[at, :cols] = own[at]
            sent[at, cols:] = units[at]


def frame(own_near, own_far, edge):
    wide = own_near.shape[1] + RIM
    return pl.pallas_call(
        frame_body,
        out_shape=[jax.ShapeDtypeStruct((own.shape[0], wide, LANES), BF) for own in (own_near, own_far)],
        compiler_params=pltpu.CompilerParams(vmem_limit_bytes=8 * 2**20),
        name="frame",
    )(own_near, own_far, edge)


def sigmoid(value):
    return 0.5 * jnp.tanh(0.5 * value) + 0.5


def with_rim(own, rim):
    return jnp.concatenate([own.astype(F32), rim.astype(F32)], axis=0)


def store_shifts(value, out, index):
    out[index, 0] = pltpu.roll(value, 1, 0).astype(BF)
    out[index, 1] = value.astype(BF)
    out[index, 2] = pltpu.roll(value, value.shape[0] - 1, 0).astype(BF)


def band_dot(first, second, weight):
    parts = [ref[index, s] for ref, index in (first, second) for s in range(3)]
    return jnp.dot(jnp.concatenate(parts, axis=1), weight[...], preferred_element_type=F32)


def edge_masks():
    row, col = lax.axis_index("row"), lax.axis_index("col")
    top = (row > 0).astype(F32)
    bottom = (row < lax.axis_size("row") - 1).astype(F32)
    left = (col > 0).astype(F32)
    right = (col < lax.axis_size("col") - 1).astype(F32)
    place = lax.broadcasted_iota(jnp.int32, (RIM, LANES), 0)
    rim = jnp.where(place < RIM // 2, right, left)
    return top, bottom, rim


def rim_masked(value, rim):
    own = value.shape[0] - RIM
    return jnp.concatenate([value[:own], value[own:] * rim], axis=0)


def add_one(acc, feat_t, pieces):
    near = jnp.concatenate(pieces, axis=1)
    acc[...] += jnp.dot(feat_t, near, preferred_element_type=F32)


def inner_body(f, g, edge, weights, hs_edge, ds2_edge, slope_edge, ds1, acc1, acc2, fs, hs, ds2, slope, ht, ft):
    w1, w2, v2 = (weights.at[at] for at in range(3))
    pairs, cols = f.shape[:2]
    _, _, rim = edge_masks()

    @pl.loop(0, pairs, unroll=True)
    def _(j):
        store_shifts(with_rim(f[j], edge[j]), fs, j)

    @pl.loop(0, pairs - 1, unroll=True)
    def _(j):
        pre = band_dot((fs, j), (fs, j + 1), w1)
        sig = sigmoid(pre)
        act = pre * sig
        slope[j] = sig + act * (1.0 - sig)
        store_shifts(rim_masked(act, rim), hs, j)
        ht[j] = hs[j, 1, :cols].T

    @pl.loop(0, pairs - 2, unroll=True)
    def _(j):
        pre = band_dot((hs, j), (hs, j + 1), w2)
        sig = sigmoid(pre)
        grad = with_rim(g[j + 1], edge[pairs + j + 1])
        delta = grad * (sig + pre * sig * (1.0 - sig))
        store_shifts(delta, ds2, j)

    @pl.loop(0, pairs - 3, unroll=True)
    def _(j):
        back = band_dot((ds2, j), (ds2, j + 1), v2)
        store_shifts(rim_masked(back * slope[j + 1], rim), ds1, j)

    acc1[...] = jnp.zeros_like(acc1)
    acc2[...] = jnp.zeros_like(acc2)

    @pl.loop(0, pairs - 2, unroll=True)
    def _(j):
        both = jnp.concatenate([ht[j], ht[j + 1]], axis=0)
        add_one(acc2, both, [ds2[j, s, :cols] for s in range(3)])

    @pl.loop(1, pairs - 1, unroll=True)
    def _(j):
        ft[j] = f[j].T

    @pl.loop(0, pairs - 3, unroll=True)
    def _(j):
        both = jnp.concatenate([ft[j + 1], ft[j + 2]], axis=0)
        add_one(acc1, both, [ds1[j, s, :cols] for s in range(3)])

    for side, at in ((0, 0), (1, pairs - 2)):
        hs_edge[side] = hs[at]
        slope_edge[side] = slope[at]
    for side, at in ((0, 0), (1, pairs - 3)):
        ds2_edge[side] = ds2[at]


def take_terms(acc1, acc2, mine, other):
    blocks = []
    for ky in range(3):
        for kx in range(3):
            at = (2 - kx) * LANES
            sums = []
            for acc in (acc1, acc2):
                first = acc[ky * HALF : (ky + 1) * HALF, at : at + HALF]
                sums.append(first + acc[(ky + 1) * HALF : (ky + 2) * HALF, at + HALF : at + LANES])
            blocks.append(jnp.concatenate(sums, axis=1))
    half = HALF // 2
    second = lax.axis_index("dp") == 1
    for tap in range(9):
        one, two = blocks[tap][:half], blocks[tap][half:]
        mine[tap * half : (tap + 1) * half] = jnp.where(second, two, one)
        other[tap * half : (tap + 1) * half] = jnp.where(second, one, two)


def half_lanes(side):
    upper = lax.broadcasted_iota(jnp.int32, (1, LANES), 1) >= HALF
    return upper == (side == 1)


def rim_body(
    f, g, edge, above, below, weights, hs_edge, ds2_edge, slope_edge, acc1_in, acc2_in,
    ds1_next, end, row, mine, other, fs, hs, ds2, slope, ds1, acc1, acc2,
):
    pairs, cols = f.shape[:2]
    top, bottom, rim = edge_masks()
    flags = (top, bottom)
    beyond = [half_lanes(side) for side in range(2)]
    w1, w2, v2 = (weights.at[at] for at in range(3))
    rows = []
    odd = odd_place("row")
    known = jnp.where(odd, top, 0.0), jnp.where(odd, 0.0, bottom)
    halo, mixed, more = ([ref[at].astype(F32) for ref in (above, below)] for at in range(3))
    near, next_near = (0, pairs - 1), (1, pairs - 2)
    sides = range(2)

    def order(side, one, two):
        return (one, two) if side == 0 else (two, one)

    for side in sides:
        store_shifts(jnp.where(beyond[side], more[side], mixed[side]), fs.at[side], 0)
        store_shifts(halo[side], fs.at[side], 1)
        store_shifts(with_rim(f[near[side]], edge[near[side]]), fs.at[side], 2)
    for k in (1, 0):
        for side in sides:
            pre = band_dot(*order(side, (fs.at[side], k), (fs.at[side], k + 1)), w1)
            sig = sigmoid(pre)
            act = pre * sig
            if k == 1:
                slope[side] = sig + act * (1.0 - sig)
            act = act * (flags[side] if k == 0 else jnp.where(beyond[side], flags[side], 1.0))
            store_shifts(rim_masked(act, rim), hs.at[side], k)
    for k in (1, 0):
        for side in sides:
            if k == 0:
                grad = pltpu.roll(jnp.where(beyond[side], mixed[side], more[side]), HALF, 1)
            else:
                grad = with_rim(g[near[side]], edge[pairs + near[side]])
            inward = (hs.at[side], 1) if k == 0 else (hs_edge, side)
            pre = band_dot(*order(side, (hs.at[side], k), inward), w2)
            sig = sigmoid(pre)
            delta = grad * (sig + pre * sig * (1.0 - sig))
            store_shifts(delta, ds2.at[side], k)
    for k in (1, 0):
        for side in sides:
            inward = (ds2.at[side], 1) if k == 0 else (ds2_edge, side)
            back = band_dot(*order(side, (ds2.at[side], k), inward), v2)
            value = back * slope[side] if k == 0 else back * slope_edge[side]
            value = rim_masked(value, rim)
            if k == 0:
                end[side] = jnp.where(beyond[side], value * known[side], value).astype(BF)
                value = jnp.where(beyond[side], 0.0, value)
            store_shifts(value, ds1.at[side], k)
            if k == 1:
                for s in range(3):
                    ds1_next[side, s] = ds1[side, 1, s]
            if k == 0:
                tall = row.shape[0]
                first, second = value[:tall], value[value.shape[0] - tall :]
                if side == 0:
                    first = pltpu.roll(first, HALF, 1)
                else:
                    second = pltpu.roll(second, HALF, 1)
                rows.append(first + second)
    row[...] = jnp.where(odd, rows[1], rows[0]).astype(BF)

    acc1[...] = acc1_in[...]
    acc2[...] = acc2_in[...]
    for side in sides:
        hid = order(side, hs[side, 1, 1, :cols].T, hs_edge[side, 1, :cols].T)
        add_one(acc2, jnp.concatenate(hid, axis=0), [ds2[side, 1, s, :cols] for s in range(3)])
        own = f[near[side]].T
        for k in (1, 0):
            feat = order(side, fs[side, 1, 1, :cols].T, own) if k == 0 else order(side, own, f[next_near[side]].T)
            add_one(acc1, jnp.concatenate(feat, axis=0), [ds1[side, k, s, :cols] for s in range(3)])
    take_terms(acc1, acc2, mine, other)


def with_row(center, row, side):
    turned = pltpu.roll(row, HALF, 1)
    first, second = (row, turned) if side == 0 else (turned, row)
    cols = center.shape[0] - row.shape[0]
    full = jnp.concatenate([first[:cols], second], axis=0)
    return center + jnp.where(half_lanes(side), full, 0.0)


def last_body(end, ds1_next, ds1, row, weights, gf, done, ends):
    pairs, cols = gf.shape[:2]
    done[...] = jnp.zeros_like(done)
    odd = odd_place("row")
    from_prev = jnp.where(odd, 0.0, row[...].astype(F32))
    from_next = jnp.where(odd, row[...].astype(F32), 0.0)
    store_shifts(with_row(end[0].astype(F32), from_prev, 0), ends, 0)
    store_shifts(with_row(end[1].astype(F32), from_next, 1), ends, 1)
    places = [(ends, 0), (ds1_next, 0)] + [(ds1, j) for j in range(pairs - 3)] + [(ds1_next, 1), (ends, 1)]
    for j in range(pairs):
        gf[j] = band_dot(places[j], places[j + 1], weights.at[3])[:cols].astype(BF)


def cost(pair_count):
    return pl.CostEstimate(flops=pair_count * 272 * 768 * 128 * 2, bytes_accessed=4 * 2**20, transcendentals=0)


PARAMS = pltpu.CompilerParams(vmem_limit_bytes=32 * 2**20)


def inner(f, g, edge, weights):
    pairs, cols = f.shape[:2]
    wide = cols + RIM

    def shifts(count):
        return (count, 3, wide, LANES)

    return pl.pallas_call(
        inner_body,
        out_shape=(
            jax.ShapeDtypeStruct(shifts(2), BF),
            jax.ShapeDtypeStruct(shifts(2), BF),
            jax.ShapeDtypeStruct((2, wide, LANES), F32),
            jax.ShapeDtypeStruct(shifts(pairs - 3), BF),
            jax.ShapeDtypeStruct((2 * LANES, 3 * LANES), F32),
            jax.ShapeDtypeStruct((2 * LANES, 3 * LANES), F32),
        ),
        scratch_shapes=[
            pltpu.VMEM(shifts(pairs), BF),
            pltpu.VMEM(shifts(pairs - 1), BF),
            pltpu.VMEM(shifts(pairs - 2), BF),
            pltpu.VMEM((pairs - 1, wide, LANES), F32),
            pltpu.VMEM((pairs - 1, LANES, cols), BF),
            pltpu.VMEM((pairs - 1, LANES, cols), BF),
        ],
        compiler_params=PARAMS,
        cost_estimate=cost(22),
        name="inner",
    )(f, g, edge, weights)


def outer(f, *rest):
    wide = f.shape[1] + RIM

    def shifts(*count):
        return (*count, 3, wide, LANES)

    row = jax.ShapeDtypeStruct((wide // 2 + RIM // 2, LANES), BF)
    return pl.pallas_call(
        rim_body,
        out_shape=(
            jax.ShapeDtypeStruct(shifts(2), BF),
            jax.ShapeDtypeStruct((2, wide, LANES), BF),
            row,
            jax.ShapeDtypeStruct((9 * HALF // 2, LANES), F32),
            jax.ShapeDtypeStruct((9 * HALF // 2, LANES), F32),
        ),
        scratch_shapes=[
            pltpu.VMEM(shifts(2, 3), BF),
            pltpu.VMEM(shifts(2, 2), BF),
            pltpu.VMEM(shifts(2, 2), BF),
            pltpu.VMEM((2, wide, LANES), F32),
            pltpu.VMEM(shifts(2, 2), BF),
            pltpu.VMEM((2 * LANES, 3 * LANES), F32),
            pltpu.VMEM((2 * LANES, 3 * LANES), F32),
        ],
        compiler_params=PARAMS,
        cost_estimate=cost(14),
        name="outer",
    )(f, *rest)


def last(end, ds1_next, ds1, row, weights, cols):
    pairs = ds1.shape[0] + 3
    return pl.pallas_call(
        last_body,
        out_shape=(
            jax.ShapeDtypeStruct((pairs, cols, LANES), BF),
            jax.ShapeDtypeStruct((8, LANES), F32),
        ),
        scratch_shapes=[pltpu.VMEM((2, 3, cols + RIM, LANES), BF)],
        compiler_params=PARAMS,
        cost_estimate=cost(8),
        name="last",
    )(end, ds1_next, ds1, row, weights)


def four_body(own, one, two, three, done, out):
    low = [ref[...].astype(F32) for ref in (own, one, two, three)]
    out[...] = (low[0] + low[1]) + (low[2] + low[3])


def sum_four(own, got, done):
    return pl.pallas_call(
        four_body,
        out_shape=jax.ShapeDtypeStruct(own.shape, F32),
        compiler_params=pltpu.CompilerParams(vmem_limit_bytes=4 * 2**20),
        name="sum_four",
    )(own, *got, done)


def finish_body(part, other, one, two, *, scale):
    half = HALF // 2
    second = lax.axis_index("dp") == 1
    for tap in range(9):
        mine, theirs = (ref[tap * half : (tap + 1) * half] for ref in (part, other))
        rows = [jnp.where(second, theirs, mine), jnp.where(second, mine, theirs)]
        both = jnp.concatenate(rows, axis=0).T * scale
        one[tap // 3, tap % 3] = both[:HALF]
        two[tap // 3, tap % 3] = both[HALF:]


def finish(part, other, scale):
    shape = jax.ShapeDtypeStruct((3, 3, HALF, HALF), F32)
    return pl.pallas_call(
        functools.partial(finish_body, scale=scale),
        out_shape=(shape, shape),
        compiler_params=pltpu.CompilerParams(vmem_limit_bytes=4 * 2**20),
        name="finish",
    )(part, other)


def reduced(mine, other, done):
    sizes = [lax.axis_size(axis) for axis in AXES]
    swap_cores = [(0, 1), (1, 0)]
    if sizes[0] != 2 or any(size & (size - 1) for size in sizes):
        first = lax.axis_index("dp") == 0
        both = lax.psum([jnp.where(first, mine, other), jnp.where(first, other, mine)], AXES)
        return jnp.where(first, *both), jnp.where(first, both[1], both[0])
    part = mine + lax.ppermute(other, "dp", swap_cores)
    across = [(0, 1 << b) for b in range(sizes[2].bit_length() - 1)]
    down = [(1 << b, 0) for b in range(sizes[1].bit_length() - 1)]
    bits = []
    while across or down:
        bits += down[:1] + across[:1]
        down, across = down[1:], across[1:]
    groups = [bits[at : at + 2] for at in range(0, len(bits), 2)]
    for at in range(len(groups)):
        mine = [groups[at], groups[(at + len(groups) // 2) % len(groups)]]
        if len(mine[0]) != len(mine[1]):
            mine[1] = mine[0]
        low = part.astype(BF)
        got = []
        for member in range(1, 1 << len(mine[0])):
            perm = []
            for core in range(2):
                flips = [flip for k, flip in enumerate(mine[core]) if member >> k & 1]
                for r in range(sizes[1]):
                    for c in range(sizes[2]):
                        to_r, to_c = r, c
                        for flip in flips:
                            to_r, to_c = to_r ^ flip[0], to_c ^ flip[1]
                        base = core * sizes[1]
                        perm.append(((base + r) * sizes[2] + c, (base + to_r) * sizes[2] + to_c))
            got.append(lax.ppermute(low, AXES, perm))
        if at == 1 and len(got) > 1:
            part = sum_four(low, got, done)
            continue
        got = [one.astype(F32) for one in got]
        part = low.astype(F32) + got[0]
        if len(got) > 1:
            part = part + (got[1] + got[2])
    return part, lax.ppermute(part, "dp", swap_cores)


def shards(features, grad_out, kernel_one, kernel_two):
    slides, chans, rows, cols = features.shape
    pairs = rows // 2
    feat, grad = to_pairs(features), to_pairs(grad_out)
    def turn(low, high, is_lower):
        return turn_edges(jnp.where(is_lower, high, low))

    both = jnp.concatenate([features, grad_out], axis=2)
    from_left, from_right = swap(both[..., : RIM // 2], both[..., cols - RIM // 2 :], "col", turn)
    edge = jnp.concatenate([from_right, from_left], axis=1)
    weights, own_near, own_far = prep(feat, grad, kernel_one, kernel_two)
    sent_near, sent_far = frame(own_near, own_far, edge)
    got_near = lax.ppermute(sent_near, "row", neighbours("row", 0))
    got_far = lax.ppermute(sent_far, "row", neighbours("row", 1))
    odd = is_low("row", 1)
    one, more = got_near[:2], got_near[2:]
    above = jnp.concatenate([jnp.where(odd, one, got_far), jnp.where(odd, more, jnp.zeros_like(more))])
    below = jnp.concatenate([jnp.where(odd, got_far, one), jnp.where(odd, jnp.zeros_like(more), more)])
    hs_edge, ds2_edge, slope_edge, ds1, acc1, acc2 = inner(feat, grad, edge, weights)
    ds1_next, end, row, mine, other = outer(
        feat, grad, edge, above, below, weights, hs_edge, ds2_edge, slope_edge, acc1, acc2
    )
    row = lax.ppermute(row, "row", neighbours("row", 1))
    gf, done = last(end, ds1_next, ds1, row, weights, cols)
    part, other = reduced(mine, other, done)
    count = slides * lax.axis_size("dp") * rows * lax.axis_size("row") * cols * lax.axis_size("col")
    grad_one, grad_two = finish(part, other, float(count) ** -0.5)
    return from_pairs(gf), grad_one, grad_two


def solution(mesh):
    return jax.shard_map(
        shards,
        mesh=mesh,
        in_specs=(P("dp", None, "row", "col"), P("dp", None, "row", "col"), P(), P()),
        out_specs=(P("dp", None, "row", "col"), P(), P()),
        check_vma=False,
    )
```

```python
import functools

import jax
import jax.numpy as jnp
from jax import lax
from jax.experimental import pallas as pl
from jax.experimental.pallas import tpu as pltpu
from jax.sharding import PartitionSpec as P

BF = jnp.bfloat16
F32 = jnp.float32
AXES = ("dp", "row", "col")
LANES = 128
HALF = LANES // 2
RIM = 16


def neighbours(axis, parity):
    count = lax.axis_size(axis)
    pairs = []
    for i in range(parity, count - 1, 2):
        pairs += [(i, i + 1), (i + 1, i)]
    return pairs


def is_low(axis, parity):
    return lax.axis_index(axis) % 2 == parity


def swap(low, high, axis, turn):
    got = []
    for parity in range(2):
        perm = neighbours(axis, parity)
        if perm:
            got.append(lax.ppermute(turn(low, high, is_low(axis, parity)), axis, perm))
        else:
            got.append(jnp.zeros_like(got[0]))
    odd = is_low(axis, 1)
    return jnp.where(odd, got[0], got[1]), jnp.where(odd, got[1], got[0])


def odd_place(axis):
    return lax.rem(lax.axis_index(axis), 2) == 1


def to_pairs(cells):
    _, chans, rows, cols = cells.shape
    part = cells[0].reshape(chans, rows // 2, 2, cols)
    return part.transpose(1, 3, 2, 0).reshape(rows // 2, cols, 2 * chans)


def edges_body(*refs):
    out = refs[-1]
    at = 0
    for cells in refs[:-1]:
        turned = jnp.swapaxes(cells[0], 0, 1)
        for pair in range(turned.shape[0] // 2):
            out[at] = turned[2 * pair : 2 * pair + 2].reshape(2 * turned.shape[1], -1).T
            at += 1


def turn_edges(*parts):
    pairs = sum(part.shape[2] // 2 for part in parts)
    return pl.pallas_call(
        edges_body,
        out_shape=jax.ShapeDtypeStruct((pairs, parts[0].shape[3], LANES), BF),
        compiler_params=pltpu.CompilerParams(vmem_limit_bytes=8 * 2**20),
        name="edges",
    )(*parts)


def from_pairs(pairs):
    count, cols, lanes = pairs.shape
    part = pairs.reshape(count, cols, 2, lanes // 2)
    return part.transpose(3, 0, 2, 1).reshape(1, lanes // 2, 2 * count, cols)


def make_weights(k1, k2, ahead, back):
    zero = jnp.zeros((HALF, HALF), BF)
    for layer, taps in enumerate((k1, k2)):
        flat = {(ky, kx): taps[ky, kx] for ky in range(3) for kx in range(3)}
        turned = {at: flat[at].astype(F32).T.astype(BF) for at in flat}
        for p in range(2):
            for r in range(2):
                kys = [2 * p + r - a for a in range(2)]
                at = (p * 2 + r) * HALF
                for kx in range(3):
                    ahead[layer, at : at + HALF, kx * LANES : (kx + 1) * LANES] = jnp.concatenate(
                        [turned.get((ky, kx), zero) for ky in kys], axis=1
                    )
                    to = ((p * 3 + kx) * 2 + r) * HALF
                    back[layer, to : to + HALF] = jnp.concatenate(
                        [flat.get((2 - ky, 2 - kx), zero) for ky in kys], axis=1
                    )


def outer_units(feats, grads, high):
    pairs = feats.shape[0]
    near = jnp.where(high, pairs - 1, 0)
    then = feats[jnp.where(high, pairs - 2, 1)].astype(F32)
    grad = pltpu.roll(grads[near].astype(F32), HALF, 1)
    lane = lax.broadcasted_iota(jnp.int32, then.shape, 1)
    own = (lane >= HALF).astype(jnp.int32) == jnp.where(high, 1, 0)
    return feats[near], jnp.where(own, then, grad).astype(BF), jnp.where(own, grad, then).astype(BF)


def prep_body(f, g, k1, k2, ahead, back, sent_near, sent_far):
    make_weights(k1, k2, ahead, back)
    odd = odd_place("row")
    for sent, high in ((sent_near, jnp.logical_not(odd)), (sent_far, odd)):
        units = outer_units(f, g, high)
        for at in range(sent.shape[0]):
            sent[at] = units[at]


def prep(feat, grad, kernel_one, kernel_two):
    weights = [jax.ShapeDtypeStruct(shape, BF) for shape in ((2, 4 * HALF, 3 * LANES), (2, 12 * HALF, LANES))]
    sent = [jax.ShapeDtypeStruct((units, *feat.shape[1:]), BF) for units in (3, 2)]
    return pl.pallas_call(
        prep_body,
        out_shape=(*weights, *sent),
        compiler_params=pltpu.CompilerParams(vmem_limit_bytes=12 * 2**20),
        cost_estimate=cost(2),
        name="prep",
    )(feat, grad, kernel_one, kernel_two)


def frame_body(own_near, own_far, edge, sent_near, sent_far):
    pairs, cols = edge.shape[0] // 2, own_near.shape[1]
    odd = odd_place("row")
    feats, grads = edge.at[:pairs], edge.at[pairs:]
    for own, sent, high in ((own_near, sent_near, jnp.logical_not(odd)), (own_far, sent_far, odd)):
        units = outer_units(feats, grads, high)
        for at in range(sent.shape[0]):
            sent[at, :cols] = own[at]
            sent[at, cols:] = units[at]


def frame(own_near, own_far, edge):
    wide = own_near.shape[1] + RIM
    return pl.pallas_call(
        frame_body,
        out_shape=[jax.ShapeDtypeStruct((own.shape[0], wide, LANES), BF) for own in (own_near, own_far)],
        compiler_params=pltpu.CompilerParams(vmem_limit_bytes=8 * 2**20),
        name="frame",
    )(own_near, own_far, edge)


def sigmoid(value):
    return 0.5 * jnp.tanh(0.5 * value) + 0.5


def with_rim(own, rim):
    return jnp.concatenate([own.astype(F32), rim.astype(F32)], axis=0)


def store_shifts(value, out, index):
    out[index, 0] = pltpu.roll(value, 1, 0).astype(BF)
    out[index, 1] = value.astype(BF)
    out[index, 2] = pltpu.roll(value, value.shape[0] - 1, 0).astype(BF)


def band_dot(first, second, weight):
    parts = [ref[index, s] for ref, index in (first, second) for s in range(3)]
    return jnp.dot(jnp.concatenate(parts, axis=1), weight[...], preferred_element_type=F32)


def row_dot(first, second, weight):
    three = jnp.dot(jnp.concatenate([first, second], axis=1), weight[...], preferred_element_type=F32)
    left = pltpu.roll(three[:, :LANES], 1, 0)
    right = pltpu.roll(three[:, 2 * LANES :], three.shape[0] - 1, 0)
    return left + three[:, LANES : 2 * LANES] + right


def edge_masks():
    row, col = lax.axis_index("row"), lax.axis_index("col")
    top = (row > 0).astype(F32)
    bottom = (row < lax.axis_size("row") - 1).astype(F32)
    left = (col > 0).astype(F32)
    right = (col < lax.axis_size("col") - 1).astype(F32)
    place = lax.broadcasted_iota(jnp.int32, (RIM, LANES), 0)
    rim = jnp.where(place < RIM // 2, right, left)
    return top, bottom, rim


def rim_masked(value, rim):
    own = value.shape[0] - RIM
    return jnp.concatenate([value[:own], value[own:] * rim], axis=0)


def add_one(acc, feat_t, pieces):
    near = jnp.concatenate(pieces, axis=1)
    acc[...] += jnp.dot(feat_t, near, preferred_element_type=F32)


def add_dot(acc, lefts, rights):
    left, right = jnp.concatenate(lefts, axis=1), jnp.concatenate(rights, axis=0)
    acc[...] += jnp.dot(left, right, preferred_element_type=F32)


def inner_body(f, g, edge, ahead, back, hs_edge, ds2_edge, slope_edge, ds1, acc1, acc2, fs, hs, ds2, slope, ht, ft):
    w1, w2, v2 = ahead.at[0], ahead.at[1], back.at[1]
    pairs, cols = f.shape[:2]
    _, _, rim = edge_masks()

    @pl.loop(0, pairs, unroll=True)
    def _(j):
        fs[j] = with_rim(f[j], edge[j]).astype(BF)

    @pl.loop(0, pairs - 1, unroll=True)
    def _(j):
        pre = row_dot(fs[j], fs[j + 1], w1)
        sig = sigmoid(pre)
        act = pre * sig
        slope[j] = sig + act * (1.0 - sig)
        hs[j] = rim_masked(act, rim).astype(BF)
        ht[j] = hs[j, :cols].T

    @pl.loop(0, pairs - 2, unroll=True)
    def _(j):
        pre = row_dot(hs[j], hs[j + 1], w2)
        sig = sigmoid(pre)
        grad = with_rim(g[j + 1], edge[pairs + j + 1])
        delta = grad * (sig + pre * sig * (1.0 - sig))
        store_shifts(delta, ds2, j)

    @pl.loop(0, pairs - 3, unroll=True)
    def _(j):
        value = band_dot((ds2, j), (ds2, j + 1), v2)
        store_shifts(rim_masked(value * slope[j + 1], rim), ds1, j)

    acc1[...] = jnp.zeros_like(acc1)
    acc2[...] = jnp.zeros_like(acc2)

    @pl.loop(0, pairs - 2, unroll=True)
    def _(j):
        both = jnp.concatenate([ht[j], ht[j + 1]], axis=0)
        add_one(acc2, both, [ds2[j, s, :cols] for s in range(3)])

    @pl.loop(1, pairs - 1, unroll=True)
    def _(j):
        ft[j] = f[j].T

    @pl.loop(0, pairs - 3, unroll=True)
    def _(j):
        both = jnp.concatenate([ft[j + 1], ft[j + 2]], axis=0)
        add_one(acc1, both, [ds1[j, s, :cols] for s in range(3)])

    for side, at in ((0, 0), (1, pairs - 2)):
        hs_edge[side] = hs[at]
        slope_edge[side] = slope[at]
    for side, at in ((0, 0), (1, pairs - 3)):
        ds2_edge[side] = ds2[at]


def take_terms(acc1, acc2, mine, other):
    blocks = []
    for ky in range(3):
        for kx in range(3):
            at = (2 - kx) * LANES
            sums = []
            for acc in (acc1, acc2):
                first = acc[ky * HALF : (ky + 1) * HALF, at : at + HALF]
                sums.append(first + acc[(ky + 1) * HALF : (ky + 2) * HALF, at + HALF : at + LANES])
            blocks.append(jnp.concatenate(sums, axis=1))
    half = HALF // 2
    second = lax.axis_index("dp") == 1
    for tap in range(9):
        one, two = blocks[tap][:half], blocks[tap][half:]
        mine[tap * half : (tap + 1) * half] = jnp.where(second, two, one)
        other[tap * half : (tap + 1) * half] = jnp.where(second, one, two)


def half_lanes(side):
    upper = lax.broadcasted_iota(jnp.int32, (1, LANES), 1) >= HALF
    return upper == (side == 1)


def rim_body(
    f, g, edge, above, below, ahead, back, hs_edge, ds2_edge, slope_edge, acc1_in, acc2_in,
    ds1_next, end, row, mine, other, fs, hs, ds2, slope, ds1, acc1, acc2,
):
    pairs, cols = f.shape[:2]
    top, bottom, rim = edge_masks()
    flags = (top, bottom)
    beyond = [half_lanes(side) for side in range(2)]
    w1, w2, v2 = ahead.at[0], ahead.at[1], back.at[1]
    rows = []
    odd = odd_place("row")
    known = jnp.where(odd, top, 0.0), jnp.where(odd, 0.0, bottom)
    halo, mixed, more = ([ref[at].astype(F32) for ref in (above, below)] for at in range(3))
    near, next_near = (0, pairs - 1), (1, pairs - 2)
    sides = range(2)

    def order(side, one, two):
        return (one, two) if side == 0 else (two, one)

    for side in sides:
        fs[side, 0] = jnp.where(beyond[side], more[side], mixed[side]).astype(BF)
        fs[side, 1] = halo[side].astype(BF)
        fs[side, 2] = with_rim(f[near[side]], edge[near[side]]).astype(BF)
    for k in (1, 0):
        for side in sides:
            pre = row_dot(*order(side, fs[side, k], fs[side, k + 1]), w1)
            sig = sigmoid(pre)
            act = pre * sig
            if k == 1:
                slope[side] = sig + act * (1.0 - sig)
            act = act * (flags[side] if k == 0 else jnp.where(beyond[side], flags[side], 1.0))
            hs[side, k] = rim_masked(act, rim).astype(BF)
    for k in (1, 0):
        for side in sides:
            if k == 0:
                grad = pltpu.roll(jnp.where(beyond[side], mixed[side], more[side]), HALF, 1)
            else:
                grad = with_rim(g[near[side]], edge[pairs + near[side]])
            inward = hs[side, 1] if k == 0 else hs_edge[side]
            pre = row_dot(*order(side, hs[side, k], inward), w2)
            sig = sigmoid(pre)
            delta = grad * (sig + pre * sig * (1.0 - sig))
            store_shifts(delta, ds2.at[side], k)
    for k in (1, 0):
        for side in sides:
            inward = (ds2.at[side], 1) if k == 0 else (ds2_edge, side)
            value = band_dot(*order(side, (ds2.at[side], k), inward), v2)
            value = value * (slope[side] if k == 0 else slope_edge[side])
            value = rim_masked(value, rim)
            if k == 0:
                end[side] = jnp.where(beyond[side], value * known[side], value).astype(BF)
                value = jnp.where(beyond[side], 0.0, value)
            store_shifts(value, ds1.at[side], k)
            if k == 1:
                for s in range(3):
                    ds1_next[side, s] = ds1[side, 1, s]
            if k == 0:
                tall = row.shape[0]
                first, second = value[:tall], value[value.shape[0] - tall :]
                if side == 0:
                    first = pltpu.roll(first, HALF, 1)
                else:
                    second = pltpu.roll(second, HALF, 1)
                rows.append(first + second)
    row[...] = jnp.where(odd, rows[1], rows[0]).astype(BF)

    acc1[...] = acc1_in[...]
    acc2[...] = acc2_in[...]
    lefts, rights = [], []
    for side in sides:
        hid = order(side, hs[side, 1, :cols].T, hs_edge[side, :cols].T)
        lefts.append(jnp.concatenate(hid, axis=0))
        rights.append(jnp.concatenate([ds2[side, 1, s, :cols] for s in range(3)], axis=1))
    add_dot(acc2, lefts, rights)
    lefts, rights = [], []
    for side in sides:
        own = f[near[side]].T
        for k in (1, 0):
            feat = order(side, fs[side, 1, :cols].T, own) if k == 0 else order(side, own, f[next_near[side]].T)
            lefts.append(jnp.concatenate(feat, axis=0))
            rights.append(jnp.concatenate([ds1[side, k, s, :cols] for s in range(3)], axis=1))
    add_dot(acc1, lefts, rights)
    take_terms(acc1, acc2, mine, other)


def with_row(center, row, side):
    turned = pltpu.roll(row, HALF, 1)
    first, second = (row, turned) if side == 0 else (turned, row)
    cols = center.shape[0] - row.shape[0]
    full = jnp.concatenate([first[:cols], second], axis=0)
    return center + jnp.where(half_lanes(side), full, 0.0)


def last_body(end, ds1_next, ds1, row, back, gf, done, ends):
    pairs, cols = gf.shape[:2]
    done[...] = jnp.zeros_like(done)
    odd = odd_place("row")
    from_prev = jnp.where(odd, 0.0, row[...].astype(F32))
    from_next = jnp.where(odd, row[...].astype(F32), 0.0)
    store_shifts(with_row(end[0].astype(F32), from_prev, 0), ends, 0)
    store_shifts(with_row(end[1].astype(F32), from_next, 1), ends, 1)
    places = [(ends, 0), (ds1_next, 0)] + [(ds1, j) for j in range(pairs - 3)] + [(ds1_next, 1), (ends, 1)]
    for j in range(pairs):
        gf[j] = band_dot(places[j], places[j + 1], back.at[0])[:cols].astype(BF)


def cost(pair_count):
    return pl.CostEstimate(flops=pair_count * 272 * 768 * 128 * 2, bytes_accessed=4 * 2**20, transcendentals=0)


PARAMS = pltpu.CompilerParams(vmem_limit_bytes=32 * 2**20)


def inner(f, g, edge, ahead, back):
    pairs, cols = f.shape[:2]
    wide = cols + RIM

    def shifts(count):
        return (count, 3, wide, LANES)

    return pl.pallas_call(
        inner_body,
        out_shape=(
            jax.ShapeDtypeStruct((2, wide, LANES), BF),
            jax.ShapeDtypeStruct(shifts(2), BF),
            jax.ShapeDtypeStruct((2, wide, LANES), F32),
            jax.ShapeDtypeStruct(shifts(pairs - 3), BF),
            jax.ShapeDtypeStruct((2 * LANES, 3 * LANES), F32),
            jax.ShapeDtypeStruct((2 * LANES, 3 * LANES), F32),
        ),
        scratch_shapes=[
            pltpu.VMEM((pairs, wide, LANES), BF),
            pltpu.VMEM((pairs - 1, wide, LANES), BF),
            pltpu.VMEM(shifts(pairs - 2), BF),
            pltpu.VMEM((pairs - 1, wide, LANES), F32),
            pltpu.VMEM((pairs - 1, LANES, cols), BF),
            pltpu.VMEM((pairs - 1, LANES, cols), BF),
        ],
        compiler_params=PARAMS,
        cost_estimate=cost(22),
        name="inner",
    )(f, g, edge, ahead, back)


def outer(f, *rest):
    wide = f.shape[1] + RIM

    def shifts(*count):
        return (*count, 3, wide, LANES)

    row = jax.ShapeDtypeStruct((wide // 2 + RIM // 2, LANES), BF)
    return pl.pallas_call(
        rim_body,
        out_shape=(
            jax.ShapeDtypeStruct(shifts(2), BF),
            jax.ShapeDtypeStruct((2, wide, LANES), BF),
            row,
            jax.ShapeDtypeStruct((9 * HALF // 2, LANES), F32),
            jax.ShapeDtypeStruct((9 * HALF // 2, LANES), F32),
        ),
        scratch_shapes=[
            pltpu.VMEM((2, 3, wide, LANES), BF),
            pltpu.VMEM((2, 2, wide, LANES), BF),
            pltpu.VMEM(shifts(2, 2), BF),
            pltpu.VMEM((2, wide, LANES), F32),
            pltpu.VMEM(shifts(2, 2), BF),
            pltpu.VMEM((2 * LANES, 3 * LANES), F32),
            pltpu.VMEM((2 * LANES, 3 * LANES), F32),
        ],
        compiler_params=PARAMS,
        cost_estimate=cost(14),
        name="outer",
    )(f, *rest)


def last(end, ds1_next, ds1, row, back, cols):
    pairs = ds1.shape[0] + 3
    return pl.pallas_call(
        last_body,
        out_shape=(
            jax.ShapeDtypeStruct((pairs, cols, LANES), BF),
            jax.ShapeDtypeStruct((8, LANES), F32),
        ),
        scratch_shapes=[pltpu.VMEM((2, 3, cols + RIM, LANES), BF)],
        compiler_params=PARAMS,
        cost_estimate=cost(8),
        name="last",
    )(end, ds1_next, ds1, row, back)


def four_body(own, one, two, three, done, out):
    low = [ref[...].astype(F32) for ref in (own, one, two, three)]
    out[...] = (low[0] + low[1]) + (low[2] + low[3])


def sum_four(own, got, done):
    return pl.pallas_call(
        four_body,
        out_shape=jax.ShapeDtypeStruct(own.shape, F32),
        compiler_params=pltpu.CompilerParams(vmem_limit_bytes=4 * 2**20),
        name="sum_four",
    )(own, *got, done)


def finish_body(part, other, one, two, *, scale):
    half = HALF // 2
    second = lax.axis_index("dp") == 1
    for tap in range(9):
        mine, theirs = (ref[tap * half : (tap + 1) * half] for ref in (part, other))
        rows = [jnp.where(second, theirs, mine), jnp.where(second, mine, theirs)]
        both = jnp.concatenate(rows, axis=0).T * scale
        one[tap // 3, tap % 3] = both[:HALF]
        two[tap // 3, tap % 3] = both[HALF:]


def finish(part, other, scale):
    shape = jax.ShapeDtypeStruct((3, 3, HALF, HALF), F32)
    return pl.pallas_call(
        functools.partial(finish_body, scale=scale),
        out_shape=(shape, shape),
        compiler_params=pltpu.CompilerParams(vmem_limit_bytes=4 * 2**20),
        name="finish",
    )(part, other)


def reduced(mine, other, done):
    sizes = [lax.axis_size(axis) for axis in AXES]
    swap_cores = [(0, 1), (1, 0)]
    if sizes[0] != 2 or any(size & (size - 1) for size in sizes):
        first = lax.axis_index("dp") == 0
        both = lax.psum([jnp.where(first, mine, other), jnp.where(first, other, mine)], AXES)
        return jnp.where(first, *both), jnp.where(first, both[1], both[0])
    part = mine + lax.ppermute(other, "dp", swap_cores)
    across = [(0, 1 << b) for b in range(sizes[2].bit_length() - 1)]
    down = [(1 << b, 0) for b in range(sizes[1].bit_length() - 1)]
    bits = []
    while across or down:
        bits += down[:1] + across[:1]
        down, across = down[1:], across[1:]
    groups = [bits[at : at + 2] for at in range(0, len(bits), 2)]
    for at in range(len(groups)):
        mine = [groups[at], groups[(at + len(groups) // 2) % len(groups)]]
        if len(mine[0]) != len(mine[1]):
            mine[1] = mine[0]
        low = part.astype(BF)
        got = []
        for member in range(1, 1 << len(mine[0])):
            perm = []
            for core in range(2):
                flips = [flip for k, flip in enumerate(mine[core]) if member >> k & 1]
                for r in range(sizes[1]):
                    for c in range(sizes[2]):
                        to_r, to_c = r, c
                        for flip in flips:
                            to_r, to_c = to_r ^ flip[0], to_c ^ flip[1]
                        base = core * sizes[1]
                        perm.append(((base + r) * sizes[2] + c, (base + to_r) * sizes[2] + to_c))
            got.append(lax.ppermute(low, AXES, perm))
        if at == 1 and len(got) > 1:
            part = sum_four(low, got, done)
            continue
        got = [one.astype(F32) for one in got]
        part = low.astype(F32) + got[0]
        if len(got) > 1:
            part = part + (got[1] + got[2])
    return part, lax.ppermute(part, "dp", swap_cores)


def shards(features, grad_out, kernel_one, kernel_two):
    slides, chans, rows, cols = features.shape
    pairs = rows // 2
    feat, grad = to_pairs(features), to_pairs(grad_out)
    def turn(low, high, is_lower):
        return turn_edges(jnp.where(is_lower, high, low))

    both = jnp.concatenate([features, grad_out], axis=2)
    from_left, from_right = swap(both[..., : RIM // 2], both[..., cols - RIM // 2 :], "col", turn)
    edge = jnp.concatenate([from_right, from_left], axis=1)
    ahead, back, own_near, own_far = prep(feat, grad, kernel_one, kernel_two)
    sent_near, sent_far = frame(own_near, own_far, edge)
    got_near = lax.ppermute(sent_near, "row", neighbours("row", 0))
    got_far = lax.ppermute(sent_far, "row", neighbours("row", 1))
    odd = is_low("row", 1)
    one, more = got_near[:2], got_near[2:]
    above = jnp.concatenate([jnp.where(odd, one, got_far), jnp.where(odd, more, jnp.zeros_like(more))])
    below = jnp.concatenate([jnp.where(odd, got_far, one), jnp.where(odd, jnp.zeros_like(more), more)])
    hs_edge, ds2_edge, slope_edge, ds1, acc1, acc2 = inner(feat, grad, edge, ahead, back)
    ds1_next, end, row, mine, other = outer(
        feat, grad, edge, above, below, ahead, back, hs_edge, ds2_edge, slope_edge, acc1, acc2
    )
    row = lax.ppermute(row, "row", neighbours("row", 1))
    gf, done = last(end, ds1_next, ds1, row, back, cols)
    part, other = reduced(mine, other, done)
    count = slides * lax.axis_size("dp") * rows * lax.axis_size("row") * cols * lax.axis_size("col")
    grad_one, grad_two = finish(part, other, float(count) ** -0.5)
    return from_pairs(gf), grad_one, grad_two


def solution(mesh):
    return jax.shard_map(
        shards,
        mesh=mesh,
        in_specs=(P("dp", None, "row", "col"), P("dp", None, "row", "col"), P(), P()),
        out_specs=(P("dp", None, "row", "col"), P(), P()),
        check_vma=False,
    )
```

```python
import functools

import jax
import jax.numpy as jnp
from jax import lax
from jax.experimental import pallas as pl
from jax.experimental.pallas import tpu as pltpu
from jax.sharding import PartitionSpec as P

BF = jnp.bfloat16
F32 = jnp.float32
AXES = ("dp", "row", "col")
LANES = 128
HALF = LANES // 2
RIM = 16


def neighbours(axis, parity):
    count = lax.axis_size(axis)
    pairs = []
    for i in range(parity, count - 1, 2):
        pairs += [(i, i + 1), (i + 1, i)]
    return pairs


def is_low(axis, parity):
    return lax.axis_index(axis) % 2 == parity


def swap(low, high, axis, turn):
    got = []
    for parity in range(2):
        perm = neighbours(axis, parity)
        if perm:
            got.append(lax.ppermute(turn(low, high, is_low(axis, parity)), axis, perm))
        else:
            got.append(jnp.zeros_like(got[0]))
    odd = is_low(axis, 1)
    return jnp.where(odd, got[0], got[1]), jnp.where(odd, got[1], got[0])


def odd_place(axis):
    return lax.rem(lax.axis_index(axis), 2) == 1


def to_pairs(cells):
    _, chans, rows, cols = cells.shape
    part = cells[0].reshape(chans, rows // 2, 2, cols)
    return part.transpose(1, 3, 2, 0).reshape(rows // 2, cols, 2 * chans)


def edges_body(*refs):
    out = refs[-1]
    at = 0
    for cells in refs[:-1]:
        turned = jnp.swapaxes(cells[0], 0, 1)
        for pair in range(turned.shape[0] // 2):
            out[at] = turned[2 * pair : 2 * pair + 2].reshape(2 * turned.shape[1], -1).T
            at += 1


def turn_edges(*parts):
    pairs = sum(part.shape[2] // 2 for part in parts)
    return pl.pallas_call(
        edges_body,
        out_shape=jax.ShapeDtypeStruct((pairs, parts[0].shape[3], LANES), BF),
        compiler_params=pltpu.CompilerParams(vmem_limit_bytes=8 * 2**20),
        name="edges",
    )(*parts)


def from_pairs(pairs):
    count, cols, lanes = pairs.shape
    part = pairs.reshape(count, cols, 2, lanes // 2)
    return part.transpose(3, 0, 2, 1).reshape(1, lanes // 2, 2 * count, cols)


def make_weights(k1, k2, ahead, back):
    zero = jnp.zeros((HALF, HALF), BF)
    for layer, taps in enumerate((k1, k2)):
        flat = {(ky, kx): taps[ky, kx] for ky in range(3) for kx in range(3)}
        turned = {at: flat[at].astype(F32).T.astype(BF) for at in flat}
        for p in range(2):
            for r in range(2):
                kys = [2 * p + r - a for a in range(2)]
                at = (p * 2 + r) * HALF
                for kx in range(3):
                    ahead[layer, at : at + HALF, kx * LANES : (kx + 1) * LANES] = jnp.concatenate(
                        [turned.get((ky, kx), zero) for ky in kys], axis=1
                    )
                    to = ((p * 3 + kx) * 2 + r) * HALF
                    back[layer, to : to + HALF] = jnp.concatenate(
                        [flat.get((2 - ky, 2 - kx), zero) for ky in kys], axis=1
                    )


def outer_units(feats, grads, high):
    pairs = feats.shape[0]
    near = jnp.where(high, pairs - 1, 0)
    then = feats[jnp.where(high, pairs - 2, 1)].astype(F32)
    grad = pltpu.roll(grads[near].astype(F32), HALF, 1)
    lane = lax.broadcasted_iota(jnp.int32, then.shape, 1)
    own = (lane >= HALF).astype(jnp.int32) == jnp.where(high, 1, 0)
    return feats[near], jnp.where(own, then, grad).astype(BF), jnp.where(own, grad, then).astype(BF)


def prep_body(f, g, k1, k2, ahead, back, sent_near, sent_far):
    make_weights(k1, k2, ahead, back)
    odd = odd_place("row")
    for sent, high in ((sent_near, jnp.logical_not(odd)), (sent_far, odd)):
        units = outer_units(f, g, high)
        for at in range(sent.shape[0]):
            sent[at] = units[at]


def prep(feat, grad, kernel_one, kernel_two):
    weights = [jax.ShapeDtypeStruct(shape, BF) for shape in ((2, 4 * HALF, 3 * LANES), (2, 12 * HALF, LANES))]
    sent = [jax.ShapeDtypeStruct((units, *feat.shape[1:]), BF) for units in (3, 2)]
    return pl.pallas_call(
        prep_body,
        out_shape=(*weights, *sent),
        compiler_params=pltpu.CompilerParams(vmem_limit_bytes=12 * 2**20),
        cost_estimate=cost(2),
        name="prep",
    )(feat, grad, kernel_one, kernel_two)


def frame_body(own_near, own_far, edge, sent_near, sent_far):
    pairs, cols = edge.shape[0] // 2, own_near.shape[1]
    odd = odd_place("row")
    feats, grads = edge.at[:pairs], edge.at[pairs:]
    for own, sent, high in ((own_near, sent_near, jnp.logical_not(odd)), (own_far, sent_far, odd)):
        units = outer_units(feats, grads, high)
        for at in range(sent.shape[0]):
            sent[at, :cols] = own[at]
            sent[at, cols:] = units[at]


def frame(own_near, own_far, edge):
    wide = own_near.shape[1] + RIM
    return pl.pallas_call(
        frame_body,
        out_shape=[jax.ShapeDtypeStruct((own.shape[0], wide, LANES), BF) for own in (own_near, own_far)],
        compiler_params=pltpu.CompilerParams(vmem_limit_bytes=8 * 2**20),
        name="frame",
    )(own_near, own_far, edge)


def sigmoid(value):
    return 0.5 * jnp.tanh(0.5 * value) + 0.5


def with_rim(own, rim):
    return jnp.concatenate([own.astype(F32), rim.astype(F32)], axis=0)


def store_shifts(value, out, index):
    out[index, 0] = pltpu.roll(value, 1, 0).astype(BF)
    out[index, 1] = value.astype(BF)
    out[index, 2] = pltpu.roll(value, value.shape[0] - 1, 0).astype(BF)


def band_dot(first, second, weight):
    parts = [ref[index, s] for ref, index in (first, second) for s in range(3)]
    return jnp.dot(jnp.concatenate(parts, axis=1), weight[...], preferred_element_type=F32)


def row_dot(first, second, weight):
    three = jnp.dot(jnp.concatenate([first, second], axis=1), weight[...], preferred_element_type=F32)
    left = pltpu.roll(three[:, :LANES], 1, 0)
    right = pltpu.roll(three[:, 2 * LANES :], three.shape[0] - 1, 0)
    return left + three[:, LANES : 2 * LANES] + right


def edge_masks():
    row, col = lax.axis_index("row"), lax.axis_index("col")
    top = (row > 0).astype(F32)
    bottom = (row < lax.axis_size("row") - 1).astype(F32)
    left = (col > 0).astype(F32)
    right = (col < lax.axis_size("col") - 1).astype(F32)
    place = lax.broadcasted_iota(jnp.int32, (RIM, LANES), 0)
    rim = jnp.where(place < RIM // 2, right, left)
    return top, bottom, rim


def rim_masked(value, rim):
    own = value.shape[0] - RIM
    return jnp.concatenate([value[:own], value[own:] * rim], axis=0)


def add_one(acc, feat_t, pieces):
    near = jnp.concatenate(pieces, axis=1)
    acc[...] += jnp.dot(feat_t, near, preferred_element_type=F32)


def add_dot(acc, lefts, rights):
    left, right = jnp.concatenate(lefts, axis=1), jnp.concatenate(rights, axis=0)
    acc[...] += jnp.dot(left, right, preferred_element_type=F32)


def inner_body(f, g, edge, ahead, back, hs_edge, ds2_edge, slope_edge, ds1, acc1, acc2, fs, hs, ds2, slope, ht, ft):
    w1, w2, v2 = ahead.at[0], ahead.at[1], back.at[1]
    pairs, cols = f.shape[:2]
    _, _, rim = edge_masks()

    @pl.loop(0, pairs, unroll=True)
    def _(j):
        fs[j] = with_rim(f[j], edge[j]).astype(BF)

    @pl.loop(0, pairs - 1, unroll=True)
    def _(j):
        pre = row_dot(fs[j], fs[j + 1], w1)
        sig = sigmoid(pre)
        act = pre * sig
        slope[j] = sig + act * (1.0 - sig)
        hs[j] = rim_masked(act, rim).astype(BF)
        ht[j] = hs[j, :cols].T

    @pl.loop(0, pairs - 2, unroll=True)
    def _(j):
        pre = row_dot(hs[j], hs[j + 1], w2)
        sig = sigmoid(pre)
        grad = with_rim(g[j + 1], edge[pairs + j + 1])
        delta = grad * (sig + pre * sig * (1.0 - sig))
        store_shifts(delta, ds2, j)

    @pl.loop(0, pairs - 3, unroll=True)
    def _(j):
        value = band_dot((ds2, j), (ds2, j + 1), v2)
        store_shifts(rim_masked(value * slope[j + 1], rim), ds1, j)

    acc1[...] = jnp.zeros_like(acc1)
    acc2[...] = jnp.zeros_like(acc2)

    @pl.loop(0, pairs - 2, unroll=True)
    def _(j):
        both = jnp.concatenate([ht[j], ht[j + 1]], axis=0)
        add_one(acc2, both, [ds2[j, s, :cols] for s in range(3)])

    @pl.loop(1, pairs - 1, unroll=True)
    def _(j):
        ft[j] = f[j].T

    @pl.loop(0, pairs - 3, unroll=True)
    def _(j):
        both = jnp.concatenate([ft[j + 1], ft[j + 2]], axis=0)
        add_one(acc1, both, [ds1[j, s, :cols] for s in range(3)])

    for side, at in ((0, 0), (1, pairs - 2)):
        hs_edge[side] = hs[at]
        slope_edge[side] = slope[at]
    for side, at in ((0, 0), (1, pairs - 3)):
        ds2_edge[side] = ds2[at]


def take_terms(acc1, acc2, mine, other):
    blocks = []
    for ky in range(3):
        for kx in range(3):
            at = (2 - kx) * LANES
            sums = []
            for acc in (acc1, acc2):
                first = acc[ky * HALF : (ky + 1) * HALF, at : at + HALF]
                sums.append(first + acc[(ky + 1) * HALF : (ky + 2) * HALF, at + HALF : at + LANES])
            blocks.append(jnp.concatenate(sums, axis=1))
    half = HALF // 2
    second = lax.axis_index("dp") == 1
    for tap in range(9):
        one, two = blocks[tap][:half], blocks[tap][half:]
        mine[tap * half : (tap + 1) * half] = jnp.where(second, two, one)
        other[tap * half : (tap + 1) * half] = jnp.where(second, one, two)


def half_lanes(side):
    upper = lax.broadcasted_iota(jnp.int32, (1, LANES), 1) >= HALF
    return upper == (side == 1)


def rim_body(
    f, g, edge, above, below, ahead, back, hs_edge, ds2_edge, slope_edge, acc1_in, acc2_in,
    ds1_next, end, row, mine, other, fs, hs, ds2, slope, ds1, acc1, acc2,
):
    pairs, cols = f.shape[:2]
    top, bottom, rim = edge_masks()
    flags = (top, bottom)
    beyond = [half_lanes(side) for side in range(2)]
    w1, w2, v2 = ahead.at[0], ahead.at[1], back.at[1]
    rows = []
    odd = odd_place("row")
    known = jnp.where(odd, top, 0.0), jnp.where(odd, 0.0, bottom)
    halo, mixed, more = ([ref[at].astype(F32) for ref in (above, below)] for at in range(3))
    near, next_near = (0, pairs - 1), (1, pairs - 2)
    sides = range(2)

    def order(side, one, two):
        return (one, two) if side == 0 else (two, one)

    for side in sides:
        fs[side, 0] = jnp.where(beyond[side], more[side], mixed[side]).astype(BF)
        fs[side, 1] = halo[side].astype(BF)
        fs[side, 2] = with_rim(f[near[side]], edge[near[side]]).astype(BF)
    for k in (1, 0):
        for side in sides:
            pre = row_dot(*order(side, fs[side, k], fs[side, k + 1]), w1)
            sig = sigmoid(pre)
            act = pre * sig
            if k == 1:
                slope[side] = sig + act * (1.0 - sig)
            act = act * (flags[side] if k == 0 else jnp.where(beyond[side], flags[side], 1.0))
            hs[side, k] = rim_masked(act, rim).astype(BF)
    for k in (1, 0):
        for side in sides:
            if k == 0:
                grad = pltpu.roll(jnp.where(beyond[side], mixed[side], more[side]), HALF, 1)
            else:
                grad = with_rim(g[near[side]], edge[pairs + near[side]])
            inward = hs[side, 1] if k == 0 else hs_edge[side]
            pre = row_dot(*order(side, hs[side, k], inward), w2)
            sig = sigmoid(pre)
            delta = grad * (sig + pre * sig * (1.0 - sig))
            store_shifts(delta, ds2.at[side], k)
    for k in (1, 0):
        for side in sides:
            inward = (ds2.at[side], 1) if k == 0 else (ds2_edge, side)
            value = band_dot(*order(side, (ds2.at[side], k), inward), v2)
            value = value * (slope[side] if k == 0 else slope_edge[side])
            value = rim_masked(value, rim)
            if k == 0:
                end[side] = jnp.where(beyond[side], value * known[side], value).astype(BF)
                value = jnp.where(beyond[side], 0.0, value)
            store_shifts(value, ds1.at[side], k)
            if k == 1:
                for s in range(3):
                    ds1_next[side, s] = ds1[side, 1, s]
            if k == 0:
                tall = row.shape[0]
                first, second = value[:tall], value[value.shape[0] - tall :]
                if side == 0:
                    first = pltpu.roll(first, HALF, 1)
                else:
                    second = pltpu.roll(second, HALF, 1)
                rows.append(first + second)
    row[...] = jnp.where(odd, rows[1], rows[0]).astype(BF)

    acc1[...] = acc1_in[...]
    acc2[...] = acc2_in[...]
    lefts, rights = [], []
    for side in sides:
        hid = order(side, hs[side, 1, :cols].T, hs_edge[side, :cols].T)
        lefts.append(jnp.concatenate(hid, axis=0))
        rights.append(jnp.concatenate([ds2[side, 1, s, :cols] for s in range(3)], axis=1))
    add_dot(acc2, lefts, rights)
    lefts, rights = [], []
    for side in sides:
        own = f[near[side]].T
        for k in (1, 0):
            feat = order(side, fs[side, 1, :cols].T, own) if k == 0 else order(side, own, f[next_near[side]].T)
            lefts.append(jnp.concatenate(feat, axis=0))
            rights.append(jnp.concatenate([ds1[side, k, s, :cols] for s in range(3)], axis=1))
    add_dot(acc1, lefts, rights)
    take_terms(acc1, acc2, mine, other)


def with_row(center, row, side):
    turned = pltpu.roll(row, HALF, 1)
    first, second = (row, turned) if side == 0 else (turned, row)
    cols = center.shape[0] - row.shape[0]
    full = jnp.concatenate([first[:cols], second], axis=0)
    return center + jnp.where(half_lanes(side), full, 0.0)


def last_body(end, ds1_next, ds1, row, back, gf, done, ends):
    pairs, cols = gf.shape[:2]
    done[...] = jnp.zeros_like(done)
    odd = odd_place("row")
    from_prev = jnp.where(odd, 0.0, row[...].astype(F32))
    from_next = jnp.where(odd, row[...].astype(F32), 0.0)
    store_shifts(with_row(end[0].astype(F32), from_prev, 0), ends, 0)
    store_shifts(with_row(end[1].astype(F32), from_next, 1), ends, 1)
    places = [(ends, 0), (ds1_next, 0)] + [(ds1, j) for j in range(pairs - 3)] + [(ds1_next, 1), (ends, 1)]
    for j in range(pairs):
        gf[j] = band_dot(places[j], places[j + 1], back.at[0])[:cols].astype(BF)


def cost(pair_count):
    return pl.CostEstimate(flops=pair_count * 272 * 768 * 128 * 2, bytes_accessed=4 * 2**20, transcendentals=0)


PARAMS = pltpu.CompilerParams(vmem_limit_bytes=32 * 2**20)


def inner(f, g, edge, ahead, back):
    pairs, cols = f.shape[:2]
    wide = cols + RIM

    def shifts(count):
        return (count, 3, wide, LANES)

    return pl.pallas_call(
        inner_body,
        out_shape=(
            jax.ShapeDtypeStruct((2, wide, LANES), BF),
            jax.ShapeDtypeStruct(shifts(2), BF),
            jax.ShapeDtypeStruct((2, wide, LANES), F32),
            jax.ShapeDtypeStruct(shifts(pairs - 3), BF),
            jax.ShapeDtypeStruct((2 * LANES, 3 * LANES), F32),
            jax.ShapeDtypeStruct((2 * LANES, 3 * LANES), F32),
        ),
        scratch_shapes=[
            pltpu.VMEM((pairs, wide, LANES), BF),
            pltpu.VMEM((pairs - 1, wide, LANES), BF),
            pltpu.VMEM(shifts(pairs - 2), BF),
            pltpu.VMEM((pairs - 1, wide, LANES), F32),
            pltpu.VMEM((pairs - 1, LANES, cols), BF),
            pltpu.VMEM((pairs - 1, LANES, cols), BF),
        ],
        compiler_params=PARAMS,
        cost_estimate=cost(22),
        name="inner",
    )(f, g, edge, ahead, back)


def outer(f, *rest):
    wide = f.shape[1] + RIM

    def shifts(*count):
        return (*count, 3, wide, LANES)

    row = jax.ShapeDtypeStruct((wide // 2 + RIM // 2, LANES), BF)
    return pl.pallas_call(
        rim_body,
        out_shape=(
            jax.ShapeDtypeStruct(shifts(2), BF),
            jax.ShapeDtypeStruct((2, wide, LANES), BF),
            row,
            jax.ShapeDtypeStruct((9 * HALF // 2, LANES), F32),
            jax.ShapeDtypeStruct((9 * HALF // 2, LANES), F32),
        ),
        scratch_shapes=[
            pltpu.VMEM((2, 3, wide, LANES), BF),
            pltpu.VMEM((2, 2, wide, LANES), BF),
            pltpu.VMEM(shifts(2, 2), BF),
            pltpu.VMEM((2, wide, LANES), F32),
            pltpu.VMEM(shifts(2, 2), BF),
            pltpu.VMEM((2 * LANES, 3 * LANES), F32),
            pltpu.VMEM((2 * LANES, 3 * LANES), F32),
        ],
        compiler_params=PARAMS,
        cost_estimate=cost(14),
        name="outer",
    )(f, *rest)


def last(end, ds1_next, ds1, row, back, cols):
    pairs = ds1.shape[0] + 3
    return pl.pallas_call(
        last_body,
        out_shape=(
            jax.ShapeDtypeStruct((pairs, cols, LANES), BF),
            jax.ShapeDtypeStruct((8, LANES), F32),
        ),
        scratch_shapes=[pltpu.VMEM((2, 3, cols + RIM, LANES), BF)],
        compiler_params=PARAMS,
        cost_estimate=cost(8),
        name="last",
    )(end, ds1_next, ds1, row, back)


def four_body(own, one, two, three, done, out):
    low = [ref[...].astype(F32) for ref in (own, one, two, three)]
    out[...] = (low[0] + low[1]) + (low[2] + low[3])


def sum_four(own, got, done):
    return pl.pallas_call(
        four_body,
        out_shape=jax.ShapeDtypeStruct(own.shape, F32),
        compiler_params=pltpu.CompilerParams(vmem_limit_bytes=4 * 2**20),
        name="sum_four",
    )(own, *got, done)


def finish_body(part, other, one, two, *, scale):
    half = HALF // 2
    second = lax.axis_index("dp") == 1
    for tap in range(9):
        mine, theirs = (ref[tap * half : (tap + 1) * half] for ref in (part, other))
        rows = [jnp.where(second, theirs, mine), jnp.where(second, mine, theirs)]
        both = jnp.concatenate(rows, axis=0).T * scale
        one[tap // 3, tap % 3] = both[:HALF]
        two[tap // 3, tap % 3] = both[HALF:]


def finish(part, other, scale):
    shape = jax.ShapeDtypeStruct((3, 3, HALF, HALF), F32)
    return pl.pallas_call(
        functools.partial(finish_body, scale=scale),
        out_shape=(shape, shape),
        compiler_params=pltpu.CompilerParams(vmem_limit_bytes=4 * 2**20),
        name="finish",
    )(part, other)


def reduced(mine, other, done):
    sizes = [lax.axis_size(axis) for axis in AXES]
    swap_cores = [(0, 1), (1, 0)]
    if sizes[0] != 2 or any(size & (size - 1) for size in sizes):
        first = lax.axis_index("dp") == 0
        both = lax.psum([jnp.where(first, mine, other), jnp.where(first, other, mine)], AXES)
        return jnp.where(first, *both), jnp.where(first, both[1], both[0])
    part = mine + lax.ppermute(other, "dp", swap_cores)
    across = [(0, 1 << b) for b in range(sizes[2].bit_length() - 1)]
    down = [(1 << b, 0) for b in range(sizes[1].bit_length() - 1)]
    bits = []
    while across or down:
        bits += down[:1] + across[:1]
        down, across = down[1:], across[1:]
    groups = [bits[at : at + 2] for at in range(0, len(bits), 2)]
    for at in range(len(groups)):
        mine = [groups[at], groups[(at + len(groups) // 2) % len(groups)]]
        if len(mine[0]) != len(mine[1]):
            mine[1] = mine[0]
        mine.reverse()
        low = part.astype(BF)
        got = []
        for member in range(1, 1 << len(mine[0])):
            perm = []
            for core in range(2):
                flips = [flip for k, flip in enumerate(mine[core]) if member >> k & 1]
                for r in range(sizes[1]):
                    for c in range(sizes[2]):
                        to_r, to_c = r, c
                        for flip in flips:
                            to_r, to_c = to_r ^ flip[0], to_c ^ flip[1]
                        base = core * sizes[1]
                        perm.append(((base + r) * sizes[2] + c, (base + to_r) * sizes[2] + to_c))
            got.append(lax.ppermute(low, AXES, perm))
        if at == 1 and len(got) > 1:
            part = sum_four(low, got, done)
            continue
        got = [one.astype(F32) for one in got]
        part = low.astype(F32) + got[0]
        if len(got) > 1:
            part = part + (got[1] + got[2])
    return part, lax.ppermute(part, "dp", swap_cores)


def shards(features, grad_out, kernel_one, kernel_two):
    slides, chans, rows, cols = features.shape
    pairs = rows // 2
    feat, grad = to_pairs(features), to_pairs(grad_out)
    def turn(low, high, is_lower):
        return turn_edges(jnp.where(is_lower, high, low))

    both = jnp.concatenate([features, grad_out], axis=2)
    from_left, from_right = swap(both[..., : RIM // 2], both[..., cols - RIM // 2 :], "col", turn)
    edge = jnp.concatenate([from_right, from_left], axis=1)
    ahead, back, own_near, own_far = prep(feat, grad, kernel_one, kernel_two)
    sent_near, sent_far = frame(own_near, own_far, edge)
    got_near = lax.ppermute(sent_near, "row", neighbours("row", 0))
    got_far = lax.ppermute(sent_far, "row", neighbours("row", 1))
    odd = is_low("row", 1)
    one, more = got_near[:2], got_near[2:]
    above = jnp.concatenate([jnp.where(odd, one, got_far), jnp.where(odd, more, jnp.zeros_like(more))])
    below = jnp.concatenate([jnp.where(odd, got_far, one), jnp.where(odd, jnp.zeros_like(more), more)])
    hs_edge, ds2_edge, slope_edge, ds1, acc1, acc2 = inner(feat, grad, edge, ahead, back)
    ds1_next, end, row, mine, other = outer(
        feat, grad, edge, above, below, ahead, back, hs_edge, ds2_edge, slope_edge, acc1, acc2
    )
    row = lax.ppermute(row, "row", neighbours("row", 1))
    gf, done = last(end, ds1_next, ds1, row, back, cols)
    part, other = reduced(mine, other, done)
    count = slides * lax.axis_size("dp") * rows * lax.axis_size("row") * cols * lax.axis_size("col")
    grad_one, grad_two = finish(part, other, float(count) ** -0.5)
    return from_pairs(gf), grad_one, grad_two


def solution(mesh):
    return jax.shard_map(
        shards,
        mesh=mesh,
        in_specs=(P("dp", None, "row", "col"), P("dp", None, "row", "col"), P(), P()),
        out_specs=(P("dp", None, "row", "col"), P(), P()),
        check_vma=False,
    )
```

```python
import functools

import jax
import jax.numpy as jnp
from jax import lax
from jax.experimental import pallas as pl
from jax.experimental.pallas import tpu as pltpu
from jax.sharding import PartitionSpec as P

BF = jnp.bfloat16
F32 = jnp.float32
AXES = ("dp", "row", "col")
LANES = 128
HALF = LANES // 2
RIM = 16


def neighbours(axis, parity):
    count = lax.axis_size(axis)
    pairs = []
    for i in range(parity, count - 1, 2):
        pairs += [(i, i + 1), (i + 1, i)]
    return pairs


def is_low(axis, parity):
    return lax.axis_index(axis) % 2 == parity


def swap(low, high, axis, turn):
    got = []
    for parity in range(2):
        perm = neighbours(axis, parity)
        if perm:
            got.append(lax.ppermute(turn(low, high, is_low(axis, parity)), axis, perm))
        else:
            got.append(jnp.zeros_like(got[0]))
    odd = is_low(axis, 1)
    return jnp.where(odd, got[0], got[1]), jnp.where(odd, got[1], got[0])


def odd_place(axis):
    return lax.rem(lax.axis_index(axis), 2) == 1


def to_pairs(cells):
    _, chans, rows, cols = cells.shape
    part = cells[0].reshape(chans, rows // 2, 2, cols)
    return part.transpose(1, 3, 2, 0).reshape(rows // 2, cols, 2 * chans)


def edges_body(*refs):
    out = refs[-1]
    at = 0
    for cells in refs[:-1]:
        turned = jnp.swapaxes(cells[0], 0, 1)
        for pair in range(turned.shape[0] // 2):
            out[at] = turned[2 * pair : 2 * pair + 2].reshape(2 * turned.shape[1], -1).T
            at += 1


def turn_edges(*parts):
    pairs = sum(part.shape[2] // 2 for part in parts)
    return pl.pallas_call(
        edges_body,
        out_shape=jax.ShapeDtypeStruct((pairs, parts[0].shape[3], LANES), BF),
        compiler_params=pltpu.CompilerParams(vmem_limit_bytes=8 * 2**20),
        name="edges",
    )(*parts)


def from_pairs(pairs):
    count, cols, lanes = pairs.shape
    part = pairs.reshape(count, cols, 2, lanes // 2)
    return part.transpose(3, 0, 2, 1).reshape(1, lanes // 2, 2 * count, cols)


def make_weights(k1, k2, ahead, back):
    zero = jnp.zeros((HALF, HALF), BF)
    for layer, taps in enumerate((k1, k2)):
        flat = {(ky, kx): taps[ky, kx] for ky in range(3) for kx in range(3)}
        turned = {at: flat[at].astype(F32).T.astype(BF) for at in flat}
        for p in range(2):
            for r in range(2):
                kys = [2 * p + r - a for a in range(2)]
                at = (p * 2 + r) * HALF
                for kx in range(3):
                    ahead[layer, at : at + HALF, kx * LANES : (kx + 1) * LANES] = jnp.concatenate(
                        [turned.get((ky, kx), zero) for ky in kys], axis=1
                    )
                    if layer == 1:
                        ahead[2, at : at + HALF, kx * LANES : (kx + 1) * LANES] = jnp.concatenate(
                            [flat.get((2 - ky, 2 - kx), zero) for ky in kys], axis=1
                        )
                    to = ((p * 3 + kx) * 2 + r) * HALF
                    back[layer, to : to + HALF] = jnp.concatenate(
                        [flat.get((2 - ky, 2 - kx), zero) for ky in kys], axis=1
                    )


def outer_units(feats, grads, high):
    pairs = feats.shape[0]
    near = jnp.where(high, pairs - 1, 0)
    then = feats[jnp.where(high, pairs - 2, 1)].astype(F32)
    grad = pltpu.roll(grads[near].astype(F32), HALF, 1)
    lane = lax.broadcasted_iota(jnp.int32, then.shape, 1)
    own = (lane >= HALF).astype(jnp.int32) == jnp.where(high, 1, 0)
    return feats[near], jnp.where(own, then, grad).astype(BF), jnp.where(own, grad, then).astype(BF)


def prep_body(f, g, k1, k2, ahead, back, sent_near, sent_far):
    make_weights(k1, k2, ahead, back)
    odd = odd_place("row")
    for sent, high in ((sent_near, jnp.logical_not(odd)), (sent_far, odd)):
        units = outer_units(f, g, high)
        for at in range(sent.shape[0]):
            sent[at] = units[at]


def prep(feat, grad, kernel_one, kernel_two):
    weights = [jax.ShapeDtypeStruct(shape, BF) for shape in ((3, 4 * HALF, 3 * LANES), (2, 12 * HALF, LANES))]
    sent = [jax.ShapeDtypeStruct((units, *feat.shape[1:]), BF) for units in (3, 2)]
    return pl.pallas_call(
        prep_body,
        out_shape=(*weights, *sent),
        compiler_params=pltpu.CompilerParams(vmem_limit_bytes=12 * 2**20),
        cost_estimate=cost(2),
        name="prep",
    )(feat, grad, kernel_one, kernel_two)


def frame_body(own_near, own_far, edge, sent_near, sent_far):
    pairs, cols = edge.shape[0] // 2, own_near.shape[1]
    odd = odd_place("row")
    feats, grads = edge.at[:pairs], edge.at[pairs:]
    for own, sent, high in ((own_near, sent_near, jnp.logical_not(odd)), (own_far, sent_far, odd)):
        units = outer_units(feats, grads, high)
        for at in range(sent.shape[0]):
            sent[at, :cols] = own[at]
            sent[at, cols:] = units[at]


def frame(own_near, own_far, edge):
    wide = own_near.shape[1] + RIM
    return pl.pallas_call(
        frame_body,
        out_shape=[jax.ShapeDtypeStruct((own.shape[0], wide, LANES), BF) for own in (own_near, own_far)],
        compiler_params=pltpu.CompilerParams(vmem_limit_bytes=8 * 2**20),
        name="frame",
    )(own_near, own_far, edge)


def sigmoid(value):
    return 0.5 * jnp.tanh(0.5 * value) + 0.5


def with_rim(own, rim):
    return jnp.concatenate([own.astype(F32), rim.astype(F32)], axis=0)


def store_shifts(value, out, index):
    out[index, 0] = pltpu.roll(value, 1, 0).astype(BF)
    out[index, 1] = value.astype(BF)
    out[index, 2] = pltpu.roll(value, value.shape[0] - 1, 0).astype(BF)


def band_dot(first, second, weight):
    parts = [ref[index, s] for ref, index in (first, second) for s in range(3)]
    return jnp.dot(jnp.concatenate(parts, axis=1), weight[...], preferred_element_type=F32)


def row_dot(first, second, weight):
    three = jnp.dot(jnp.concatenate([first, second], axis=1), weight[...], preferred_element_type=F32)
    left = pltpu.roll(three[:, :LANES], 1, 0)
    right = pltpu.roll(three[:, 2 * LANES :], three.shape[0] - 1, 0)
    return left + three[:, LANES : 2 * LANES] + right


def edge_masks():
    row, col = lax.axis_index("row"), lax.axis_index("col")
    top = (row > 0).astype(F32)
    bottom = (row < lax.axis_size("row") - 1).astype(F32)
    left = (col > 0).astype(F32)
    right = (col < lax.axis_size("col") - 1).astype(F32)
    place = lax.broadcasted_iota(jnp.int32, (RIM, LANES), 0)
    rim = jnp.where(place < RIM // 2, right, left)
    return top, bottom, rim


def rim_masked(value, rim):
    own = value.shape[0] - RIM
    return jnp.concatenate([value[:own], value[own:] * rim], axis=0)


def add_one(acc, feat_t, pieces):
    near = jnp.concatenate(pieces, axis=1)
    acc[...] += jnp.dot(feat_t, near, preferred_element_type=F32)


def add_dot(acc, lefts, rights):
    left, right = jnp.concatenate(lefts, axis=1), jnp.concatenate(rights, axis=0)
    acc[...] += jnp.dot(left, right, preferred_element_type=F32)


def inner_body(f, g, edge, ahead, back, hs_edge, ds2_edge, slope_edge, ds1, acc1, acc2, fs, hs, ds2, slope, ht, ft):
    w1, w2, v2 = ahead.at[0], ahead.at[1], back.at[1]
    pairs, cols = f.shape[:2]
    _, _, rim = edge_masks()

    @pl.loop(0, pairs, unroll=True)
    def _(j):
        fs[j] = with_rim(f[j], edge[j]).astype(BF)

    @pl.loop(0, pairs - 1, unroll=True)
    def _(j):
        pre = row_dot(fs[j], fs[j + 1], w1)
        sig = sigmoid(pre)
        act = pre * sig
        slope[j] = sig + act * (1.0 - sig)
        hs[j] = rim_masked(act, rim).astype(BF)
        ht[j] = hs[j, :cols].T

    @pl.loop(0, pairs - 2, unroll=True)
    def _(j):
        pre = row_dot(hs[j], hs[j + 1], w2)
        sig = sigmoid(pre)
        grad = with_rim(g[j + 1], edge[pairs + j + 1])
        delta = grad * (sig + pre * sig * (1.0 - sig))
        store_shifts(delta, ds2, j)

    @pl.loop(0, pairs - 3, unroll=True)
    def _(j):
        value = band_dot((ds2, j), (ds2, j + 1), v2)
        store_shifts(rim_masked(value * slope[j + 1], rim), ds1, j)

    acc1[...] = jnp.zeros_like(acc1)
    acc2[...] = jnp.zeros_like(acc2)

    @pl.loop(0, pairs - 2, unroll=True)
    def _(j):
        both = jnp.concatenate([ht[j], ht[j + 1]], axis=0)
        add_one(acc2, both, [ds2[j, s, :cols] for s in range(3)])

    @pl.loop(1, pairs - 1, unroll=True)
    def _(j):
        ft[j] = f[j].T

    @pl.loop(0, pairs - 3, unroll=True)
    def _(j):
        both = jnp.concatenate([ft[j + 1], ft[j + 2]], axis=0)
        add_one(acc1, both, [ds1[j, s, :cols] for s in range(3)])

    for side, at in ((0, 0), (1, pairs - 2)):
        hs_edge[side] = hs[at]
        slope_edge[side] = slope[at]
    for side, at in ((0, 0), (1, pairs - 3)):
        ds2_edge[side] = ds2[at]


def take_terms(acc1, acc2, mine, other):
    blocks = []
    for ky in range(3):
        for kx in range(3):
            at = (2 - kx) * LANES
            sums = []
            for acc in (acc1, acc2):
                first = acc[ky * HALF : (ky + 1) * HALF, at : at + HALF]
                sums.append(first + acc[(ky + 1) * HALF : (ky + 2) * HALF, at + HALF : at + LANES])
            blocks.append(jnp.concatenate(sums, axis=1))
    half = HALF // 2
    second = lax.axis_index("dp") == 1
    for tap in range(9):
        one, two = blocks[tap][:half], blocks[tap][half:]
        mine[tap * half : (tap + 1) * half] = jnp.where(second, two, one)
        other[tap * half : (tap + 1) * half] = jnp.where(second, one, two)


def half_lanes(side):
    upper = lax.broadcasted_iota(jnp.int32, (1, LANES), 1) >= HALF
    return upper == (side == 1)


def rim_body(
    f, g, edge, above, below, ahead, back, hs_edge, ds2_edge, slope_edge, acc1_in, acc2_in,
    ds1_next, end, row, mine, other, fs, hs, ds2, slope, ds1, acc1, acc2,
):
    pairs, cols = f.shape[:2]
    top, bottom, rim = edge_masks()
    flags = (top, bottom)
    beyond = [half_lanes(side) for side in range(2)]
    w1, w2, v2 = ahead.at[0], ahead.at[1], ahead.at[2]
    rows = []
    odd = odd_place("row")
    known = jnp.where(odd, top, 0.0), jnp.where(odd, 0.0, bottom)
    halo, mixed, more = ([ref[at].astype(F32) for ref in (above, below)] for at in range(3))
    near, next_near = (0, pairs - 1), (1, pairs - 2)
    sides = range(2)

    def order(side, one, two):
        return (one, two) if side == 0 else (two, one)

    for side in sides:
        fs[side, 0] = jnp.where(beyond[side], more[side], mixed[side]).astype(BF)
        fs[side, 1] = halo[side].astype(BF)
        fs[side, 2] = with_rim(f[near[side]], edge[near[side]]).astype(BF)
    for k in (1, 0):
        for side in sides:
            pre = row_dot(*order(side, fs[side, k], fs[side, k + 1]), w1)
            sig = sigmoid(pre)
            act = pre * sig
            if k == 1:
                slope[side] = sig + act * (1.0 - sig)
            act = act * (flags[side] if k == 0 else jnp.where(beyond[side], flags[side], 1.0))
            hs[side, k] = rim_masked(act, rim).astype(BF)
    for k in (1, 0):
        for side in sides:
            if k == 0:
                grad = pltpu.roll(jnp.where(beyond[side], mixed[side], more[side]), HALF, 1)
            else:
                grad = with_rim(g[near[side]], edge[pairs + near[side]])
            inward = hs[side, 1] if k == 0 else hs_edge[side]
            pre = row_dot(*order(side, hs[side, k], inward), w2)
            sig = sigmoid(pre)
            delta = grad * (sig + pre * sig * (1.0 - sig))
            if k == 1:
                store_shifts(delta, ds2.at[side], k)
            else:
                ds2[side, 0, 1] = delta.astype(BF)
    for k in (1, 0):
        for side in sides:
            inward = ds2[side, 1, 1] if k == 0 else ds2_edge[side, 1]
            value = row_dot(*order(side, ds2[side, k, 1], inward), v2)
            value = value * (slope[side] if k == 0 else slope_edge[side])
            value = rim_masked(value, rim)
            if k == 0:
                end[side] = jnp.where(beyond[side], value * known[side], value).astype(BF)
                value = jnp.where(beyond[side], 0.0, value)
            store_shifts(value, ds1.at[side], k)
            if k == 1:
                for s in range(3):
                    ds1_next[side, s] = ds1[side, 1, s]
            if k == 0:
                tall = row.shape[0]
                first, second = value[:tall], value[value.shape[0] - tall :]
                if side == 0:
                    first = pltpu.roll(first, HALF, 1)
                else:
                    second = pltpu.roll(second, HALF, 1)
                rows.append(first + second)
    row[...] = jnp.where(odd, rows[1], rows[0]).astype(BF)

    acc1[...] = acc1_in[...]
    acc2[...] = acc2_in[...]
    lefts, rights = [], []
    for side in sides:
        hid = order(side, hs[side, 1, :cols].T, hs_edge[side, :cols].T)
        lefts.append(jnp.concatenate(hid, axis=0))
        rights.append(jnp.concatenate([ds2[side, 1, s, :cols] for s in range(3)], axis=1))
    add_dot(acc2, lefts, rights)
    lefts, rights = [], []
    for side in sides:
        own = f[near[side]].T
        for k in (1, 0):
            feat = order(side, fs[side, 1, :cols].T, own) if k == 0 else order(side, own, f[next_near[side]].T)
            lefts.append(jnp.concatenate(feat, axis=0))
            rights.append(jnp.concatenate([ds1[side, k, s, :cols] for s in range(3)], axis=1))
    add_dot(acc1, lefts, rights)
    take_terms(acc1, acc2, mine, other)


def with_row(center, row, side):
    turned = pltpu.roll(row, HALF, 1)
    first, second = (row, turned) if side == 0 else (turned, row)
    cols = center.shape[0] - row.shape[0]
    full = jnp.concatenate([first[:cols], second], axis=0)
    return center + jnp.where(half_lanes(side), full, 0.0)


def last_body(end, ds1_next, ds1, row, back, gf, done, ends):
    pairs, cols = gf.shape[:2]
    done[...] = jnp.zeros_like(done)
    odd = odd_place("row")
    from_prev = jnp.where(odd, 0.0, row[...].astype(F32))
    from_next = jnp.where(odd, row[...].astype(F32), 0.0)
    store_shifts(with_row(end[0].astype(F32), from_prev, 0), ends, 0)
    store_shifts(with_row(end[1].astype(F32), from_next, 1), ends, 1)
    places = [(ends, 0), (ds1_next, 0)] + [(ds1, j) for j in range(pairs - 3)] + [(ds1_next, 1), (ends, 1)]
    for j in range(pairs):
        gf[j] = band_dot(places[j], places[j + 1], back.at[0])[:cols].astype(BF)


def cost(pair_count):
    return pl.CostEstimate(flops=pair_count * 272 * 768 * 128 * 2, bytes_accessed=4 * 2**20, transcendentals=0)


PARAMS = pltpu.CompilerParams(vmem_limit_bytes=32 * 2**20)


def inner(f, g, edge, ahead, back):
    pairs, cols = f.shape[:2]
    wide = cols + RIM

    def shifts(count):
        return (count, 3, wide, LANES)

    return pl.pallas_call(
        inner_body,
        out_shape=(
            jax.ShapeDtypeStruct((2, wide, LANES), BF),
            jax.ShapeDtypeStruct(shifts(2), BF),
            jax.ShapeDtypeStruct((2, wide, LANES), F32),
            jax.ShapeDtypeStruct(shifts(pairs - 3), BF),
            jax.ShapeDtypeStruct((2 * LANES, 3 * LANES), F32),
            jax.ShapeDtypeStruct((2 * LANES, 3 * LANES), F32),
        ),
        scratch_shapes=[
            pltpu.VMEM((pairs, wide, LANES), BF),
            pltpu.VMEM((pairs - 1, wide, LANES), BF),
            pltpu.VMEM(shifts(pairs - 2), BF),
            pltpu.VMEM((pairs - 1, wide, LANES), F32),
            pltpu.VMEM((pairs - 1, LANES, cols), BF),
            pltpu.VMEM((pairs - 1, LANES, cols), BF),
        ],
        compiler_params=PARAMS,
        cost_estimate=cost(22),
        name="inner",
    )(f, g, edge, ahead, back)


def outer(f, *rest):
    wide = f.shape[1] + RIM

    def shifts(*count):
        return (*count, 3, wide, LANES)

    row = jax.ShapeDtypeStruct((wide // 2 + RIM // 2, LANES), BF)
    return pl.pallas_call(
        rim_body,
        out_shape=(
            jax.ShapeDtypeStruct(shifts(2), BF),
            jax.ShapeDtypeStruct((2, wide, LANES), BF),
            row,
            jax.ShapeDtypeStruct((9 * HALF // 2, LANES), F32),
            jax.ShapeDtypeStruct((9 * HALF // 2, LANES), F32),
        ),
        scratch_shapes=[
            pltpu.VMEM((2, 3, wide, LANES), BF),
            pltpu.VMEM((2, 2, wide, LANES), BF),
            pltpu.VMEM(shifts(2, 2), BF),
            pltpu.VMEM((2, wide, LANES), F32),
            pltpu.VMEM(shifts(2, 2), BF),
            pltpu.VMEM((2 * LANES, 3 * LANES), F32),
            pltpu.VMEM((2 * LANES, 3 * LANES), F32),
        ],
        compiler_params=PARAMS,
        cost_estimate=cost(14),
        name="outer",
    )(f, *rest)


def last(end, ds1_next, ds1, row, back, cols):
    pairs = ds1.shape[0] + 3
    return pl.pallas_call(
        last_body,
        out_shape=(
            jax.ShapeDtypeStruct((pairs, cols, LANES), BF),
            jax.ShapeDtypeStruct((8, LANES), F32),
        ),
        scratch_shapes=[pltpu.VMEM((2, 3, cols + RIM, LANES), BF)],
        compiler_params=PARAMS,
        cost_estimate=cost(8),
        name="last",
    )(end, ds1_next, ds1, row, back)


def four_body(own, one, two, three, done, out):
    low = [ref[...].astype(F32) for ref in (own, one, two, three)]
    out[...] = (low[0] + low[1]) + (low[2] + low[3])


def sum_four(own, got, done):
    return pl.pallas_call(
        four_body,
        out_shape=jax.ShapeDtypeStruct(own.shape, F32),
        compiler_params=pltpu.CompilerParams(vmem_limit_bytes=4 * 2**20),
        name="sum_four",
    )(own, *got, done)


def finish_body(part, other, one, two, *, scale):
    half = HALF // 2
    second = lax.axis_index("dp") == 1
    for tap in range(9):
        mine, theirs = (ref[tap * half : (tap + 1) * half] for ref in (part, other))
        rows = [jnp.where(second, theirs, mine), jnp.where(second, mine, theirs)]
        both = jnp.concatenate(rows, axis=0).T * scale
        one[tap // 3, tap % 3] = both[:HALF]
        two[tap // 3, tap % 3] = both[HALF:]


def finish(part, other, scale):
    shape = jax.ShapeDtypeStruct((3, 3, HALF, HALF), F32)
    return pl.pallas_call(
        functools.partial(finish_body, scale=scale),
        out_shape=(shape, shape),
        compiler_params=pltpu.CompilerParams(vmem_limit_bytes=4 * 2**20),
        name="finish",
    )(part, other)


def reduced(mine, other, done):
    sizes = [lax.axis_size(axis) for axis in AXES]
    swap_cores = [(0, 1), (1, 0)]
    if sizes[0] != 2 or any(size & (size - 1) for size in sizes):
        first = lax.axis_index("dp") == 0
        both = lax.psum([jnp.where(first, mine, other), jnp.where(first, other, mine)], AXES)
        return jnp.where(first, *both), jnp.where(first, both[1], both[0])
    part = mine + lax.ppermute(other, "dp", swap_cores)
    across = [(0, 1 << b) for b in range(sizes[2].bit_length() - 1)]
    down = [(1 << b, 0) for b in range(sizes[1].bit_length() - 1)]
    bits = []
    while across or down:
        bits += down[:1] + across[:1]
        down, across = down[1:], across[1:]
    groups = [bits[at : at + 2] for at in range(0, len(bits), 2)]
    for at in range(len(groups)):
        mine = [groups[at], groups[(at + len(groups) // 2) % len(groups)]]
        if len(mine[0]) != len(mine[1]):
            mine[1] = mine[0]
        mine.reverse()
        low = part.astype(BF)
        got = []
        for member in range(1, 1 << len(mine[0])):
            perm = []
            for core in range(2):
                flips = [flip for k, flip in enumerate(mine[core]) if member >> k & 1]
                for r in range(sizes[1]):
                    for c in range(sizes[2]):
                        to_r, to_c = r, c
                        for flip in flips:
                            to_r, to_c = to_r ^ flip[0], to_c ^ flip[1]
                        base = core * sizes[1]
                        perm.append(((base + r) * sizes[2] + c, (base + to_r) * sizes[2] + to_c))
            got.append(lax.ppermute(low, AXES, perm))
        if at == 1 and len(got) > 1:
            part = sum_four(low, got, done)
            continue
        got = [one.astype(F32) for one in got]
        part = low.astype(F32) + got[0]
        if len(got) > 1:
            part = part + (got[1] + got[2])
    return part, lax.ppermute(part, "dp", swap_cores)


def shards(features, grad_out, kernel_one, kernel_two):
    slides, chans, rows, cols = features.shape
    pairs = rows // 2
    feat, grad = to_pairs(features), to_pairs(grad_out)
    def turn(low, high, is_lower):
        return turn_edges(jnp.where(is_lower, high, low))

    both = jnp.concatenate([features, grad_out], axis=2)
    from_left, from_right = swap(both[..., : RIM // 2], both[..., cols - RIM // 2 :], "col", turn)
    edge = jnp.concatenate([from_right, from_left], axis=1)
    ahead, back, own_near, own_far = prep(feat, grad, kernel_one, kernel_two)
    sent_near, sent_far = frame(own_near, own_far, edge)
    got_near = lax.ppermute(sent_near, "row", neighbours("row", 0))
    got_far = lax.ppermute(sent_far, "row", neighbours("row", 1))
    odd = is_low("row", 1)
    one, more = got_near[:2], got_near[2:]
    above = jnp.concatenate([jnp.where(odd, one, got_far), jnp.where(odd, more, jnp.zeros_like(more))])
    below = jnp.concatenate([jnp.where(odd, got_far, one), jnp.where(odd, jnp.zeros_like(more), more)])
    hs_edge, ds2_edge, slope_edge, ds1, acc1, acc2 = inner(feat, grad, edge, ahead, back)
    ds1_next, end, row, mine, other = outer(
        feat, grad, edge, above, below, ahead, back, hs_edge, ds2_edge, slope_edge, acc1, acc2
    )
    row = lax.ppermute(row, "row", neighbours("row", 1))
    gf, done = last(end, ds1_next, ds1, row, back, cols)
    part, other = reduced(mine, other, done)
    count = slides * lax.axis_size("dp") * rows * lax.axis_size("row") * cols * lax.axis_size("col")
    grad_one, grad_two = finish(part, other, float(count) ** -0.5)
    return from_pairs(gf), grad_one, grad_two


def solution(mesh):
    return jax.shard_map(
        shards,
        mesh=mesh,
        in_specs=(P("dp", None, "row", "col"), P("dp", None, "row", "col"), P(), P()),
        out_specs=(P("dp", None, "row", "col"), P(), P()),
        check_vma=False,
    )
```

```python
import functools

import jax
import jax.numpy as jnp
from jax import lax
from jax.experimental import pallas as pl
from jax.experimental.pallas import tpu as pltpu
from jax.sharding import PartitionSpec as P

BF = jnp.bfloat16
F32 = jnp.float32
AXES = ("dp", "row", "col")
LANES = 128
HALF = LANES // 2
RIM = 16


def neighbours(axis, parity):
    count = lax.axis_size(axis)
    pairs = []
    for i in range(parity, count - 1, 2):
        pairs += [(i, i + 1), (i + 1, i)]
    return pairs


def is_low(axis, parity):
    return lax.axis_index(axis) % 2 == parity


def swap(low, high, axis, turn):
    got = []
    for parity in range(2):
        perm = neighbours(axis, parity)
        if perm:
            got.append(lax.ppermute(turn(low, high, is_low(axis, parity)), axis, perm))
        else:
            got.append(jnp.zeros_like(got[0]))
    odd = is_low(axis, 1)
    return jnp.where(odd, got[0], got[1]), jnp.where(odd, got[1], got[0])


def odd_place(axis):
    return lax.rem(lax.axis_index(axis), 2) == 1


def to_pairs(cells):
    _, chans, rows, cols = cells.shape
    part = cells[0].reshape(chans, rows // 2, 2, cols)
    return part.transpose(1, 3, 2, 0).reshape(rows // 2, cols, 2 * chans)


def edges_body(*refs):
    out = refs[-1]
    at = 0
    for cells in refs[:-1]:
        turned = jnp.swapaxes(cells[0], 0, 1)
        for pair in range(turned.shape[0] // 2):
            out[at] = turned[2 * pair : 2 * pair + 2].reshape(2 * turned.shape[1], -1).T
            at += 1


def turn_edges(*parts):
    pairs = sum(part.shape[2] // 2 for part in parts)
    return pl.pallas_call(
        edges_body,
        out_shape=jax.ShapeDtypeStruct((pairs, parts[0].shape[3], LANES), BF),
        compiler_params=pltpu.CompilerParams(vmem_limit_bytes=8 * 2**20),
        name="edges",
    )(*parts)


def from_pairs(pairs):
    count, cols, lanes = pairs.shape
    part = pairs.reshape(count, cols, 2, lanes // 2)
    return part.transpose(3, 0, 2, 1).reshape(1, lanes // 2, 2 * count, cols)


def make_weights(k1, k2, ahead, back):
    zero = jnp.zeros((HALF, HALF), BF)
    for layer, taps in enumerate((k1, k2)):
        flat = {(ky, kx): taps[ky, kx] for ky in range(3) for kx in range(3)}
        turned = {at: flat[at].astype(F32).T.astype(BF) for at in flat}
        for p in range(2):
            for r in range(2):
                kys = [2 * p + r - a for a in range(2)]
                at = (p * 2 + r) * HALF
                for kx in range(3):
                    ahead[layer, at : at + HALF, kx * LANES : (kx + 1) * LANES] = jnp.concatenate(
                        [turned.get((ky, kx), zero) for ky in kys], axis=1
                    )
                    if layer == 1:
                        ahead[2, at : at + HALF, kx * LANES : (kx + 1) * LANES] = jnp.concatenate(
                            [flat.get((2 - ky, 2 - kx), zero) for ky in kys], axis=1
                        )
                    to = ((p * 3 + kx) * 2 + r) * HALF
                    back[layer, to : to + HALF] = jnp.concatenate(
                        [flat.get((2 - ky, 2 - kx), zero) for ky in kys], axis=1
                    )


def outer_units(feats, grads, high):
    pairs = feats.shape[0]
    near = jnp.where(high, pairs - 1, 0)
    then = feats[jnp.where(high, pairs - 2, 1)].astype(F32)
    grad = pltpu.roll(grads[near].astype(F32), HALF, 1)
    lane = lax.broadcasted_iota(jnp.int32, then.shape, 1)
    own = (lane >= HALF).astype(jnp.int32) == jnp.where(high, 1, 0)
    return feats[near], jnp.where(own, then, grad).astype(BF), jnp.where(own, grad, then).astype(BF)


def prep_body(f, g, k1, k2, ahead, back, sent_near, sent_far):
    make_weights(k1, k2, ahead, back)
    odd = odd_place("row")
    for sent, high in ((sent_near, jnp.logical_not(odd)), (sent_far, odd)):
        units = outer_units(f, g, high)
        for at in range(sent.shape[0]):
            sent[at] = units[at]


def prep(feat, grad, kernel_one, kernel_two):
    weights = [jax.ShapeDtypeStruct(shape, BF) for shape in ((3, 4 * HALF, 3 * LANES), (2, 12 * HALF, LANES))]
    sent = [jax.ShapeDtypeStruct((units, *feat.shape[1:]), BF) for units in (3, 2)]
    return pl.pallas_call(
        prep_body,
        out_shape=(*weights, *sent),
        compiler_params=pltpu.CompilerParams(vmem_limit_bytes=12 * 2**20),
        cost_estimate=cost(2),
        name="prep",
    )(feat, grad, kernel_one, kernel_two)


def frame_body(own_near, own_far, edge, sent_near, sent_far):
    pairs, cols = edge.shape[0] // 2, own_near.shape[1]
    odd = odd_place("row")
    feats, grads = edge.at[:pairs], edge.at[pairs:]
    for own, sent, high in ((own_near, sent_near, jnp.logical_not(odd)), (own_far, sent_far, odd)):
        units = outer_units(feats, grads, high)
        for at in range(sent.shape[0]):
            sent[at, :cols] = own[at]
            sent[at, cols:] = units[at]


def frame(own_near, own_far, edge):
    wide = own_near.shape[1] + RIM
    return pl.pallas_call(
        frame_body,
        out_shape=[jax.ShapeDtypeStruct((own.shape[0], wide, LANES), BF) for own in (own_near, own_far)],
        compiler_params=pltpu.CompilerParams(vmem_limit_bytes=8 * 2**20),
        name="frame",
    )(own_near, own_far, edge)


def sigmoid(value):
    return 0.5 * jnp.tanh(0.5 * value) + 0.5


def with_rim(own, rim):
    return jnp.concatenate([own.astype(F32), rim.astype(F32)], axis=0)


def store_shifts(value, out, index):
    out[index, 0] = pltpu.roll(value, 1, 0).astype(BF)
    out[index, 1] = value.astype(BF)
    out[index, 2] = pltpu.roll(value, value.shape[0] - 1, 0).astype(BF)


def band_dot(first, second, weight):
    parts = [ref[index, s] for ref, index in (first, second) for s in range(3)]
    return jnp.dot(jnp.concatenate(parts, axis=1), weight[...], preferred_element_type=F32)


def row_dot(first, second, weight):
    three = jnp.dot(jnp.concatenate([first, second], axis=1), weight[...], preferred_element_type=F32)
    left = pltpu.roll(three[:, :LANES], 1, 0)
    right = pltpu.roll(three[:, 2 * LANES :], three.shape[0] - 1, 0)
    return left + three[:, LANES : 2 * LANES] + right


def edge_masks():
    row, col = lax.axis_index("row"), lax.axis_index("col")
    top = (row > 0).astype(F32)
    bottom = (row < lax.axis_size("row") - 1).astype(F32)
    left = (col > 0).astype(F32)
    right = (col < lax.axis_size("col") - 1).astype(F32)
    place = lax.broadcasted_iota(jnp.int32, (RIM, LANES), 0)
    rim = jnp.where(place < RIM // 2, right, left)
    return top, bottom, rim


def rim_masked(value, rim):
    own = value.shape[0] - RIM
    return jnp.concatenate([value[:own], value[own:] * rim], axis=0)


def add_one(acc, feat_t, pieces):
    near = jnp.concatenate(pieces, axis=1)
    acc[...] += jnp.dot(feat_t, near, preferred_element_type=F32)


def add_dot(acc, lefts, rights):
    left, right = jnp.concatenate(lefts, axis=1), jnp.concatenate(rights, axis=0)
    acc[...] += jnp.dot(left, right, preferred_element_type=F32)


def inner_body(f, g, edge, ahead, back, hs_edge, ds2_edge, slope_edge, ds1, acc1, acc2, fs, hs, ds2, slope, ht, ft):
    w1, w2, v2 = ahead.at[0], ahead.at[1], back.at[1]
    pairs, cols = f.shape[:2]
    _, _, rim = edge_masks()

    @pl.loop(0, pairs, unroll=True)
    def _(j):
        fs[j] = with_rim(f[j], edge[j]).astype(BF)

    @pl.loop(0, pairs - 1, unroll=True)
    def _(j):
        pre = row_dot(fs[j], fs[j + 1], w1)
        sig = sigmoid(pre)
        act = pre * sig
        slope[j] = sig + act * (1.0 - sig)
        hs[j] = rim_masked(act, rim).astype(BF)
        ht[j] = hs[j, :cols].T

    @pl.loop(0, pairs - 2, unroll=True)
    def _(j):
        pre = row_dot(hs[j], hs[j + 1], w2)
        sig = sigmoid(pre)
        grad = with_rim(g[j + 1], edge[pairs + j + 1])
        delta = grad * (sig + pre * sig * (1.0 - sig))
        store_shifts(delta, ds2, j)

    @pl.loop(0, pairs - 3, unroll=True)
    def _(j):
        value = band_dot((ds2, j), (ds2, j + 1), v2)
        store_shifts(rim_masked(value * slope[j + 1], rim), ds1, j)

    acc1[...] = jnp.zeros_like(acc1)
    acc2[...] = jnp.zeros_like(acc2)

    @pl.loop(0, pairs - 2, unroll=True)
    def _(j):
        both = jnp.concatenate([ht[j], ht[j + 1]], axis=0)
        add_one(acc2, both, [ds2[j, s, :cols] for s in range(3)])

    @pl.loop(1, pairs - 1, unroll=True)
    def _(j):
        ft[j] = f[j].T

    @pl.loop(0, pairs - 3, unroll=True)
    def _(j):
        both = jnp.concatenate([ft[j + 1], ft[j + 2]], axis=0)
        add_one(acc1, both, [ds1[j, s, :cols] for s in range(3)])

    for side, at in ((0, 0), (1, pairs - 2)):
        hs_edge[side] = hs[at]
        slope_edge[side] = slope[at]
    for side, at in ((0, 0), (1, pairs - 3)):
        ds2_edge[side] = ds2[at]


def take_terms(acc1, acc2, mine, other):
    blocks = []
    for ky in range(3):
        for kx in range(3):
            at = (2 - kx) * LANES
            sums = []
            for acc in (acc1, acc2):
                first = acc[ky * HALF : (ky + 1) * HALF, at : at + HALF]
                sums.append(first + acc[(ky + 1) * HALF : (ky + 2) * HALF, at + HALF : at + LANES])
            blocks.append(jnp.concatenate(sums, axis=1))
    half = HALF // 2
    second = lax.axis_index("dp") == 1
    for tap in range(9):
        one, two = blocks[tap][:half], blocks[tap][half:]
        mine[tap * half : (tap + 1) * half] = jnp.where(second, two, one)
        other[tap * half : (tap + 1) * half] = jnp.where(second, one, two).astype(BF)


def half_lanes(side):
    upper = lax.broadcasted_iota(jnp.int32, (1, LANES), 1) >= HALF
    return upper == (side == 1)


def rim_body(
    f, g, edge, above, below, ahead, back, hs_edge, ds2_edge, slope_edge, acc1_in, acc2_in,
    ds1_next, end, row, mine, other, fs, hs, ds2, slope, ds1, acc1, acc2,
):
    pairs, cols = f.shape[:2]
    top, bottom, rim = edge_masks()
    flags = (top, bottom)
    beyond = [half_lanes(side) for side in range(2)]
    w1, w2, v2 = ahead.at[0], ahead.at[1], ahead.at[2]
    rows = []
    odd = odd_place("row")
    known = jnp.where(odd, top, 0.0), jnp.where(odd, 0.0, bottom)
    halo, mixed, more = ([ref[at].astype(F32) for ref in (above, below)] for at in range(3))
    near, next_near = (0, pairs - 1), (1, pairs - 2)
    sides = range(2)

    def order(side, one, two):
        return (one, two) if side == 0 else (two, one)

    for side in sides:
        fs[side, 0] = jnp.where(beyond[side], more[side], mixed[side]).astype(BF)
        fs[side, 1] = halo[side].astype(BF)
        fs[side, 2] = with_rim(f[near[side]], edge[near[side]]).astype(BF)
    for k in (1, 0):
        for side in sides:
            pre = row_dot(*order(side, fs[side, k], fs[side, k + 1]), w1)
            sig = sigmoid(pre)
            act = pre * sig
            if k == 1:
                slope[side] = sig + act * (1.0 - sig)
            act = act * (flags[side] if k == 0 else jnp.where(beyond[side], flags[side], 1.0))
            hs[side, k] = rim_masked(act, rim).astype(BF)
    for k in (1, 0):
        for side in sides:
            if k == 0:
                grad = pltpu.roll(jnp.where(beyond[side], mixed[side], more[side]), HALF, 1)
            else:
                grad = with_rim(g[near[side]], edge[pairs + near[side]])
            inward = hs[side, 1] if k == 0 else hs_edge[side]
            pre = row_dot(*order(side, hs[side, k], inward), w2)
            sig = sigmoid(pre)
            delta = grad * (sig + pre * sig * (1.0 - sig))
            if k == 1:
                store_shifts(delta, ds2.at[side], k)
            else:
                ds2[side, 0, 1] = delta.astype(BF)
    for k in (1, 0):
        for side in sides:
            inward = ds2[side, 1, 1] if k == 0 else ds2_edge[side, 1]
            value = row_dot(*order(side, ds2[side, k, 1], inward), v2)
            value = value * (slope[side] if k == 0 else slope_edge[side])
            value = rim_masked(value, rim)
            if k == 0:
                end[side] = jnp.where(beyond[side], value * known[side], value).astype(BF)
                value = jnp.where(beyond[side], 0.0, value)
            store_shifts(value, ds1.at[side], k)
            if k == 1:
                for s in range(3):
                    ds1_next[side, s] = ds1[side, 1, s]
            if k == 0:
                tall = row.shape[0]
                first, second = value[:tall], value[value.shape[0] - tall :]
                if side == 0:
                    first = pltpu.roll(first, HALF, 1)
                else:
                    second = pltpu.roll(second, HALF, 1)
                rows.append(first + second)
    row[...] = jnp.where(odd, rows[1], rows[0]).astype(BF)

    acc1[...] = acc1_in[...]
    acc2[...] = acc2_in[...]
    lefts, rights = [], []
    for side in sides:
        hid = order(side, hs[side, 1, :cols].T, hs_edge[side, :cols].T)
        lefts.append(jnp.concatenate(hid, axis=0))
        rights.append(jnp.concatenate([ds2[side, 1, s, :cols] for s in range(3)], axis=1))
    add_dot(acc2, lefts, rights)
    lefts, rights = [], []
    for side in sides:
        own = f[near[side]].T
        for k in (1, 0):
            feat = order(side, fs[side, 1, :cols].T, own) if k == 0 else order(side, own, f[next_near[side]].T)
            lefts.append(jnp.concatenate(feat, axis=0))
            rights.append(jnp.concatenate([ds1[side, k, s, :cols] for s in range(3)], axis=1))
    add_dot(acc1, lefts, rights)
    take_terms(acc1, acc2, mine, other)


def with_row(center, row, side):
    turned = pltpu.roll(row, HALF, 1)
    first, second = (row, turned) if side == 0 else (turned, row)
    cols = center.shape[0] - row.shape[0]
    full = jnp.concatenate([first[:cols], second], axis=0)
    return center + jnp.where(half_lanes(side), full, 0.0)


def last_body(end, ds1_next, ds1, row, back, gf, done, ends):
    pairs, cols = gf.shape[:2]
    done[...] = jnp.zeros_like(done)
    odd = odd_place("row")
    from_prev = jnp.where(odd, 0.0, row[...].astype(F32))
    from_next = jnp.where(odd, row[...].astype(F32), 0.0)
    store_shifts(with_row(end[0].astype(F32), from_prev, 0), ends, 0)
    store_shifts(with_row(end[1].astype(F32), from_next, 1), ends, 1)
    places = [(ends, 0), (ds1_next, 0)] + [(ds1, j) for j in range(pairs - 3)] + [(ds1_next, 1), (ends, 1)]
    for j in range(pairs):
        gf[j] = band_dot(places[j], places[j + 1], back.at[0])[:cols].astype(BF)


def cost(pair_count):
    return pl.CostEstimate(flops=pair_count * 272 * 768 * 128 * 2, bytes_accessed=4 * 2**20, transcendentals=0)


PARAMS = pltpu.CompilerParams(vmem_limit_bytes=32 * 2**20)


def inner(f, g, edge, ahead, back):
    pairs, cols = f.shape[:2]
    wide = cols + RIM

    def shifts(count):
        return (count, 3, wide, LANES)

    return pl.pallas_call(
        inner_body,
        out_shape=(
            jax.ShapeDtypeStruct((2, wide, LANES), BF),
            jax.ShapeDtypeStruct(shifts(2), BF),
            jax.ShapeDtypeStruct((2, wide, LANES), F32),
            jax.ShapeDtypeStruct(shifts(pairs - 3), BF),
            jax.ShapeDtypeStruct((2 * LANES, 3 * LANES), F32),
            jax.ShapeDtypeStruct((2 * LANES, 3 * LANES), F32),
        ),
        scratch_shapes=[
            pltpu.VMEM((pairs, wide, LANES), BF),
            pltpu.VMEM((pairs - 1, wide, LANES), BF),
            pltpu.VMEM(shifts(pairs - 2), BF),
            pltpu.VMEM((pairs - 1, wide, LANES), F32),
            pltpu.VMEM((pairs - 1, LANES, cols), BF),
            pltpu.VMEM((pairs - 1, LANES, cols), BF),
        ],
        compiler_params=PARAMS,
        cost_estimate=cost(22),
        name="inner",
    )(f, g, edge, ahead, back)


def outer(f, *rest):
    wide = f.shape[1] + RIM

    def shifts(*count):
        return (*count, 3, wide, LANES)

    row = jax.ShapeDtypeStruct((wide // 2 + RIM // 2, LANES), BF)
    return pl.pallas_call(
        rim_body,
        out_shape=(
            jax.ShapeDtypeStruct(shifts(2), BF),
            jax.ShapeDtypeStruct((2, wide, LANES), BF),
            row,
            jax.ShapeDtypeStruct((9 * HALF // 2, LANES), F32),
            jax.ShapeDtypeStruct((9 * HALF // 2, LANES), BF),
        ),
        scratch_shapes=[
            pltpu.VMEM((2, 3, wide, LANES), BF),
            pltpu.VMEM((2, 2, wide, LANES), BF),
            pltpu.VMEM(shifts(2, 2), BF),
            pltpu.VMEM((2, wide, LANES), F32),
            pltpu.VMEM(shifts(2, 2), BF),
            pltpu.VMEM((2 * LANES, 3 * LANES), F32),
            pltpu.VMEM((2 * LANES, 3 * LANES), F32),
        ],
        compiler_params=PARAMS,
        cost_estimate=cost(14),
        name="outer",
    )(f, *rest)


def last(end, ds1_next, ds1, row, back, cols):
    pairs = ds1.shape[0] + 3
    return pl.pallas_call(
        last_body,
        out_shape=(
            jax.ShapeDtypeStruct((pairs, cols, LANES), BF),
            jax.ShapeDtypeStruct((8, LANES), F32),
        ),
        scratch_shapes=[pltpu.VMEM((2, 3, cols + RIM, LANES), BF)],
        compiler_params=PARAMS,
        cost_estimate=cost(8),
        name="last",
    )(end, ds1_next, ds1, row, back)


def four_body(own, one, two, three, done, out):
    low = [ref[...].astype(F32) for ref in (own, one, two, three)]
    out[...] = (low[0] + low[1]) + (low[2] + low[3])


def sum_four(own, got, done):
    return pl.pallas_call(
        four_body,
        out_shape=jax.ShapeDtypeStruct(own.shape, F32),
        compiler_params=pltpu.CompilerParams(vmem_limit_bytes=4 * 2**20),
        name="sum_four",
    )(own, *got, done)


def finish_body(part, other, one, two, *, scale):
    half = HALF // 2
    second = lax.axis_index("dp") == 1
    for tap in range(9):
        mine, theirs = (ref[tap * half : (tap + 1) * half] for ref in (part, other))
        rows = [jnp.where(second, theirs, mine), jnp.where(second, mine, theirs)]
        both = jnp.concatenate(rows, axis=0).T * scale
        one[tap // 3, tap % 3] = both[:HALF]
        two[tap // 3, tap % 3] = both[HALF:]


def finish(part, other, scale):
    shape = jax.ShapeDtypeStruct((3, 3, HALF, HALF), F32)
    return pl.pallas_call(
        functools.partial(finish_body, scale=scale),
        out_shape=(shape, shape),
        compiler_params=pltpu.CompilerParams(vmem_limit_bytes=4 * 2**20),
        name="finish",
    )(part, other)


def reduced(mine, other, done):
    sizes = [lax.axis_size(axis) for axis in AXES]
    swap_cores = [(0, 1), (1, 0)]
    if sizes[0] != 2 or any(size & (size - 1) for size in sizes):
        first = lax.axis_index("dp") == 0
        both = lax.psum([jnp.where(first, mine, other), jnp.where(first, other, mine)], AXES)
        return jnp.where(first, *both), jnp.where(first, both[1], both[0])
    part = mine + lax.ppermute(other, "dp", swap_cores).astype(F32)
    across = [(0, 1 << b) for b in range(sizes[2].bit_length() - 1)]
    down = [(1 << b, 0) for b in range(sizes[1].bit_length() - 1)]
    bits = []
    while across or down:
        bits += down[:1] + across[:1]
        down, across = down[1:], across[1:]
    groups = [bits[at : at + 2] for at in range(0, len(bits), 2)]
    for at in range(len(groups)):
        mine = [groups[at], groups[(at + len(groups) // 2) % len(groups)]]
        if len(mine[0]) != len(mine[1]):
            mine[1] = mine[0]
        mine.reverse()
        low = part.astype(BF)
        got = []
        for member in range(1, 1 << len(mine[0])):
            perm = []
            for core in range(2):
                flips = [flip for k, flip in enumerate(mine[core]) if member >> k & 1]
                for r in range(sizes[1]):
                    for c in range(sizes[2]):
                        to_r, to_c = r, c
                        for flip in flips:
                            to_r, to_c = to_r ^ flip[0], to_c ^ flip[1]
                        base = core * sizes[1]
                        perm.append(((base + r) * sizes[2] + c, (base + to_r) * sizes[2] + to_c))
            got.append(lax.ppermute(low, AXES, perm))
        if at == 1 and len(got) > 1:
            part = sum_four(low, got, done)
            continue
        got = [one.astype(F32) for one in got]
        part = low.astype(F32) + got[0]
        if len(got) > 1:
            part = part + (got[1] + got[2])
    return part, lax.ppermute(part, "dp", swap_cores)


def shards(features, grad_out, kernel_one, kernel_two):
    slides, chans, rows, cols = features.shape
    pairs = rows // 2
    feat, grad = to_pairs(features), to_pairs(grad_out)
    def turn(low, high, is_lower):
        return turn_edges(jnp.where(is_lower, high, low))

    both = jnp.concatenate([features, grad_out], axis=2)
    from_left, from_right = swap(both[..., : RIM // 2], both[..., cols - RIM // 2 :], "col", turn)
    edge = jnp.concatenate([from_right, from_left], axis=1)
    ahead, back, own_near, own_far = prep(feat, grad, kernel_one, kernel_two)
    sent_near, sent_far = frame(own_near, own_far, edge)
    got_near = lax.ppermute(sent_near, "row", neighbours("row", 0))
    got_far = lax.ppermute(sent_far, "row", neighbours("row", 1))
    odd = is_low("row", 1)
    one, more = got_near[:2], got_near[2:]
    above = jnp.concatenate([jnp.where(odd, one, got_far), jnp.where(odd, more, jnp.zeros_like(more))])
    below = jnp.concatenate([jnp.where(odd, got_far, one), jnp.where(odd, jnp.zeros_like(more), more)])
    hs_edge, ds2_edge, slope_edge, ds1, acc1, acc2 = inner(feat, grad, edge, ahead, back)
    ds1_next, end, row, mine, other = outer(
        feat, grad, edge, above, below, ahead, back, hs_edge, ds2_edge, slope_edge, acc1, acc2
    )
    row = lax.ppermute(row, "row", neighbours("row", 1))
    gf, done = last(end, ds1_next, ds1, row, back, cols)
    part, other = reduced(mine, other, done)
    count = slides * lax.axis_size("dp") * rows * lax.axis_size("row") * cols * lax.axis_size("col")
    grad_one, grad_two = finish(part, other, float(count) ** -0.5)
    return from_pairs(gf), grad_one, grad_two


def solution(mesh):
    return jax.shard_map(
        shards,
        mesh=mesh,
        in_specs=(P("dp", None, "row", "col"), P("dp", None, "row", "col"), P(), P()),
        out_specs=(P("dp", None, "row", "col"), P(), P()),
        check_vma=False,
    )
```
